32 devices in a mesh: fsdp: 4 (over z), seq: 8 (over y, x, core).
Axes of the slice: x: 2, y: 2, z: 4, core: 2. Of those that a mesh axis runs over, the one named last changes fastest.
Arguments:
- tokens: bfloat16 [4096, 2048], P(('fsdp', 'seq')), may hold values from -6 to 6
- cotangent: bfloat16 [4096, 2048], P(('fsdp', 'seq')), may hold values from -6 to 6
- adapter_index: int32 [4], replicated, may hold values from 0 to 7, as said below
- qkv_weight: bfloat16 [3, 2048, 2048], P(None, 'fsdp', 'seq'), may hold values from -0.125 to 0.125
- dense_weight: bfloat16 [2048, 2048], P('seq', 'fsdp'), may hold values from -2 to 2
- inner_weight: bfloat16 [2048, 8192], P('fsdp', 'seq'), may hold values from -0.125 to 0.125
- outer_weight: bfloat16 [8192, 2048], P('seq', 'fsdp'), may hold values from -0.0625 to 0.0625
- qkv_bias: bfloat16 [6144], replicated, may hold values from -2 to 2
- dense_bias: bfloat16 [2048], replicated, may hold values from -2 to 2
- inner_bias: bfloat16 [8192], replicated, may hold values from -2 to 2
- outer_bias: bfloat16 [2048], replicated, may hold values from -2 to 2
- norm_gain: bfloat16 [2048], replicated, may hold values from 0.25 to 1.75
- norm_bias: bfloat16 [2048], replicated, may hold values from -2 to 2
- qkv_down: bfloat16 [2048, 128], P(('fsdp', 'seq')), may hold values from -0.125 to 0.125
- qkv_up: bfloat16 [6144, 128], P(('fsdp', 'seq')), may hold values from -0.75 to 0.75
- dense_down: bfloat16 [2048, 128], P(('fsdp', 'seq')), may hold values from -0.125 to 0.125
- dense_up: bfloat16 [2048, 128], P(('fsdp', 'seq')), may hold values from -3 to 3
- inner_down: bfloat16 [2048, 128], P(('fsdp', 'seq')), may hold values from -0.125 to 0.125
- inner_up: bfloat16 [8192, 128], P(('fsdp', 'seq')), may hold values from -0.75 to 0.75
- outer_down: bfloat16 [8192, 128], P(('fsdp', 'seq')), may hold values from -0.0625 to 0.0625
- outer_up: bfloat16 [2048, 128], P(('fsdp', 'seq')), may hold values from -0.75 to 0.75
Outputs:
- layer_out: bfloat16 [4096, 2048], P(('fsdp', 'seq'))
- input_grad: float32 [4096, 2048], P(('fsdp', 'seq'))
- qkv_down_grad: float32 [2048, 128], P(('fsdp', 'seq'))
- qkv_up_grad: float32 [6144, 128], P(('fsdp', 'seq'))
- dense_down_grad: float32 [2048, 128], P(('fsdp', 'seq'))
- dense_up_grad: float32 [2048, 128], P(('fsdp', 'seq'))
- inner_down_grad: float32 [2048, 128], P(('fsdp', 'seq'))
- inner_up_grad: float32 [8192, 128], P(('fsdp', 'seq'))
- outer_down_grad: float32 [8192, 128], P(('fsdp', 'seq'))
- outer_up_grad: float32 [2048, 128], P(('fsdp', 'seq'))
The draws below stay inside these ranges and needn't reach their ends.
Inputs may be any that keep to these rules, and one draw needn't show every extreme that they name: `adapter_index`: the adapter of each sequence; 0 and 7 each belong to some sequence.
All inputs are finite; a program needn't handle non-finite values.
Results may differ from the reference program's by a relative error of at most 0.011.
The reference program's roundings to bfloat16 on the way count: a program that leaves them out, or rounds other values in their place, can miss the bound.
Values may be sent and summed in bfloat16 or wider, within the bound.
A program may use at most 320 MiB of HBM per device.

```python
import jax
import jax.numpy as jnp
from jax import lax

D = 2048
H = 32
HD = 64
ROT = 32
FF = 8192
RANK = 16
ADAPT = 8
BLOCK = 256
QBLK = 512
SEQS = 4
LEN = 1024
TOKENS = 4096


def draw_adapter_index(key, part):
    values = jax.random.randint(jax.random.fold_in(key, 1), (SEQS,), 0, ADAPT)
    high_at = jax.random.randint(jax.random.fold_in(key, 2), (), 0, SEQS)
    low_at = (high_at + 1 + jax.random.randint(jax.random.fold_in(key, 3), (), 0, SEQS - 1)) % SEQS
    values = values.at[high_at].set(ADAPT - 1)
    values = values.at[low_at].set(0)
    return values.astype(jnp.int32)


def block_scale(stream_key, dims, cuts, least, high):
    def one(axis_at, shards_of):
        heights = jax.random.uniform(jax.random.fold_in(jax.random.fold_in(stream_key, 6), axis_at), (shards_of,), jnp.float32, least / len(cuts), high / len(cuts))
        return jnp.repeat(jnp.exp(heights), dims[axis_at] // shards_of).reshape((-1,) + (1,) * (len(dims) - axis_at - 1))

    loudness = one(*cuts[0])
    for cut in cuts[1:]:
        loudness = loudness * one(*cut)
    return loudness


def noise(stream_key, dims, scale, reach, shards=(), kind=jnp.bfloat16):
    level = block_scale(stream_key, dims, shards, -0.22, 0.18) if shards else 1.0
    drawn = jax.random.normal(stream_key, dims, jnp.float32) * scale * level
    return jnp.minimum(jnp.maximum(drawn, -reach), reach).astype(kind)


def setup_inputs(seed: int = 0) -> dict:
    splits = jax.random.split(jax.random.key(seed), 22)
    return {
        "tokens": noise(splits[0], (TOKENS, D), 1.0, 6.0, ((0, 32),)),
        "cotangent": noise(splits[1], (TOKENS, D), 1.0, 6.0, ((0, 32),)),
        "adapter_index": draw_adapter_index(jax.random.fold_in(splits[21], 71), 0),
        "qkv_weight": noise(splits[3], (3, D, D), D ** -0.5, 0.125, ((1, 4), (2, 8))),
        "dense_weight": noise(splits[4], (D, D), (max(D // 256, 1)) ** -0.5, 2.0, ((0, 8), (1, 4))),
        "inner_weight": noise(splits[5], (D, FF), D ** -0.5, 0.125, ((0, 4), (1, 8))),
        "outer_weight": noise(splits[6], (FF, D), FF ** -0.5, 0.0625, ((0, 8), (1, 4))),
        "qkv_bias": noise(splits[7], (3 * D,), 0.3, 2.0),
        "dense_bias": noise(splits[8], (D,), 0.3, 2.0),
        "inner_bias": noise(splits[9], (FF,), 0.3, 2.0),
        "outer_bias": noise(splits[10], (D,), 0.3, 2.0),
        "norm_gain": jnp.clip(1.0 + 0.15 * jax.random.normal(splits[11], (D,), jnp.float32), 0.25, 1.75).astype(jnp.bfloat16),
        "norm_bias": noise(splits[12], (D,), 0.3, 2.0),
        "qkv_down": noise(splits[13], (D, ADAPT * RANK), D ** -0.5, 0.125, ((0, 32),)),
        "qkv_up": noise(splits[14], (3 * D, ADAPT * RANK), (4 * RANK) ** -0.5, 0.75, ((0, 32),)),
        "dense_down": noise(splits[15], (D, ADAPT * RANK), D ** -0.5, 0.125, ((0, 32),)),
        "dense_up": noise(splits[16], (D, ADAPT * RANK), (max(RANK // 4, 1)) ** -0.5, 3.0, ((0, 32),)),
        "inner_down": noise(splits[17], (D, ADAPT * RANK), D ** -0.5, 0.125, ((0, 32),)),
        "inner_up": noise(splits[18], (FF, ADAPT * RANK), (4 * RANK) ** -0.5, 0.75, ((0, 32),)),
        "outer_down": noise(splits[19], (FF, ADAPT * RANK), FF ** -0.5, 0.0625, ((0, 32),)),
        "outer_up": noise(splits[20], (D, ADAPT * RANK), (4 * RANK) ** -0.5, 0.75, ((0, 32),)),
    }


EPSILON = 1e-05
ADAPTER_SCALE = 2.0
ROPE_BASE = 10000.0
MASKED = -1e+30
PRECISE = lax.Precision.HIGHEST

@jax.custom_vjp
def low(v):
    return lax.optimization_barrier(v.astype(jnp.bfloat16)).astype(jnp.float32)

@jax.custom_vjp
def low_back(v):
    return v

def low_keep(v):
    return (low(v), None)

def low_pass(kept, grad):
    return (grad,)

def back_keep(v):
    return (v, None)

def back_low(kept, grad):
    return (low(grad),)
low.defvjp(low_keep, low_pass)
low_back.defvjp(back_keep, back_low)

def matrix_product(left_side, right_side):
    return jnp.dot(left_side, right_side, precision=PRECISE, preferred_element_type=jnp.float32)

def norm_layer(values, scale_gain, offset_bias):
    row_mean = lax.optimization_barrier(jnp.mean(values, axis=-1, keepdims=True))
    centred = values - row_mean
    spread = lax.optimization_barrier(jnp.mean(centred * centred, axis=-1, keepdims=True))
    return centred * lax.rsqrt(spread + EPSILON) * scale_gain + offset_bias

def rope_tables(positions):
    frequency = ROPE_BASE ** (-2.0 * jnp.arange(ROT // 2, dtype=jnp.float32) / ROT)
    angles = positions.astype(jnp.float32)[:, None] * frequency[None, :]
    return (jnp.cos(angles)[:, None, :], jnp.sin(angles)[:, None, :])

def rotate(values, cos_table, sin_table):
    first_half = values[..., :ROT // 2]
    second_half = values[..., ROT // 2:ROT]
    return jnp.concatenate([first_half * cos_table - second_half * sin_table, second_half * cos_table + first_half * sin_table, values[..., ROT:]], axis=-1)

def sequence_layer(source, index_value, trained, frozen):
    qkv_weight, dense_weight, inner_weight, outer_weight, qkv_bias, dense_bias, inner_bias, outer_bias, norm_gain, norm_bias = frozen
    qkv_down, qkv_up, dense_down, dense_up, inner_down, inner_up, outer_down, outer_up = trained
    column_mask = (jnp.arange(ADAPT * RANK) // RANK == index_value).astype(jnp.float32)

    def adapter_term(inputs, down_matrix, up_projection_matrix):
        adapter_factors = low_back(low(matrix_product(inputs, down_matrix) * column_mask))
        return ADAPTER_SCALE * matrix_product(adapter_factors, up_projection_matrix.T)
    normed = low(norm_layer(source, norm_gain, norm_bias))
    projected = low_back(matrix_product(normed, qkv_weight) + qkv_bias + adapter_term(normed, qkv_down, qkv_up))
    pieces = projected.reshape(LEN, 3, H, HD)
    cos_table, sin_table = rope_tables(jnp.arange(LEN))
    query_all = low_back(low(rotate(pieces[:, 0], cos_table, sin_table)))
    key_all = low_back(low(rotate(pieces[:, 1], cos_table, sin_table)))
    value_all = low_back(low(pieces[:, 2]))
    key_block = jnp.arange(LEN) // BLOCK

    def attend(offset):
        query_rows = lax.dynamic_slice_in_dim(query_all, offset, QBLK, 0)
        scores = low_back(jnp.einsum('qhd,khd->hqk', query_rows, key_all, precision=PRECISE) * HD ** (-0.5))
        allowed = key_block[None, :] <= ((offset + jnp.arange(QBLK)) // BLOCK)[:, None]
        scores = jnp.where(allowed[None], scores, MASKED)
        row_max = lax.optimization_barrier(jnp.max(scores, axis=-1, keepdims=True))
        exponent = jnp.exp(scores - row_max)
        probability = low(exponent / lax.optimization_barrier(jnp.sum(exponent, axis=-1, keepdims=True)))
        return jnp.einsum('hqk,khd->qhd', probability, value_all, precision=PRECISE)
    starts = (jnp.arange(LEN // QBLK) * QBLK).astype(jnp.int32)
    attended = lax.map(jax.checkpoint(attend), starts).reshape(LEN, D)
    attended = low_back(low(attended))
    attn_branch = matrix_product(attended, dense_weight) + dense_bias + adapter_term(attended, dense_down, dense_up)
    pre_act = low_back(matrix_product(normed, inner_weight) + inner_bias + adapter_term(normed, inner_down, inner_up))
    activated = low(jax.nn.gelu(pre_act, approximate=True))
    mlp_branch = matrix_product(activated, outer_weight) + outer_bias + adapter_term(activated, outer_down, outer_up)
    return source + attn_branch + mlp_branch

def reference(tokens, cotangent, adapter_index, qkv_weight, dense_weight, inner_weight, outer_weight, qkv_bias, dense_bias, inner_bias, outer_bias, norm_gain, norm_bias, qkv_down, qkv_up, dense_down, dense_up, inner_down, inner_up, outer_down, outer_up):
    stacked_qkv = qkv_weight.astype(jnp.float32)
    flat_qkv = jnp.concatenate([stacked_qkv[0], stacked_qkv[1], stacked_qkv[2]], axis=1)
    frozen = (flat_qkv,) + tuple((matrix.astype(jnp.float32) for matrix in (dense_weight, inner_weight, outer_weight, qkv_bias, dense_bias, inner_bias, outer_bias, norm_gain, norm_bias)))
    adapters = tuple((matrix.astype(jnp.float32) for matrix in (qkv_down, qkv_up, dense_down, dense_up, inner_down, inner_up, outer_down, outer_up)))

    def forward(source, trained):

        def one_sequence(seq_pair):
            return sequence_layer(seq_pair[0], seq_pair[1], trained, frozen)
        stacked = lax.map(jax.checkpoint(one_sequence), (source.reshape(SEQS, LEN, D), adapter_index))
        return stacked.reshape(TOKENS, D)
    layer_out, pullback = jax.vjp(forward, tokens.astype(jnp.float32), adapters)
    input_grad, adapter_grads = pullback(cotangent.astype(jnp.float32))
    return (layer_out.astype(jnp.bfloat16), input_grad, adapter_grads[0], adapter_grads[1], adapter_grads[2], adapter_grads[3], adapter_grads[4], adapter_grads[5], adapter_grads[6], adapter_grads[7])
```

```python
import jax
import jax.numpy as jnp
from jax import lax
from jax.sharding import PartitionSpec as P

H = 32
HD = 64
ROT = 32
RANK = 16
ADAPT = 8
BLOCK = 256
EPSILON = 1e-05
ADAPTER_SCALE = 2.0
ROPE_BASE = 10000.0
MASKED = -1e30
F32 = jnp.float32
BF16 = jnp.bfloat16


def dot(a, b, dims=((1,), (0,))):
    return lax.dot_general(a, b, (dims, ((), ())), preferred_element_type=F32)


def dot_nt(a, b):
    return dot(a, b, ((1,), (1,)))


def dot_tn(a, b):
    return dot(a, b, ((0,), (0,)))


def norm_layer(values, scale_gain, offset_bias):
    row_mean = jnp.mean(values, axis=-1, keepdims=True)
    centred = values - row_mean
    spread = jnp.mean(centred * centred, axis=-1, keepdims=True)
    return centred * lax.rsqrt(spread + EPSILON) * scale_gain + offset_bias


def rope_tables(length, heads):
    frequency = ROPE_BASE ** (-2.0 * jnp.arange(ROT // 2, dtype=F32) / ROT)
    angles = jnp.arange(length).astype(F32)[:, None] * frequency[None, :]
    return jnp.cos(angles)[:, None, :], jnp.sin(angles)[:, None, :]


def rotate(values, cos_table, sin_table):
    a = values[..., : ROT // 2]
    b = values[..., ROT // 2 : ROT]
    return jnp.concatenate(
        [a * cos_table - b * sin_table, b * cos_table + a * sin_table, values[..., ROT:]], axis=-1
    )


def on_device(
    tokens,
    cotangent,
    adapter_index,
    qkv_weight,
    dense_weight,
    inner_weight,
    outer_weight,
    qkv_bias,
    dense_bias,
    inner_bias,
    outer_bias,
    norm_gain,
    norm_bias,
    *maps,
):
    planes = lax.axis_size("fsdp")
    groups = lax.axis_size("seq")
    rows, width = tokens.shape
    length = rows * groups
    heads = H // groups
    mine = heads * HD
    units = inner_weight.shape[1]
    s = lax.axis_index("seq")

    counts = [m.shape[0] for m in maps]
    stacked = jnp.concatenate(maps, axis=0)
    wanted = (adapter_index[:, None] * RANK + jnp.arange(RANK)[None, :]).reshape(-1)
    pick = (wanted[:, None] == jnp.arange(ADAPT * RANK)[None, :]).astype(BF16)
    chosen = dot_nt(pick, stacked).astype(BF16).reshape(planes, RANK, -1)
    chosen = lax.all_to_all(chosen, "fsdp", split_axis=0, concat_axis=0, tiled=True)
    chosen = lax.all_gather(chosen, "seq", axis=1, tiled=False)
    full = []
    at = 0
    for n in counts:
        part = chosen[:, :, :, at : at + n]
        full.append(part.transpose(2, 0, 1, 3).reshape(RANK, -1))
        at += n
    qkv_down, qkv_up, dense_down, dense_up, inner_down, inner_up, outer_down, outer_up = full

    def own(m, n):
        return lax.dynamic_slice_in_dim(m, s * n, n, axis=1)

    qkv_up = jnp.concatenate(
        [own(qkv_up[:, c * width : (c + 1) * width], mine) for c in range(3)], axis=1
    )
    dense_down = own(dense_down, mine)
    inner_up = own(inner_up, units)
    outer_down = own(outer_down, units)

    wqkv = lax.all_gather(qkv_weight, "fsdp", axis=1, tiled=True)
    wdense = lax.all_gather(dense_weight, "fsdp", axis=1, tiled=True)
    winner = lax.all_gather(inner_weight, "fsdp", axis=0, tiled=True)
    wouter = lax.all_gather(outer_weight, "fsdp", axis=1, tiled=True)

    gain = norm_gain.astype(F32)
    shift = norm_bias.astype(F32)
    source = tokens.astype(F32)
    normed_own = norm_layer(source, gain, shift).astype(BF16)
    normed = lax.all_gather(normed_own, "seq", axis=0, tiled=True)
    cot = lax.all_gather(cotangent, "seq", axis=0, tiled=True)

    coeffs = dot_nt(normed, jnp.concatenate([qkv_down, inner_down], axis=0)).astype(BF16)
    qkv_coeff, inner_coeff = coeffs[:, :RANK], coeffs[:, RANK:]
    cgs = (
        ADAPTER_SCALE * dot_nt(cot, jnp.concatenate([dense_up, outer_up], axis=0))
    ).astype(BF16)
    dense_cg, outer_cg = cgs[:, :RANK], cgs[:, RANK:]

    bias = jnp.stack([own(qkv_bias.reshape(3, width)[c : c + 1], mine)[0] for c in range(3)])
    projected = (
        jnp.concatenate([dot(normed, wqkv[c]) for c in range(3)], axis=1)
        + bias.reshape(-1).astype(F32)
        + ADAPTER_SCALE * dot(qkv_coeff, qkv_up)
    ).reshape(length, 3, heads, HD)
    cos_table, sin_table = rope_tables(length, heads)
    query = rotate(projected[:, 0], cos_table, sin_table).astype(BF16).transpose(1, 0, 2)
    key = rotate(projected[:, 1], cos_table, sin_table).astype(BF16).transpose(1, 0, 2)
    value = projected[:, 2].astype(BF16).transpose(1, 0, 2)
    attended_grad = (dot_nt(cot, wdense) + dot(dense_cg, dense_down)).astype(BF16)
    head_grad = attended_grad.reshape(length, heads, HD).transpose(1, 0, 2)

    scale = HD ** (-0.5)

    def bmm(spec, a, b):
        return jnp.einsum(spec, a, b, preferred_element_type=F32)

    key_grad = jnp.zeros((heads, length, HD), F32)
    value_grad = jnp.zeros((heads, length, HD), F32)
    attended_parts = []
    query_parts = []
    for b in range(length // BLOCK):
        lo, hi = b * BLOCK, (b + 1) * BLOCK
        q = query[:, lo:hi]
        k = key[:, :hi]
        v = value[:, :hi]
        g = head_grad[:, lo:hi]
        scores = bmm("hqd,hkd->hqk", q, k) * scale
        row_max = jnp.max(scores, axis=-1, keepdims=True)
        exponent = jnp.exp(scores - row_max)
        prob = exponent / jnp.sum(exponent, axis=-1, keepdims=True)
        prob_low = prob.astype(BF16)
        attended_parts.append(bmm("hqk,hkd->hqd", prob_low, v).astype(BF16))
        prob_grad = bmm("hqd,hkd->hqk", g, v)
        row_dot = jnp.sum(prob_grad * prob, axis=-1, keepdims=True)
        score_grad = (prob * (prob_grad - row_dot)).astype(BF16)
        query_parts.append((bmm("hqk,hkd->hqd", score_grad, k) * scale).astype(BF16))
        key_grad = key_grad.at[:, :hi].add(bmm("hqk,hqd->hkd", score_grad, q) * scale)
        value_grad = value_grad.at[:, :hi].add(bmm("hqk,hqd->hkd", prob_low, g))

    def rows_first(x):
        return x.transpose(1, 0, 2)

    attended = rows_first(jnp.concatenate(attended_parts, axis=1)).reshape(length, mine)
    query_grad = rows_first(jnp.concatenate(query_parts, axis=1)).astype(F32)
    key_back = rows_first(key_grad.astype(BF16)).astype(F32)
    value_back = rows_first(value_grad.astype(BF16)).reshape(length, mine)
    projected_grad = jnp.concatenate(
        [
            rotate(query_grad, cos_table, -sin_table).astype(BF16).reshape(length, mine),
            rotate(key_back, cos_table, -sin_table).astype(BF16).reshape(length, mine),
            value_back,
        ],
        axis=1,
    )

    pre_act = (
        dot(normed, winner)
        + own(inner_bias[None], units).astype(F32)
        + ADAPTER_SCALE * dot(inner_coeff, inner_up)
    )
    act32, gelu_back = jax.vjp(lambda v: jax.nn.gelu(v, approximate=True), pre_act)
    activated = act32.astype(BF16)
    act_grad = dot_nt(cot, wouter) + dot(outer_cg, outer_down)
    pre_grad = gelu_back(act_grad)[0].astype(BF16)

    def scatter(x):
        return lax.psum_scatter(x, "seq", scatter_dimension=0, tiled=True)

    branch = scatter((dot(attended, wdense) + dot(activated, wouter)))
    coeff_sum = scatter(
        jnp.concatenate([dot_nt(attended, dense_down), dot_nt(activated, outer_down)], axis=1)
    )
    back = dot_nt(pre_grad, winner)
    for c in range(3):
        back = back + dot_nt(projected_grad[:, c * mine : (c + 1) * mine], wqkv[c])
    back = scatter(back)
    cg_sum = scatter(
        ADAPTER_SCALE
        * jnp.concatenate([dot_nt(projected_grad, qkv_up), dot_nt(pre_grad, inner_up)], axis=1)
    )
    late_own = jnp.concatenate([coeff_sum, cg_sum], axis=1).astype(BF16)
    late = lax.all_gather(late_own, "seq", axis=0, tiled=True)

    layer_out = (
        source
        + branch
        + dense_bias.astype(F32)
        + outer_bias.astype(F32)
        + ADAPTER_SCALE
        * dot(late_own[:, : 2 * RANK], jnp.concatenate([dense_up, outer_up], axis=0))
    ).astype(BF16)
    normed_grad = back + dot(
        late_own[:, 2 * RANK :], jnp.concatenate([qkv_down, inner_down], axis=0)
    )
    row_mean = jnp.mean(source, axis=-1, keepdims=True)
    centred = source - row_mean
    inv = lax.rsqrt(jnp.mean(centred * centred, axis=-1, keepdims=True) + EPSILON)
    xhat = centred * inv
    e = normed_grad * gain
    input_grad = cotangent.astype(F32) + inv * (
        e
        - jnp.mean(e, axis=-1, keepdims=True)
        - xhat * jnp.mean(e * xhat, axis=-1, keepdims=True)
    )

    share = width // groups
    cot_mine = own(cot, share)
    normed_mine = own(normed, share)
    qkv_up_g = ADAPTER_SCALE * dot_tn(qkv_coeff, projected_grad)
    inner_up_g = ADAPTER_SCALE * dot_tn(inner_coeff, pre_grad)
    dense_down_g = dot_tn(dense_cg, attended)
    outer_down_g = dot_tn(outer_cg, activated)
    ups = ADAPTER_SCALE * dot_tn(late[:, : 2 * RANK], cot_mine)
    downs = dot_tn(late[:, 2 * RANK :], normed_mine)
    mine_grads = [
        downs[:RANK],
        qkv_up_g,
        dense_down_g,
        ups[:RANK],
        downs[RANK:],
        inner_up_g,
        outer_down_g,
        ups[RANK:],
    ]
    packed = jnp.concatenate(mine_grads, axis=1)
    everyone = lax.all_gather(packed, "seq", axis=0, tiled=False)
    owned = []
    at = 0
    for i, (n, g) in enumerate(zip(counts, mine_grads)):
        w = g.shape[1]
        part = everyone[:, :, at : at + w]
        at += w
        blocks = 3 if i == 1 else 1
        part = part.reshape(groups, RANK, blocks, w // blocks).transpose(1, 2, 0, 3)
        part = part.reshape(RANK, planes, groups, n)
        owned.append(lax.dynamic_index_in_dim(part, s, 2, keepdims=False))
    owned = jnp.concatenate(owned, axis=2).transpose(1, 0, 2)
    arrived = lax.all_to_all(owned, "fsdp", split_axis=0, concat_axis=0, tiled=True)
    place = pick.astype(F32).reshape(planes * RANK, ADAPT * RANK)
    spread = lax.dot_general(
        arrived.reshape(planes * RANK, -1),
        place,
        (((0,), (0,)), ((), ())),
        precision=lax.Precision.HIGHEST,
        preferred_element_type=F32,
    )
    outs = []
    at = 0
    for n in counts:
        outs.append(spread[at : at + n])
        at += n
    return (layer_out, input_grad, *outs)


def solution(mesh):
    both = P(("fsdp", "seq"), None)
    placed = (
        both,
        both,
        P(),
        P(None, "fsdp", "seq"),
        P("seq", "fsdp"),
        P("fsdp", "seq"),
        P("seq", "fsdp"),
    ) + (P(),) * 6 + (both,) * 8
    return jax.shard_map(
        on_device, mesh=mesh, in_specs=placed, out_specs=(both,) * 10, check_vma=False
    )
```

```python
import functools

import jax
import jax.numpy as jnp
import numpy as np
from jax import lax
from jax.experimental import pallas as pl
from jax.experimental.pallas import tpu as pltpu
from jax.sharding import PartitionSpec as P

H = 32
HD = 64
ROT = 32
RANK = 16
ADAPT = 8
BLOCK = 256
EPSILON = 1e-05
ADAPTER_SCALE = 2.0
ROPE_BASE = 10000.0
MASKED = -1e30
F32 = jnp.float32
BF16 = jnp.bfloat16


def dot(a, b, dims=((1,), (0,))):
    return lax.dot_general(a, b, (dims, ((), ())), preferred_element_type=F32)


def dot_nt(a, b):
    return dot(a, b, ((1,), (1,)))


def dot_tn(a, b):
    return dot(a, b, ((0,), (0,)))


def norm_layer(values, scale_gain, offset_bias):
    row_mean = jnp.mean(values, axis=-1, keepdims=True)
    centred = values - row_mean
    spread = jnp.mean(centred * centred, axis=-1, keepdims=True)
    return centred * lax.rsqrt(spread + EPSILON) * scale_gain + offset_bias


def rope_tables(length, heads):
    frequency = ROPE_BASE ** (-2.0 * jnp.arange(ROT // 2, dtype=F32) / ROT)
    angles = jnp.arange(length).astype(F32)[:, None] * frequency[None, :]
    return jnp.cos(angles)[:, None, :], jnp.sin(angles)[:, None, :]


def rotate(values, cos_table, sin_table):
    a = values[..., : ROT // 2]
    b = values[..., ROT // 2 : ROT]
    return jnp.concatenate(
        [a * cos_table - b * sin_table, b * cos_table + a * sin_table, values[..., ROT:]], axis=-1
    )


MESH = pl.DeviceIdType.MESH
TILE = 256
UNIT = 256


def rope_constants(length):
    frequency = ROPE_BASE ** (-2.0 * np.arange(ROT // 2, dtype=np.float64) / ROT)
    angles = np.arange(length, dtype=np.float64)[:, None] * frequency[None, :]
    cos = np.ones((length, HD))
    sin = np.zeros((length, HD))
    half = ROT // 2
    cos[:, :half] = np.cos(angles)
    cos[:, half:ROT] = np.cos(angles)
    sin[:, :half] = -np.sin(angles)
    sin[:, half:ROT] = np.sin(angles)
    return (
        jnp.asarray(np.tile(cos, (1, 2)), F32),
        jnp.asarray(np.tile(sin, (1, 2)), F32),
    )


def turn(x, cos, sin, sign):
    lane = lax.broadcasted_iota(jnp.int32, x.shape, 1) % HD
    partner = jnp.where(
        lane < ROT // 2,
        pltpu.roll(x, x.shape[1] - ROT // 2, 1),
        pltpu.roll(x, ROT // 2, 1),
    )
    return x * cos + partner * (sin * sign)


def turn_all(x, cos, sin, sign):
    step = cos.shape[1]
    return jnp.concatenate(
        [turn(x[:, i : i + step], cos, sin, sign) for i in range(0, x.shape[1], step)], axis=1
    )


def layer_kernel(
    planes,
    tok_ref,
    cotown_ref,
    wq_in,
    wd_in,
    wi_in,
    wo_in,
    qb_ref,
    db_ref,
    ib_ref,
    ob_ref,
    gain_ref,
    shift_ref,
    downs_ref,
    ups_ref,
    qup_ref,
    ddown_ref,
    iup_ref,
    odown_ref,
    cos_ref,
    sin_ref,
    out_ref,
    igrad_ref,
    packed_ref,
    normed,
    cot,
    wq,
    wd,
    wi,
    wo,
    qkv,
    hg,
    att,
    dk,
    dv,
    pg,
    acc_a,
    acc_b,
    pre,
    act,
    ag,
    pgrad,
    coeff,
    cgs,
    coeff_t,
    cgs_t,
    res,
    keep,
    s1_send,
    s1_recv,
    a_send,
    a_recv,
    c_send,
    c_recv,
    ar_send,
    ar_recv,
    local_sem,
    zs_sem,
    zr_sem,
    ag_ssem,
    ag_rsem,
    s1_ssem,
    s1_rsem,
    a_ssem,
    a_rsem,
    c_ssem,
    c_rsem,
    ar_ssem,
    ar_rsem,
):
    z = lax.axis_index("fsdp")
    s = lax.axis_index("seq")
    core = s % 2
    chip = s // 2
    to_core = (z, chip * 2 + (1 - core))
    chip_x = chip + 1 - 2 * (chip % 2)
    chip_y = (chip + 2) % 4
    chip_d = chip_x + 2 - 4 * (chip_x // 2)
    to_x = (z, chip_x * 2 + core)
    to_y = (z, chip_y * 2 + core)
    rows, width = tok_ref.shape
    length = normed.shape[0]
    units = act.shape[1]
    fan = width // planes
    mine = wq.shape[3]
    tiles = length // TILE

    def remote(src, dst, ssem, rsem, where):
        return pltpu.make_async_remote_copy(
            src_ref=src, dst_ref=dst, send_sem=ssem, recv_sem=rsem, device_id=where,
            device_id_type=MESH,
        )

    def block(i, n):
        return pl.ds(pl.multiple_of(i * n, n), n)

    bar = pltpu.get_barrier_semaphore()
    for where in (to_core, to_x, to_y):
        pl.semaphore_signal(bar, inc=1, device_id=where, device_id_type=MESH)

    @pl.when(z > 0)
    def _():
        pl.semaphore_signal(bar, inc=1, device_id=(z - 1, s), device_id_type=MESH)

    @pl.when(z < planes - 1)
    def _():
        pl.semaphore_signal(bar, inc=1, device_id=(z + 1, s), device_id_type=MESH)

    above = jnp.where(z < planes - 1, 1, 0)
    pl.semaphore_wait(bar, 3 + above + jnp.where(z > 0, 1, 0))

    chunks = []
    for c in range(3):
        chunks.append((wq_in.at[c], lambda j, c=c: wq.at[j, c]))
    chunks.append((wd_in, lambda j: wd.at[j]))
    part = fan // 4
    for i in range(4):
        chunks.append(
            (
                wi_in.at[pl.ds(i * part, part), :],
                lambda j, i=i: wi.at[j, pl.ds(i * part, part), :],
            )
        )
    deep = units // 2
    for j2 in range(fan // UNIT):
        for i in range(2):
            chunks.append(
                (
                    wo_in.at[pl.ds(i * deep, deep), pl.ds(j2 * UNIT, UNIT)],
                    lambda j, i=i, j2=j2: wo.at[
                        j, pl.ds(i * deep, deep), pl.ds(j2 * UNIT, UNIT)
                    ],
                )
            )
    n_chunks = len(chunks)
    last_step = n_chunks + planes - 1

    def zcopy(c, direction, k):
        src, place = chunks[c]
        j = z - k if direction == 0 else z + k
        return remote(
            src if k == 0 else place(j),
            place(j),
            zs_sem.at[c, direction, k],
            zr_sem.at[c, j],
            (z + 1, s) if direction == 0 else (z - 1, s),
        )

    def zhas(direction, k):
        if direction == 0:
            return jnp.logical_and(z - k >= 0, z + 1 < planes)
        return jnp.logical_and(z + k < planes, z - 1 >= 0)

    def zsend(c, k):
        for direction in (0, 1):

            @pl.when(zhas(direction, k))
            def _(direction=direction):
                zcopy(c, direction, k).start()

    def zwait(c, k):
        for direction in (0, 1):
            j = z - k if direction == 0 else z + k
            there = z - k >= 0 if direction == 0 else z + k < planes

            @pl.when(there)
            def _(j=j, direction=direction):
                place = chunks[c][1](j)
                pltpu.make_async_copy(place, place, zr_sem.at[c, j]).wait()

    def zstep(t):
        if t == 0:
            zsend(0, 0)
            zsend(1, 0)
        elif t + 1 < n_chunks:
            zsend(t + 1, 0)
        for k in range(1, planes):
            c = t - k
            if 0 <= c < n_chunks:
                zwait(c, k)
                if k < planes - 1:
                    zsend(c, k)

    own = []
    for c in range(n_chunks):
        src, place = chunks[c]
        own.append(pltpu.make_async_copy(src, place(z), local_sem.at[c]))
    for copy in own:
        copy.start()

    zstep(0)

    half = width // 2

    def gather_copies(p, buf):
        me = buf.at[block(s, rows), :]
        bx = chip_x * 2 + core
        by = chip_y * 2 + core
        bd = chip_d * 2 + core
        blk_x = buf.at[block(bx, rows), :]
        blk_y = buf.at[block(by, rows), :]
        blk_d = buf.at[block(bd, rows), :]
        x0 = buf.at[block(bx, rows), pl.ds(0, half)]
        y1 = buf.at[block(by, rows), pl.ds(half, half)]
        d0 = buf.at[block(bd, rows), pl.ds(0, half)]
        d1 = buf.at[block(bd, rows), pl.ds(half, half)]
        ss, rs = ag_ssem.at[p], ag_rsem.at[p]

        def same(ref, i, where):
            return remote(ref, ref, ss.at[i], rs.at[i], where)

        sends = [
            same(me, 0, to_x),
            same(me, 1, to_y),
            same(me, 2, to_core),
            same(x0, 3, to_y),
            same(blk_x, 4, to_core),
            same(y1, 5, to_x),
            same(blk_y, 6, to_core),
            same(blk_d, 7, to_core),
        ]
        other = 1 - core
        into = [
            blk_x,
            blk_y,
            buf.at[block(chip * 2 + other, rows), :],
            d0,
            buf.at[block(chip_x * 2 + other, rows), :],
            d1,
            buf.at[block(chip_y * 2 + other, rows), :],
            buf.at[block(chip_d * 2 + other, rows), :],
        ]

        def arrived(i):
            pltpu.make_async_copy(into[i], into[i], rs.at[i]).wait()

        return sends, arrived

    cot[block(s, rows), :] = cotown_ref[...]
    c_sends, c_arrived = gather_copies(0, cot)
    for i in range(3):
        c_sends[i].start()

    x = tok_ref[...].astype(F32)
    mean = jnp.mean(x, axis=-1, keepdims=True)
    centred = x - mean
    inv = lax.rsqrt(jnp.mean(centred * centred, axis=-1, keepdims=True) + EPSILON)
    normed[block(s, rows), :] = (
        centred * inv * gain_ref[...].astype(F32) + shift_ref[...].astype(F32)
    ).astype(BF16)
    n_sends, n_arrived = gather_copies(1, normed)
    for i in range(3):
        n_sends[i].start()
    for sends, arrived in ((c_sends, c_arrived), (n_sends, n_arrived)):
        arrived(0)
        sends[3].start()
        sends[4].start()
        arrived(1)
        sends[5].start()
        sends[6].start()
    zstep(1)
    for sends, arrived in ((c_sends, c_arrived), (n_sends, n_arrived)):
        arrived(3)
        arrived(5)
        sends[7].start()
    for sends, arrived in ((c_sends, c_arrived), (n_sends, n_arrived)):
        for i in (2, 4, 6, 7):
            arrived(i)
    zstep(2)

    def low(t, carry):
        r = block(t, TILE)
        c = dot_nt(normed[r, :], downs_ref[...])
        coeff[r, :] = c.astype(BF16)
        g = ADAPTER_SCALE * dot_nt(cot[r, :], ups_ref[...])
        cgs[r, :] = g.astype(BF16)
        return carry

    lax.fori_loop(0, tiles, low, 0)
    for copy in own:
        copy.wait()
    zstep(3)
    zstep(4)
    zstep(5)
    zstep(6)

    def project(t, carry):
        r = block(t, TILE)
        cos = cos_ref[r, :]
        sin = sin_ref[r, :]
        for c in range(3):
            v = ADAPTER_SCALE * dot(coeff[r, :RANK], qup_ref[:, c * mine : (c + 1) * mine])
            v = v + qb_ref[c : c + 1, block(s, mine)].astype(F32)
            for j in range(planes):
                v = v + dot(normed[r, j * fan : (j + 1) * fan], wq[j, c])
            if c < 2:
                v = turn_all(v, cos, sin, 1.0)
            v = v.astype(BF16)
            if c == 0:
                v = v * jnp.asarray(HD**-0.5, BF16)
            qkv[c, r, :] = v
        g = dot(cgs[r, :RANK], ddown_ref[...])
        for j in range(planes):
            g = g + dot_nt(cot[r, j * fan : (j + 1) * fan], wd[j])
        hg[r, :] = g.astype(BF16)
        return carry

    lax.fori_loop(0, tiles, project, 0)
    zstep(7)

    dk[...] = jnp.zeros_like(dk)
    dv[...] = jnp.zeros_like(dv)
    heads = mine // HD

    for b in range(length // BLOCK):
        lo, hi = b * BLOCK, (b + 1) * BLOCK
        acc_a[...] = jnp.zeros_like(acc_a)
        acc_b[...] = jnp.zeros_like(acc_b)

        def one_head(h, carry, lo=lo, hi=hi):
            lane = lax.broadcasted_iota(jnp.int32, (1, mine), 1)
            mask = (lane // HD == h).astype(BF16)
            mask32 = (lane // HD == h).astype(F32)
            q = qkv[0, lo:hi, :] * mask
            g = hg[lo:hi, :] * mask
            k = qkv[1, :hi, :]
            v = qkv[2, :hi, :]
            sc = dot_nt(q, k)
            e = jnp.exp(sc - jnp.max(sc, axis=-1, keepdims=True))
            p = e * (1.0 / jnp.sum(e, axis=-1, keepdims=True))
            pb = p.astype(BF16)
            acc_a[...] += dot(pb, v) * mask32
            dp = dot_nt(g, v)
            ds = (p * (dp - jnp.sum(dp * p, axis=-1, keepdims=True))).astype(BF16)
            acc_b[...] += dot(ds, k) * mask32
            dk[:hi, :] += dot_tn(ds, q)
            dv[:hi, :] += dot_tn(pb, g)
            return carry

        lax.fori_loop(0, heads, one_head, 0)
        att[lo:hi, :] = acc_a[...].astype(BF16)
        back = (acc_b[...] * (HD**-0.5)).astype(BF16).astype(F32)
        pg[0, lo:hi, :] = turn_all(back, cos_ref[lo:hi, :], sin_ref[lo:hi, :], -1.0).astype(BF16)
        if b % 2 == 1:
            zstep(8 + b // 2)

    def finish(t, carry):
        r = block(t, TILE)
        back = dk[r, :].astype(BF16).astype(F32)
        pg[1, r, :] = turn_all(back, cos_ref[r, :], sin_ref[r, :], -1.0).astype(BF16)
        pg[2, r, :] = dv[r, :].astype(BF16)
        return carry

    lax.fori_loop(0, tiles, finish, 0)

    coeff_t[...] = dot_nt(downs_ref[...], normed[...]).astype(BF16)
    cgs_t[...] = (ADAPTER_SCALE * dot_nt(ups_ref[...], cot[...])).astype(BF16)

    share = width // 8
    at_qup = share
    at_ddown = at_qup + 3 * mine
    at_dup = at_ddown + mine
    at_idown = at_dup + share
    at_iup = at_idown + share
    at_odown = at_iup + units
    at_oup = at_odown + units
    for c in range(3):
        packed_ref[:, at_qup + c * mine : at_qup + (c + 1) * mine] = ADAPTER_SCALE * dot(
            coeff_t[:RANK, :], pg[c]
        )
    packed_ref[:, at_ddown : at_ddown + mine] = dot(cgs_t[:RANK, :], att[...])
    zstep(10)

    k0 = 0.7978845608028654
    k1 = 0.044715

    def inner(t, carry):
        r = block(t, TILE)
        v = ADAPTER_SCALE * dot(coeff[r, RANK : 2 * RANK], iup_ref[...])
        v = v + ib_ref[:, block(s, units)].astype(F32)
        for j in range(planes):
            v = v + dot(normed[r, j * fan : (j + 1) * fan], wi[j])
        sq = v * v
        th = jnp.tanh(k0 * v * (1.0 + k1 * sq))
        act[r, :] = (0.5 * v * (1.0 + th)).astype(BF16)
        pre[r, :] = 0.5 * (1.0 + th) + 0.5 * v * (1.0 - th * th) * (k0 * (1.0 + 3.0 * k1 * sq))
        return carry

    lax.fori_loop(0, tiles, inner, 0)
    packed_ref[:, at_odown : at_odown + units] = dot(cgs_t[RANK : 2 * RANK, :], act[...])
    zstep(11)

    partners = (to_core, to_x, to_y)

    def reduce_copy(w, i):
        return remote(
            ar_send.at[w], ar_recv.at[w, i], ar_ssem.at[w, i], ar_rsem.at[w, i], partners[i]
        )

    def reduce_round(w, i):
        if i > 0:
            reduce_copy(w, i - 1).wait()
            ar_send[w] += ar_recv[w, i - 1]
        if i < 3:
            reduce_copy(w, i).start()

    ar_send[0, :RANK, :] = dot_nt(ddown_ref[...], att[...])
    ar_send[0, RANK : 2 * RANK, :] = dot_nt(odown_ref[...], act[...])
    for i in range(4):
        reduce_round(0, i)
    coeff_dense = ar_send[0].astype(BF16)
    for i in range(2):
        g = ADAPTER_SCALE * dot(
            coeff_dense[i * RANK : (i + 1) * RANK, :], cot[:, block(s, share)]
        )
        at = (at_dup, at_oup)[i]
        packed_ref[:, at : at + share] = g

    p_units = width // UNIT
    per = fan // UNIT
    early = p_units - planes
    total = 2 * p_units

    def place_of(n):
        first = n < p_units
        j = jnp.where(first, n % planes, (n - p_units) // per)
        i = jnp.where(first, n // planes, (n - p_units) % per)
        return j, i

    def keep_split(n, k, r):
        slot = n % 2
        a = r[:rows, :]
        b = r[rows:, :]
        first = core == 0
        keep[n % 4, k] = jnp.where(first, a, b)
        s1_send[slot, k] = jnp.where(first, b, a).astype(BF16)

    def s1_copy(n):
        return remote(s1_send.at[n % 2], s1_recv.at[n], s1_ssem.at[n % 2], s1_rsem.at[n], to_core)

    def a_copy(n, i):
        return remote(
            a_send.at[n % 2, i], a_recv.at[n, i], a_ssem.at[n % 2, i], a_rsem.at[n, i],
            (to_x, to_y)[i],
        )

    def c_copy(n, i):
        return remote(
            c_send.at[n % 2, i], c_recv.at[n, i], c_ssem.at[n % 2, i], c_rsem.at[n, i],
            (to_x, to_y)[i],
        )

    hu = UNIT // 2

    def stage0_branch(n):
        j, i = place_of(n)

        def tile(k, carry):
            r = block(k, TILE)
            cols = block(i, UNIT)
            keep_split(n, k, dot(act[r, :], wo[j, :, cols]) + dot(att[r, :], wd[j, :, cols]))
            return carry

        lax.fori_loop(0, tiles, tile, 0)
        s1_copy(n).start()

    def stage0_back(n):
        j, i = place_of(n)

        def tile(k, carry):
            r = block(k, TILE)
            rws = block(i, UNIT)
            v = dot_nt(pgrad[r, :], wi[j, rws, :])
            for c in range(3):
                v = v + dot_nt(pg[c, r, :], wq[j, c, rws, :])
            keep_split(n, k, v)
            return carry

        lax.fori_loop(0, tiles, tile, 0)
        s1_copy(n).start()

    def stage1(n):
        s1_copy(n).wait()
        q = n % 4
        for k in range(4):
            keep[q, k] += s1_recv[n, k].astype(F32)
        far = keep[q, chip_d]
        a_send[n % 2, 0] = far[:, :hu].astype(BF16)
        a_send[n % 2, 1] = far[:, hu:].astype(BF16)
        for i in range(2):
            a_copy(n, i).start()

    def stage2(n):
        q = n % 4
        for i in range(2):
            a_copy(n, i).wait()
        keep[q, chip_y, :, :hu] += a_recv[n, 0].astype(F32)
        keep[q, chip_x, :, hu:] += a_recv[n, 1].astype(F32)
        c_send[n % 2, 0] = keep[q, chip_x].astype(BF16)
        c_send[n % 2, 1] = keep[q, chip_y].astype(BF16)
        for i in range(2):
            c_copy(n, i).start()

    def stage3(n):
        q = n % 4
        for i in range(2):
            c_copy(n, i).wait()
        j, i = place_of(n)
        v = keep[q, chip] + c_recv[n, 0].astype(F32) + c_recv[n, 1].astype(F32)
        res[n // p_units, :, block(j * per + i, UNIT)] = v

    def pipeline(first, lo, hi, stage0, extra=None):
        def body(n, carry):
            if stage0 is not None:
                stage0(n)
            for back, stage in ((1, stage1), (2, stage2), (3, stage3)):
                m = n - back
                ok = m >= first
                if stage0 is None:
                    ok = jnp.logical_and(ok, m < hi - 3)

                @pl.when(ok)
                def _(m=m, stage=stage):
                    stage(m)

            if extra is not None:
                extra(n)
            return carry

        lax.fori_loop(lo, hi, body, 0)

    zstep(12)
    pipeline(0, 0, early, stage0_branch)
    pipeline(0, early, early + 3, None)

    def act_back(t, carry):
        r = block(t, TILE)
        v = dot(cgs[r, RANK : 2 * RANK], odown_ref[...])
        for j in range(planes):
            for i in range(per - 1):
                c0 = j * fan + i * UNIT
                v = v + dot_nt(cot[r, c0 : c0 + UNIT], wo[j, :, i * UNIT : (i + 1) * UNIT])
        ag[r, :] = v
        return carry

    lax.fori_loop(0, tiles, act_back, 0)
    for t in range(13, last_step):
        zstep(t)

    pipeline(early, early, p_units, stage0_branch)

    def act_last(t, carry):
        r = block(t, TILE)
        v = ag[r, :]
        for j in range(planes):
            i = per - 1
            c0 = j * fan + i * UNIT
            v = v + dot_nt(cot[r, c0 : c0 + UNIT], wo[j, :, i * UNIT : (i + 1) * UNIT])
        pgrad[r, :] = (v * pre[r, :]).astype(BF16)
        return carry

    lax.fori_loop(0, tiles, act_last, 0)

    up_part = dot_nt(iup_ref[...], pgrad[...])
    q_part = dot_nt(qup_ref[:, :mine], pg[0])
    for c in range(1, 3):
        q_part = q_part + dot_nt(qup_ref[:, c * mine : (c + 1) * mine], pg[c])
    ar_send[1, :RANK, :] = ADAPTER_SCALE * q_part
    ar_send[1, RANK : 2 * RANK, :] = ADAPTER_SCALE * up_part
    reduce_round(1, 0)

    def rounds(n):
        for i in range(1, 4):

            @pl.when(n == p_units + 2 * i - 1)
            def _(i=i):
                reduce_round(1, i)

    pipeline(early, p_units, total, stage0_back, rounds)
    packed_ref[:, at_iup : at_iup + units] = ADAPTER_SCALE * dot(
        coeff_t[RANK : 2 * RANK, :], pgrad[...]
    )
    late = ar_send[1].astype(BF16)
    g = dot(late, normed[:, block(s, share)])
    packed_ref[:, :share] = g[:RANK]
    packed_ref[:, at_idown : at_idown + share] = g[RANK:]
    pipeline(early, total, total + 3, None)

    first_t = ar_send[0, :, block(s, rows)].astype(BF16)
    late_t = ar_send[1, :, block(s, rows)].astype(BF16)
    out = tok_ref[...].astype(F32) + res[0] + ADAPTER_SCALE * dot_tn(first_t, ups_ref[...])
    out_ref[...] = (out + db_ref[...].astype(F32) + ob_ref[...].astype(F32)).astype(BF16)
    x = tok_ref[...].astype(F32)
    mean = jnp.mean(x, axis=-1, keepdims=True)
    centred = x - mean
    inv = lax.rsqrt(jnp.mean(centred * centred, axis=-1, keepdims=True) + EPSILON)
    xhat = centred * inv
    e = (res[1] + dot_tn(late_t, downs_ref[...])) * gain_ref[...].astype(F32)
    igrad_ref[...] = cotown_ref[...].astype(F32) + inv * (
        e
        - jnp.mean(e, axis=-1, keepdims=True)
        - xhat * jnp.mean(e * xhat, axis=-1, keepdims=True)
    )

    for sends, _ in ((c_sends, None), (n_sends, None)):
        for copy in sends:
            copy.wait_send()
    for c in range(n_chunks):
        for k in range(planes - 1):
            for direction in (0, 1):

                @pl.when(zhas(direction, k))
                def _(c=c, k=k, direction=direction):
                    zcopy(c, direction, k).wait_send()


def run_layer(planes, args, shapes):
    rows, width, length, units, mine = shapes
    fan = width // planes
    vm = pl.BlockSpec(memory_space=pltpu.VMEM)
    hbm = pl.BlockSpec(memory_space=pl.ANY)
    n_chunks = 8 + 2 * (fan // UNIT)
    total = 2 * width // UNIT
    dma = pltpu.SemaphoreType.DMA
    cols = width // 8 * 4 + 4 * mine + 2 * units
    return pl.pallas_call(
        functools.partial(layer_kernel, planes),
        out_shape=(
            jax.ShapeDtypeStruct((rows, width), BF16),
            jax.ShapeDtypeStruct((rows, width), F32),
            jax.ShapeDtypeStruct((RANK, cols), F32),
        ),
        in_specs=[vm, vm, hbm, hbm, hbm, hbm] + [vm] * 14,
        out_specs=(vm, vm, vm),
        scratch_shapes=[
            pltpu.VMEM((length, width), BF16),
            pltpu.VMEM((length, width), BF16),
            pltpu.VMEM((planes, 3, fan, mine), BF16),
            pltpu.VMEM((planes, mine, fan), BF16),
            pltpu.VMEM((planes, fan, units), BF16),
            pltpu.VMEM((planes, units, fan), BF16),
            pltpu.VMEM((3, length, mine), BF16),
            pltpu.VMEM((length, mine), BF16),
            pltpu.VMEM((length, mine), BF16),
            pltpu.VMEM((length, mine), F32),
            pltpu.VMEM((length, mine), F32),
            pltpu.VMEM((3, length, mine), BF16),
            pltpu.VMEM((BLOCK, mine), F32),
            pltpu.VMEM((BLOCK, mine), F32),
            pltpu.VMEM((length, units), F32),
            pltpu.VMEM((length, units), BF16),
            pltpu.VMEM((length, units), F32),
            pltpu.VMEM((length, units), BF16),
            pltpu.VMEM((length, 2 * RANK), BF16),
            pltpu.VMEM((length, 2 * RANK), BF16),
            pltpu.VMEM((2 * RANK, length), BF16),
            pltpu.VMEM((2 * RANK, length), BF16),
            pltpu.VMEM((2, rows, width), F32),
            pltpu.VMEM((4, 4, rows, UNIT), F32),
            pltpu.VMEM((2, 4, rows, UNIT), BF16),
            pltpu.VMEM((total, 4, rows, UNIT), BF16),
            pltpu.VMEM((2, 2, rows, UNIT // 2), BF16),
            pltpu.VMEM((total, 2, rows, UNIT // 2), BF16),
            pltpu.VMEM((2, 2, rows, UNIT), BF16),
            pltpu.VMEM((total, 2, rows, UNIT), BF16),
            pltpu.VMEM((2, 2 * RANK, length), F32),
            pltpu.VMEM((2, 3, 2 * RANK, length), F32),
            dma((n_chunks,)),
            dma((n_chunks, 2, planes)),
            dma((n_chunks, planes)),
            dma((2, 8)),
            dma((2, 8)),
            dma((2,)),
            dma((total,)),
            dma((2, 2)),
            dma((total, 2)),
            dma((2, 2)),
            dma((total, 2)),
            dma((2, 3)),
            dma((2, 3)),
        ],
        compiler_params=pltpu.CompilerParams(
            collective_id=0, has_side_effects=True, vmem_limit_bytes=63 * 1024 * 1024
        ),
    )(*args)


def fits(planes, groups, shapes):
    rows, width, length, units, mine = shapes
    return (
        groups == 8
        and planes > 1
        and rows * 2 == TILE
        and length <= 1024
        and width % (planes * UNIT) == 0
        and mine % 128 == 0
        and units % 256 == 0
    )


def deliver(packed, sizes, counts, pick, planes, groups):
    s = lax.axis_index("seq")
    everyone = lax.all_gather(packed, "seq", axis=0, tiled=False)
    owned = []
    at = 0
    for i, (n, w) in enumerate(zip(counts, sizes)):
        part = everyone[:, :, at : at + w]
        at += w
        blocks = 3 if i == 1 else 1
        part = part.reshape(groups, RANK, blocks, w // blocks).transpose(1, 2, 0, 3)
        part = part.reshape(RANK, planes, groups, n)
        owned.append(lax.dynamic_index_in_dim(part, s, 2, keepdims=False))
    owned = jnp.concatenate(owned, axis=2).transpose(1, 0, 2)
    arrived = lax.all_to_all(owned, "fsdp", split_axis=0, concat_axis=0, tiled=True)
    place = pick.astype(F32).reshape(planes * RANK, ADAPT * RANK)
    spread = lax.dot_general(
        arrived.reshape(planes * RANK, -1),
        place,
        (((0,), (0,)), ((), ())),
        precision=lax.Precision.HIGHEST,
        preferred_element_type=F32,
    )
    outs = []
    at = 0
    for n in counts:
        outs.append(spread[at : at + n])
        at += n
    return outs


def on_device(
    tokens,
    cotangent,
    adapter_index,
    qkv_weight,
    dense_weight,
    inner_weight,
    outer_weight,
    qkv_bias,
    dense_bias,
    inner_bias,
    outer_bias,
    norm_gain,
    norm_bias,
    *maps,
):
    planes = lax.axis_size("fsdp")
    groups = lax.axis_size("seq")
    rows, width = tokens.shape
    length = rows * groups
    heads = H // groups
    mine = heads * HD
    units = inner_weight.shape[1]
    s = lax.axis_index("seq")

    counts = [m.shape[0] for m in maps]
    stacked = jnp.concatenate(maps, axis=0)
    wanted = (adapter_index[:, None] * RANK + jnp.arange(RANK)[None, :]).reshape(-1)
    pick = (wanted[:, None] == jnp.arange(ADAPT * RANK)[None, :]).astype(BF16)
    chosen = dot_nt(pick, stacked).astype(BF16).reshape(planes, RANK, -1)
    chosen = lax.all_to_all(chosen, "fsdp", split_axis=0, concat_axis=0, tiled=True)
    chosen = lax.all_gather(chosen, "seq", axis=1, tiled=False)
    full = []
    at = 0
    for n in counts:
        part = chosen[:, :, :, at : at + n]
        full.append(part.transpose(2, 0, 1, 3).reshape(RANK, -1))
        at += n
    qkv_down, qkv_up, dense_down, dense_up, inner_down, inner_up, outer_down, outer_up = full

    def own(m, n):
        return lax.dynamic_slice_in_dim(m, s * n, n, axis=1)

    qkv_up = jnp.concatenate(
        [own(qkv_up[:, c * width : (c + 1) * width], mine) for c in range(3)], axis=1
    )
    dense_down = own(dense_down, mine)
    inner_up = own(inner_up, units)
    outer_down = own(outer_down, units)

    shapes = (rows, width, length, units, mine)
    if fits(planes, groups, shapes):
        cos, sin = rope_constants(length)
        layer_out, input_grad, packed = run_layer(
            planes,
            (
                tokens,
                cotangent,
                qkv_weight,
                dense_weight,
                inner_weight,
                outer_weight,
                qkv_bias.reshape(3, width),
                dense_bias[None],
                inner_bias[None],
                outer_bias[None],
                norm_gain[None],
                norm_bias[None],
                jnp.concatenate([qkv_down, inner_down], axis=0),
                jnp.concatenate([dense_up, outer_up], axis=0),
                qkv_up,
                dense_down,
                inner_up,
                outer_down,
                cos,
                sin,
            ),
            shapes,
        )
        sizes = [width // groups, 3 * mine, mine, width // groups, width // groups]
        sizes += [units, units, width // groups]
        outs = deliver(packed, sizes, counts, pick, planes, groups)
        return (layer_out, input_grad, *outs)

    wqkv = lax.all_gather(qkv_weight, "fsdp", axis=1, tiled=True)
    wdense = lax.all_gather(dense_weight, "fsdp", axis=1, tiled=True)
    winner = lax.all_gather(inner_weight, "fsdp", axis=0, tiled=True)
    wouter = lax.all_gather(outer_weight, "fsdp", axis=1, tiled=True)

    gain = norm_gain.astype(F32)
    shift = norm_bias.astype(F32)
    source = tokens.astype(F32)
    normed_own = norm_layer(source, gain, shift).astype(BF16)
    normed = lax.all_gather(normed_own, "seq", axis=0, tiled=True)
    cot = lax.all_gather(cotangent, "seq", axis=0, tiled=True)

    coeffs = dot_nt(normed, jnp.concatenate([qkv_down, inner_down], axis=0)).astype(BF16)
    qkv_coeff, inner_coeff = coeffs[:, :RANK], coeffs[:, RANK:]
    cgs = (
        ADAPTER_SCALE * dot_nt(cot, jnp.concatenate([dense_up, outer_up], axis=0))
    ).astype(BF16)
    dense_cg, outer_cg = cgs[:, :RANK], cgs[:, RANK:]

    bias = jnp.stack([own(qkv_bias.reshape(3, width)[c : c + 1], mine)[0] for c in range(3)])
    projected = (
        jnp.concatenate([dot(normed, wqkv[c]) for c in range(3)], axis=1)
        + bias.reshape(-1).astype(F32)
        + ADAPTER_SCALE * dot(qkv_coeff, qkv_up)
    ).reshape(length, 3, heads, HD)
    cos_table, sin_table = rope_tables(length, heads)
    query = rotate(projected[:, 0], cos_table, sin_table).astype(BF16).transpose(1, 0, 2)
    key = rotate(projected[:, 1], cos_table, sin_table).astype(BF16).transpose(1, 0, 2)
    value = projected[:, 2].astype(BF16).transpose(1, 0, 2)
    attended_grad = (dot_nt(cot, wdense) + dot(dense_cg, dense_down)).astype(BF16)
    head_grad = attended_grad.reshape(length, heads, HD).transpose(1, 0, 2)

    scale = HD ** (-0.5)

    def bmm(spec, a, b):
        return jnp.einsum(spec, a, b, preferred_element_type=F32)

    key_grad = jnp.zeros((heads, length, HD), F32)
    value_grad = jnp.zeros((heads, length, HD), F32)
    attended_parts = []
    query_parts = []
    for b in range(length // BLOCK):
        lo, hi = b * BLOCK, (b + 1) * BLOCK
        q = query[:, lo:hi]
        k = key[:, :hi]
        v = value[:, :hi]
        g = head_grad[:, lo:hi]
        scores = bmm("hqd,hkd->hqk", q, k) * scale
        row_max = jnp.max(scores, axis=-1, keepdims=True)
        exponent = jnp.exp(scores - row_max)
        prob = exponent / jnp.sum(exponent, axis=-1, keepdims=True)
        prob_low = prob.astype(BF16)
        attended_parts.append(bmm("hqk,hkd->hqd", prob_low, v).astype(BF16))
        prob_grad = bmm("hqd,hkd->hqk", g, v)
        row_dot = jnp.sum(prob_grad * prob, axis=-1, keepdims=True)
        score_grad = (prob * (prob_grad - row_dot)).astype(BF16)
        query_parts.append((bmm("hqk,hkd->hqd", score_grad, k) * scale).astype(BF16))
        key_grad = key_grad.at[:, :hi].add(bmm("hqk,hqd->hkd", score_grad, q) * scale)
        value_grad = value_grad.at[:, :hi].add(bmm("hqk,hqd->hkd", prob_low, g))

    def rows_first(x):
        return x.transpose(1, 0, 2)

    attended = rows_first(jnp.concatenate(attended_parts, axis=1)).reshape(length, mine)
    query_grad = rows_first(jnp.concatenate(query_parts, axis=1)).astype(F32)
    key_back = rows_first(key_grad.astype(BF16)).astype(F32)
    value_back = rows_first(value_grad.astype(BF16)).reshape(length, mine)
    projected_grad = jnp.concatenate(
        [
            rotate(query_grad, cos_table, -sin_table).astype(BF16).reshape(length, mine),
            rotate(key_back, cos_table, -sin_table).astype(BF16).reshape(length, mine),
            value_back,
        ],
        axis=1,
    )

    pre_act = (
        dot(normed, winner)
        + own(inner_bias[None], units).astype(F32)
        + ADAPTER_SCALE * dot(inner_coeff, inner_up)
    )
    act32, gelu_back = jax.vjp(lambda v: jax.nn.gelu(v, approximate=True), pre_act)
    activated = act32.astype(BF16)
    act_grad = dot_nt(cot, wouter) + dot(outer_cg, outer_down)
    pre_grad = gelu_back(act_grad)[0].astype(BF16)

    def scatter(x):
        return lax.psum_scatter(x, "seq", scatter_dimension=0, tiled=True)

    branch = scatter((dot(attended, wdense) + dot(activated, wouter)))
    coeff_sum = scatter(
        jnp.concatenate([dot_nt(attended, dense_down), dot_nt(activated, outer_down)], axis=1)
    )
    back = dot_nt(pre_grad, winner)
    for c in range(3):
        back = back + dot_nt(projected_grad[:, c * mine : (c + 1) * mine], wqkv[c])
    back = scatter(back)
    cg_sum = scatter(
        ADAPTER_SCALE
        * jnp.concatenate([dot_nt(projected_grad, qkv_up), dot_nt(pre_grad, inner_up)], axis=1)
    )
    late_own = jnp.concatenate([coeff_sum, cg_sum], axis=1).astype(BF16)
    late = lax.all_gather(late_own, "seq", axis=0, tiled=True)

    layer_out = (
        source
        + branch
        + dense_bias.astype(F32)
        + outer_bias.astype(F32)
        + ADAPTER_SCALE
        * dot(late_own[:, : 2 * RANK], jnp.concatenate([dense_up, outer_up], axis=0))
    ).astype(BF16)
    normed_grad = back + dot(
        late_own[:, 2 * RANK :], jnp.concatenate([qkv_down, inner_down], axis=0)
    )
    row_mean = jnp.mean(source, axis=-1, keepdims=True)
    centred = source - row_mean
    inv = lax.rsqrt(jnp.mean(centred * centred, axis=-1, keepdims=True) + EPSILON)
    xhat = centred * inv
    e = normed_grad * gain
    input_grad = cotangent.astype(F32) + inv * (
        e
        - jnp.mean(e, axis=-1, keepdims=True)
        - xhat * jnp.mean(e * xhat, axis=-1, keepdims=True)
    )

    share = width // groups
    cot_mine = own(cot, share)
    normed_mine = own(normed, share)
    qkv_up_g = ADAPTER_SCALE * dot_tn(qkv_coeff, projected_grad)
    inner_up_g = ADAPTER_SCALE * dot_tn(inner_coeff, pre_grad)
    dense_down_g = dot_tn(dense_cg, attended)
    outer_down_g = dot_tn(outer_cg, activated)
    ups = ADAPTER_SCALE * dot_tn(late[:, : 2 * RANK], cot_mine)
    downs = dot_tn(late[:, 2 * RANK :], normed_mine)
    mine_grads = [
        downs[:RANK],
        qkv_up_g,
        dense_down_g,
        ups[:RANK],
        downs[RANK:],
        inner_up_g,
        outer_down_g,
        ups[RANK:],
    ]
    packed = jnp.concatenate(mine_grads, axis=1)
    sizes = [g.shape[1] for g in mine_grads]
    outs = deliver(packed, sizes, counts, pick, planes, groups)
    return (layer_out, input_grad, *outs)


def solution(mesh):
    both = P(("fsdp", "seq"), None)
    placed = (
        both,
        both,
        P(),
        P(None, "fsdp", "seq"),
        P("seq", "fsdp"),
        P("fsdp", "seq"),
        P("seq", "fsdp"),
    ) + (P(),) * 6 + (both,) * 8
    return jax.shard_map(
        on_device, mesh=mesh, in_specs=placed, out_specs=(both,) * 10, check_vma=False
    )
```

```python
import functools

import jax
import jax.numpy as jnp
import numpy as np
from jax import lax
from jax.experimental import pallas as pl
from jax.experimental.pallas import tpu as pltpu
from jax.sharding import PartitionSpec as P

H = 32
HD = 64
ROT = 32
RANK = 16
ADAPT = 8
BLOCK = 256
EPSILON = 1e-05
ADAPTER_SCALE = 2.0
ROPE_BASE = 10000.0
MASKED = -1e30
F32 = jnp.float32
BF16 = jnp.bfloat16


def dot(a, b, dims=((1,), (0,))):
    return lax.dot_general(a, b, (dims, ((), ())), preferred_element_type=F32)


def dot_nt(a, b):
    return dot(a, b, ((1,), (1,)))


def dot_tn(a, b):
    return dot(a, b, ((0,), (0,)))


def norm_layer(values, scale_gain, offset_bias):
    row_mean = jnp.mean(values, axis=-1, keepdims=True)
    centred = values - row_mean
    spread = jnp.mean(centred * centred, axis=-1, keepdims=True)
    return centred * lax.rsqrt(spread + EPSILON) * scale_gain + offset_bias


def rope_tables(length, heads):
    frequency = ROPE_BASE ** (-2.0 * jnp.arange(ROT // 2, dtype=F32) / ROT)
    angles = jnp.arange(length).astype(F32)[:, None] * frequency[None, :]
    return jnp.cos(angles)[:, None, :], jnp.sin(angles)[:, None, :]


def rotate(values, cos_table, sin_table):
    a = values[..., : ROT // 2]
    b = values[..., ROT // 2 : ROT]
    return jnp.concatenate(
        [a * cos_table - b * sin_table, b * cos_table + a * sin_table, values[..., ROT:]], axis=-1
    )


MESH = pl.DeviceIdType.MESH
TILE = 256
UNIT = 256


def rope_constants(length):
    frequency = ROPE_BASE ** (-2.0 * np.arange(ROT // 2, dtype=np.float64) / ROT)
    angles = np.arange(length, dtype=np.float64)[:, None] * frequency[None, :]
    cos = np.ones((length, HD))
    sin = np.zeros((length, HD))
    half = ROT // 2
    cos[:, :half] = np.cos(angles)
    cos[:, half:ROT] = np.cos(angles)
    sin[:, :half] = -np.sin(angles)
    sin[:, half:ROT] = np.sin(angles)
    return (
        jnp.asarray(np.tile(cos, (1, 2)), F32),
        jnp.asarray(np.tile(sin, (1, 2)), F32),
    )


def turn(x, cos, sin, sign):
    lane = lax.broadcasted_iota(jnp.int32, x.shape, 1) % HD
    partner = jnp.where(
        lane < ROT // 2,
        pltpu.roll(x, x.shape[1] - ROT // 2, 1),
        pltpu.roll(x, ROT // 2, 1),
    )
    return x * cos + partner * (sin * sign)


def turn_all(x, cos, sin, sign):
    step = cos.shape[1]
    return jnp.concatenate(
        [turn(x[:, i : i + step], cos, sin, sign) for i in range(0, x.shape[1], step)], axis=1
    )


def layer_kernel(
    planes,
    tok_ref,
    cotown_ref,
    wq_in,
    wd_in,
    wi_in,
    wo_in,
    qb_ref,
    db_ref,
    ib_ref,
    ob_ref,
    gain_ref,
    shift_ref,
    index_ref,
    map_refs,
    cos_ref,
    sin_ref,
    out_ref,
    igrad_ref,
    grad_refs,
    stack,
    sel,
    adm,
    downs_ref,
    ups_ref,
    ddown_all,
    qup_all,
    iup_ref,
    odown_ref,
    qgrad,
    a_msg,
    a_h1,
    a_h2,
    b_msg,
    b_h1,
    b_h2,
    q_h1,
    q_h2,
    normed,
    cot,
    wq,
    wd,
    wi,
    wo,
    qkv,
    hg,
    att,
    pg,
    acc_a,
    acc_b,
    pre,
    act,
    ag,
    pgrad,
    coeff,
    cgs,
    coeff_t,
    cgs_t,
    res,
    keep,
    s1_send,
    s1_recv,
    a_send,
    a_recv,
    c_send,
    c_recv,
    ar_send,
    ar_recv,
    local_sem,
    zs_sem,
    zr_sem,
    ag_ssem,
    ag_rsem,
    s1_ssem,
    s1_rsem,
    a_ssem,
    a_rsem,
    c_ssem,
    c_rsem,
    ar_ssem,
    ar_rsem,
    adz_ssem,
    adz_rsem,
    h1_ssem,
    h1_rsem,
    h2_ssem,
    h2_rsem,
    q1_ssem,
    q1_rsem,
    q2_ssem,
    q2_rsem,
):
    z = lax.axis_index("fsdp")
    s = lax.axis_index("seq")
    core = s % 2
    chip = s // 2
    to_core = (z, chip * 2 + (1 - core))
    chip_x = chip + 1 - 2 * (chip % 2)
    chip_y = (chip + 2) % 4
    chip_d = chip_x + 2 - 4 * (chip_x // 2)
    to_x = (z, chip_x * 2 + core)
    to_y = (z, chip_y * 2 + core)
    rows, width = tok_ref.shape
    length = normed.shape[0]
    units = act.shape[1]
    fan = width // planes
    mine = wq.shape[3]
    tiles = length // TILE

    def remote(src, dst, ssem, rsem, where):
        return pltpu.make_async_remote_copy(
            src_ref=src, dst_ref=dst, send_sem=ssem, recv_sem=rsem, device_id=where,
            device_id_type=MESH,
        )

    def block(i, n):
        return pl.ds(pl.multiple_of(i * n, n), n)

    bar = pltpu.get_barrier_semaphore()
    for k in range(1, 8):
        pl.semaphore_signal(bar, inc=1, device_id=(z, (s + k) % 8), device_id_type=MESH)
    for k in range(1, planes):
        pl.semaphore_signal(bar, inc=1, device_id=((z + k) % planes, s), device_id_type=MESH)
    pl.semaphore_wait(bar, 7 + planes - 1)

    chunks = []
    for c in range(3):
        chunks.append((wq_in.at[c], lambda j, c=c: wq.at[j, c]))
    chunks.append((wd_in, lambda j: wd.at[j]))
    part = fan // 4
    for i in range(4):
        chunks.append(
            (
                wi_in.at[pl.ds(i * part, part), :],
                lambda j, i=i: wi.at[j, pl.ds(i * part, part), :],
            )
        )
    deep = units // 2
    for j2 in range(fan // UNIT):
        for i in range(2):
            chunks.append(
                (
                    wo_in.at[pl.ds(i * deep, deep), pl.ds(j2 * UNIT, UNIT)],
                    lambda j, i=i, j2=j2: wo.at[
                        j, pl.ds(i * deep, deep), pl.ds(j2 * UNIT, UNIT)
                    ],
                )
            )
    n_chunks = len(chunks)
    last_step = n_chunks + planes - 1

    def zcopy(c, direction, k):
        src, place = chunks[c]
        j = z - k if direction == 0 else z + k
        return remote(
            src if k == 0 else place(j),
            place(j),
            zs_sem.at[c, direction, k],
            zr_sem.at[c, j],
            (z + 1, s) if direction == 0 else (z - 1, s),
        )

    def zhas(direction, k):
        if direction == 0:
            return jnp.logical_and(z - k >= 0, z + 1 < planes)
        return jnp.logical_and(z + k < planes, z - 1 >= 0)

    def zsend(c, k):
        for direction in (0, 1):

            @pl.when(zhas(direction, k))
            def _(direction=direction):
                zcopy(c, direction, k).start()

    def zwait(c, k):
        for direction in (0, 1):
            j = z - k if direction == 0 else z + k
            there = z - k >= 0 if direction == 0 else z + k < planes

            @pl.when(there)
            def _(j=j, direction=direction):
                place = chunks[c][1](j)
                pltpu.make_async_copy(place, place, zr_sem.at[c, j]).wait()

    def zstep(t):
        if t == 0:
            zsend(0, 0)
            zsend(1, 0)
        elif t + 1 < n_chunks:
            zsend(t + 1, 0)
        for k in range(1, planes):
            c = t - k
            if 0 <= c < n_chunks:
                zwait(c, k)
                if k < planes - 1:
                    zsend(c, k)

    own = []
    for c in range(n_chunks):
        src, place = chunks[c]
        own.append(pltpu.make_async_copy(src, place(z), local_sem.at[c]))
    for copy in own:
        copy.start()

    zstep(0)

    half = width // 2

    def row_view(buf, b, part):
        if part is None:
            return buf.at[block(b, rows), :]
        return buf.at[block(b, rows), pl.ds(part * half, half)]

    def lead_view(buf, b, part):
        if part is None:
            return buf.at[b]
        return buf.at[b, pl.ds(part * (planes // 2), planes // 2)]

    def gather_copies(p, buf, view):
        bx = chip_x * 2 + core
        by = chip_y * 2 + core
        bd = chip_d * 2 + core
        me = view(buf, s, None)
        blk_x = view(buf, bx, None)
        blk_y = view(buf, by, None)
        blk_d = view(buf, bd, None)
        x0 = view(buf, bx, 0)
        y1 = view(buf, by, 1)
        d0 = view(buf, bd, 0)
        d1 = view(buf, bd, 1)
        ss, rs = ag_ssem.at[p], ag_rsem.at[p]

        def same(ref, i, where):
            return remote(ref, ref, ss.at[i], rs.at[i], where)

        sends = [
            same(me, 0, to_x),
            same(me, 1, to_y),
            same(me, 2, to_core),
            same(x0, 3, to_y),
            same(blk_x, 4, to_core),
            same(y1, 5, to_x),
            same(blk_y, 6, to_core),
            same(blk_d, 7, to_core),
        ]
        other = 1 - core
        into = [
            blk_x,
            blk_y,
            view(buf, chip * 2 + other, None),
            d0,
            view(buf, chip_x * 2 + other, None),
            d1,
            view(buf, chip_y * 2 + other, None),
            view(buf, chip_d * 2 + other, None),
        ]

        def arrived(i):
            pltpu.make_async_copy(into[i], into[i], rs.at[i]).wait()

        return sends, arrived

    cot[block(s, rows), :] = cotown_ref[...]
    c_sends, c_arrived = gather_copies(0, cot, row_view)
    for i in range(3):
        c_sends[i].start()

    counts = [m.shape[0] for m in map_refs]
    spans = [2 * n if n % 128 else n for n in counts]
    bases = [sum(spans[:i]) for i in range(8)]
    stack[...] = jnp.zeros_like(stack)
    odd = s % 2
    for m, n, span, base in zip(map_refs, counts, spans, bases):
        at = base + (odd * n if span != n else 0)
        stack[pl.ds(pl.multiple_of(at, 64), n), :] = m[...]
    lane = lax.broadcasted_iota(jnp.int32, (RANK, ADAPT * RANK), 1)
    column = lax.broadcasted_iota(jnp.int32, (RANK, ADAPT * RANK), 0)
    picks = []
    for g in range(planes):
        picks.append((lane == column + index_ref[g] * RANK).astype(F32))
        sel[g] = dot_nt(picks[g].astype(BF16), stack[...]).astype(BF16)

    def adapter_copy(k):
        g = (z + k) % planes
        return remote(sel.at[g], adm.at[s, z], adz_ssem.at[k - 1], adz_rsem.at[z], (g, s))

    for k in range(1, planes):
        adapter_copy(k).start()
    adm[s, z] = sel[z]

    x = tok_ref[...].astype(F32)
    mean = jnp.mean(x, axis=-1, keepdims=True)
    centred = x - mean
    inv = lax.rsqrt(jnp.mean(centred * centred, axis=-1, keepdims=True) + EPSILON)
    normed[block(s, rows), :] = (
        centred * inv * gain_ref[...].astype(F32) + shift_ref[...].astype(F32)
    ).astype(BF16)
    n_sends, n_arrived = gather_copies(1, normed, row_view)
    for i in range(3):
        n_sends[i].start()
    for k in range(1, planes):
        g = (z + k) % planes
        pltpu.make_async_copy(adm.at[s, g], adm.at[s, g], adz_rsem.at[g]).wait()
    m_sends, m_arrived = gather_copies(2, adm, lead_view)
    for i in range(3):
        m_sends[i].start()
    gathers = ((c_sends, c_arrived), (n_sends, n_arrived), (m_sends, m_arrived))
    for sends, arrived in gathers:
        arrived(0)
        sends[3].start()
        sends[4].start()
        arrived(1)
        sends[5].start()
        sends[6].start()
    zstep(1)
    for sends, arrived in gathers:
        arrived(3)
        arrived(5)
        sends[7].start()
    for sends, arrived in gathers:
        for i in (2, 4, 6, 7):
            arrived(i)
    zstep(2)

    def order(f, carry):
        for pair in range(4):

            def both(i):
                cols = slice(bases[i], bases[i] + spans[i])
                return adm[2 * pair, f, :, cols] + adm[2 * pair + 1, f, :, cols]

            where = block(f * 4 + pair, 128)
            downs_ref[:RANK, where] = both(0)
            downs_ref[RANK:, where] = both(4)
            ups_ref[:RANK, where] = both(3)
            ups_ref[RANK:, where] = both(7)
            ddown_all[:, where] = both(2)
            qup_all[:, block(f * 4 + pair, spans[1])] = both(1)
        return carry

    lax.fori_loop(0, planes, order, 0)
    for j in range(4):
        q = s * 4 + j
        n = counts[5]
        iup_ref[:, j * n : (j + 1) * n] = adm[q % 8, q // 8, :, bases[5] : bases[5] + n]
        odown_ref[:, j * n : (j + 1) * n] = adm[q % 8, q // 8, :, bases[6] : bases[6] + n]

    def qup(c):
        return qup_all[:, pl.ds(pl.multiple_of(c * width + s * mine, mine), mine)]

    def ddown():
        return ddown_all[:, block(s, mine)]

    def low(t, carry):
        r = block(t, TILE)
        c = dot_nt(normed[r, :], downs_ref[...])
        coeff[r, :] = c.astype(BF16)
        g = ADAPTER_SCALE * dot_nt(cot[r, :], ups_ref[...])
        cgs[r, :] = g.astype(BF16)
        return carry

    lax.fori_loop(0, tiles, low, 0)
    for copy in own:
        copy.wait()
    zstep(3)
    zstep(4)
    zstep(5)
    zstep(6)

    def project(t, carry):
        r = block(t, TILE)
        cos = cos_ref[r, :]
        sin = sin_ref[r, :]
        for c in range(3):
            v = ADAPTER_SCALE * dot(coeff[r, :RANK], qup(c))
            v = v + qb_ref[c : c + 1, block(s, mine)].astype(F32)
            for j in range(planes):
                v = v + dot(normed[r, j * fan : (j + 1) * fan], wq[j, c])
            if c < 2:
                v = turn_all(v, cos, sin, 1.0)
            v = v.astype(BF16)
            if c == 0:
                v = v * jnp.asarray(HD**-0.5, BF16)
            qkv[c, r, :] = v
        g = dot(cgs[r, :RANK], ddown())
        for j in range(planes):
            g = g + dot_nt(cot[r, j * fan : (j + 1) * fan], wd[j])
        hg[r, :] = g.astype(BF16)
        return carry

    lax.fori_loop(0, tiles, project, 0)
    zstep(7)

    dk = ag.at[:, pl.ds(0, mine)]
    dv = ag.at[:, pl.ds(mine, mine)]
    ag[:, : 2 * mine] = jnp.zeros((length, 2 * mine), F32)
    heads = mine // HD

    for b in range(length // BLOCK):
        lo, hi = b * BLOCK, (b + 1) * BLOCK
        acc_a[...] = jnp.zeros_like(acc_a)
        acc_b[...] = jnp.zeros_like(acc_b)

        def one_head(h, carry, lo=lo, hi=hi):
            lane = lax.broadcasted_iota(jnp.int32, (1, mine), 1)
            mask = (lane // HD == h).astype(BF16)
            mask32 = (lane // HD == h).astype(F32)
            q = qkv[0, lo:hi, :] * mask
            g = hg[lo:hi, :] * mask
            k = qkv[1, :hi, :]
            v = qkv[2, :hi, :]
            sc = dot_nt(q, k)
            e = jnp.exp(sc - jnp.max(sc, axis=-1, keepdims=True))
            p = e * (1.0 / jnp.sum(e, axis=-1, keepdims=True))
            pb = p.astype(BF16)
            acc_a[...] += dot(pb, v) * mask32
            dp = dot_nt(g, v)
            ds = (p * (dp - jnp.sum(dp * p, axis=-1, keepdims=True))).astype(BF16)
            acc_b[...] += dot(ds, k) * mask32
            dk[:hi, :] += dot_tn(ds, q)
            dv[:hi, :] += dot_tn(pb, g)
            return carry

        lax.fori_loop(0, heads, one_head, 0)
        att[lo:hi, :] = acc_a[...].astype(BF16)
        back = (acc_b[...] * (HD**-0.5)).astype(BF16).astype(F32)
        pg[0, lo:hi, :] = turn_all(back, cos_ref[lo:hi, :], sin_ref[lo:hi, :], -1.0).astype(BF16)
        if b % 2 == 1:
            zstep(8 + b // 2)

    def finish(t, carry):
        r = block(t, TILE)
        back = dk[r, :].astype(BF16).astype(F32)
        pg[1, r, :] = turn_all(back, cos_ref[r, :], sin_ref[r, :], -1.0).astype(BF16)
        pg[2, r, :] = dv[r, :].astype(BF16)
        return carry

    lax.fori_loop(0, tiles, finish, 0)

    coeff_t[...] = dot_nt(downs_ref[...], normed[...]).astype(BF16)
    cgs_t[...] = (ADAPTER_SCALE * dot_nt(ups_ref[...], cot[...])).astype(BF16)

    share = width // 8

    def wait_on(ref, sem):
        pltpu.make_async_copy(ref, ref, sem).wait()

    def hop1(w, msg, h1, start):
        for j in range(4):
            to = 4 * (s % 2) + j
            there = (z, to)

            @pl.when(to != s)
            def _(j=j, there=there):
                copy = remote(
                    msg.at[j], h1.at[s // 2], h1_ssem.at[w, j], h1_rsem.at[w, s // 2], there
                )
                if start:
                    copy.start()
                else:
                    copy.wait_send()

            if start:

                @pl.when(to == s)
                def _(j=j):
                    pltpu.make_async_copy(
                        msg.at[j], h1.at[s // 2], h1_rsem.at[w, s // 2]
                    ).start()

    def hop2_copy(w, h1, h2, k):
        g = (z + k) % planes
        return remote(h1.at[g], h2.at[z], h2_ssem.at[w, k - 1], h2_rsem.at[w, z], (g, s))

    def hop2(w, h1, h2):
        for g in range(planes):
            wait_on(h1.at[g], h1_rsem.at[w, g])
        for k in range(1, planes):
            hop2_copy(w, h1, h2, k).start()
        h2[z] = h1[z]

    def landed(w, h1, h2):
        for k in range(1, planes):
            g = (z + k) % planes
            wait_on(h2.at[g], h2_rsem.at[w, g])
        for k in range(1, planes):
            hop2_copy(w, h1, h2, k).wait_send()

    def place(parts, i, rows_of):
        full = None
        for g in range(planes):
            v = lax.dot_general(
                parts[g], picks[g], (((0,), (0,)), ((), ())),
                precision=lax.Precision.HIGHEST, preferred_element_type=F32,
            )
            full = v if full is None else full + v
        grad_refs[i][...] = rows_of(full)

    def half_rows(v):
        return jnp.where(s % 2 == 0, v[:64], v[64:])

    def all_rows(v):
        return v

    for c in range(3):
        g = ADAPTER_SCALE * dot(coeff_t[:RANK, :], pg[c])
        for i in range(2):
            qgrad[2 * c + i] = g[:, i * 128 : (i + 1) * 128]

    def qkv_hop1(start):
        for c in range(3):
            for i in range(2):
                t = 16 * c + 2 * s + i
                for o in range(2):
                    owner = 2 * (t // 3) + o
                    slot = t % 3 - o
                    ok = jnp.logical_and(slot >= 0, slot <= 1)
                    to = owner % 8
                    src = qgrad.at[2 * c + i]
                    n = 4 * c + 2 * i + o

                    @pl.when(jnp.logical_and(ok, to != s))
                    def _(src=src, owner=owner, slot=slot, to=to, n=n):
                        copy = remote(
                            src, q_h1.at[owner // 8, slot], q1_ssem.at[n],
                            q1_rsem.at[owner // 8, slot], (z, to),
                        )
                        if start:
                            copy.start()
                        else:
                            copy.wait_send()

                    if start:

                        @pl.when(jnp.logical_and(ok, to == s))
                        def _(src=src, owner=owner, slot=slot):
                            pltpu.make_async_copy(
                                src, q_h1.at[owner // 8, slot], q1_rsem.at[owner // 8, slot]
                            ).start()

    def qkv_hop2_copy(k):
        g = (z + k) % planes
        return remote(q_h1.at[g], q_h2.at[z], q2_ssem.at[k - 1], q2_rsem.at[z], (g, s))

    def qkv_hop2():
        for g in range(planes):
            for slot in range(2):
                wait_on(q_h1.at[g, slot], q1_rsem.at[g, slot])
        for k in range(1, planes):
            qkv_hop2_copy(k).start()
        q_h2[z] = q_h1[z]

    def qkv_landed():
        for k in range(1, planes):
            g = (z + k) % planes
            wait_on(q_h2.at[g], q2_rsem.at[g])
        for k in range(1, planes):
            qkv_hop2_copy(k).wait_send()

    qkv_hop1(True)
    g = dot(cgs_t[:RANK, :], att[...])
    for j in range(4):
        a_msg[j, :, 256:384] = g[:, (j // 2) * 128 : (j // 2 + 1) * 128]
    zstep(10)

    k0 = 0.7978845608028654
    k1 = 0.044715

    def inner(t, carry):
        r = block(t, TILE)
        v = ADAPTER_SCALE * dot(coeff[r, RANK : 2 * RANK], iup_ref[...])
        v = v + ib_ref[:, block(s, units)].astype(F32)
        for j in range(planes):
            v = v + dot(normed[r, j * fan : (j + 1) * fan], wi[j])
        sq = v * v
        th = jnp.tanh(k0 * v * (1.0 + k1 * sq))
        act[r, :] = (0.5 * v * (1.0 + th)).astype(BF16)
        pre[r, :] = 0.5 * (1.0 + th) + 0.5 * v * (1.0 - th * th) * (k0 * (1.0 + 3.0 * k1 * sq))
        return carry

    lax.fori_loop(0, tiles, inner, 0)
    g = dot(cgs_t[RANK : 2 * RANK, :], act[...])
    for j in range(4):
        a_msg[j, :, :256] = g[:, j * 256 : (j + 1) * 256]
    qkv_hop2()
    zstep(11)

    partners = (to_core, to_x, to_y)

    def reduce_copy(w, i):
        return remote(
            ar_send.at[w], ar_recv.at[w, i], ar_ssem.at[w, i], ar_rsem.at[w, i], partners[i]
        )

    def reduce_round(w, i):
        if i > 0:
            reduce_copy(w, i - 1).wait()
            ar_send[w] += ar_recv[w, i - 1]
        if i < 3:
            reduce_copy(w, i).start()

    ar_send[0, :RANK, :] = dot_nt(ddown(), att[...])
    ar_send[0, RANK : 2 * RANK, :] = dot_nt(odown_ref[...], act[...])
    for i in range(4):
        reduce_round(0, i)
    coeff_dense = ar_send[0].astype(BF16)
    for i in range(2):
        g = ADAPTER_SCALE * dot(
            coeff_dense[i * RANK : (i + 1) * RANK, :], cot[:, block(s, share)]
        )
        for j in range(4):
            at = 384 + i * 128
            a_msg[j, :, at : at + 128] = g[:, (j // 2) * 128 : (j // 2 + 1) * 128]
    hop1(0, a_msg, a_h1, True)

    p_units = width // UNIT
    per = fan // UNIT
    early = p_units - planes
    total = 2 * p_units

    def place_of(n):
        first = n < p_units
        j = jnp.where(first, n % planes, (n - p_units) // per)
        i = jnp.where(first, n // planes, (n - p_units) % per)
        return j, i

    def keep_split(n, k, r):
        slot = n % 2
        a = r[:rows, :]
        b = r[rows:, :]
        first = core == 0
        keep[n % 4, k] = jnp.where(first, a, b)
        s1_send[slot, k] = jnp.where(first, b, a).astype(BF16)

    def s1_copy(n):
        return remote(s1_send.at[n % 2], s1_recv.at[n], s1_ssem.at[n % 2], s1_rsem.at[n], to_core)

    def a_copy(n, i):
        return remote(
            a_send.at[n % 2, i], a_recv.at[n, i], a_ssem.at[n % 2, i], a_rsem.at[n, i],
            (to_x, to_y)[i],
        )

    def c_copy(n, i):
        return remote(
            c_send.at[n % 2, i], c_recv.at[n, i], c_ssem.at[n % 2, i], c_rsem.at[n, i],
            (to_x, to_y)[i],
        )

    hu = UNIT // 2

    def stage0_branch(n):
        j, i = place_of(n)

        def tile(k, carry):
            r = block(k, TILE)
            cols = block(i, UNIT)
            keep_split(n, k, dot(act[r, :], wo[j, :, cols]) + dot(att[r, :], wd[j, :, cols]))
            return carry

        lax.fori_loop(0, tiles, tile, 0)
        s1_copy(n).start()

    def stage0_back(n):
        j, i = place_of(n)

        def tile(k, carry):
            r = block(k, TILE)
            rws = block(i, UNIT)
            v = dot_nt(pgrad[r, :], wi[j, rws, :])
            for c in range(3):
                v = v + dot_nt(pg[c, r, :], wq[j, c, rws, :])
            keep_split(n, k, v)
            return carry

        lax.fori_loop(0, tiles, tile, 0)
        s1_copy(n).start()

    def stage1(n):
        s1_copy(n).wait()
        q = n % 4
        for k in range(4):
            keep[q, k] += s1_recv[n, k].astype(F32)
        far = keep[q, chip_d]
        a_send[n % 2, 0] = far[:, :hu].astype(BF16)
        a_send[n % 2, 1] = far[:, hu:].astype(BF16)
        for i in range(2):
            a_copy(n, i).start()

    def stage2(n):
        q = n % 4
        for i in range(2):
            a_copy(n, i).wait()
        keep[q, chip_y, :, :hu] += a_recv[n, 0].astype(F32)
        keep[q, chip_x, :, hu:] += a_recv[n, 1].astype(F32)
        c_send[n % 2, 0] = keep[q, chip_x].astype(BF16)
        c_send[n % 2, 1] = keep[q, chip_y].astype(BF16)
        for i in range(2):
            c_copy(n, i).start()

    def stage3(n):
        q = n % 4
        for i in range(2):
            c_copy(n, i).wait()
        j, i = place_of(n)
        v = keep[q, chip] + c_recv[n, 0].astype(F32) + c_recv[n, 1].astype(F32)
        cols = block(j * per + i, UNIT)

        @pl.when(n < p_units)
        def _():
            res[:, cols] = v

        @pl.when(n >= p_units)
        def _():
            igrad_ref[:, cols] = v

    def pipeline(first, lo, hi, stage0, extra=None):
        def body(n, carry):
            if stage0 is not None:
                stage0(n)
            for back, stage in ((1, stage1), (2, stage2), (3, stage3)):
                m = n - back
                ok = m >= first
                if stage0 is None:
                    ok = jnp.logical_and(ok, m < hi - 3)

                @pl.when(ok)
                def _(m=m, stage=stage):
                    stage(m)

            if extra is not None:
                extra(n)
            return carry

        lax.fori_loop(lo, hi, body, 0)

    zstep(12)
    pipeline(0, 0, early, stage0_branch)
    pipeline(0, early, early + 3, None)

    def act_back(t, carry):
        r = block(t, TILE)
        v = dot(cgs[r, RANK : 2 * RANK], odown_ref[...])
        for j in range(planes):
            for i in range(per - 1):
                c0 = j * fan + i * UNIT
                v = v + dot_nt(cot[r, c0 : c0 + UNIT], wo[j, :, i * UNIT : (i + 1) * UNIT])
        ag[r, :] = v
        return carry

    hop2(0, a_h1, a_h2)
    lax.fori_loop(0, tiles, act_back, 0)
    qkv_landed()
    landed(0, a_h1, a_h2)
    place([a_h2[g, :, :256] for g in range(planes)], 6, all_rows)
    place([a_h2[g, :, 256:384] for g in range(planes)], 2, half_rows)
    place([a_h2[g, :, 384:512] for g in range(planes)], 3, half_rows)
    place([a_h2[g, :, 512:640] for g in range(planes)], 7, half_rows)

    def qkv_rows(v):
        return jnp.where(s % 2 == 0, v[:192], v[64:])

    place(
        [jnp.concatenate([q_h2[g, 0], q_h2[g, 1]], axis=1) for g in range(planes)], 1, qkv_rows
    )
    for t in range(13, last_step):
        zstep(t)

    pipeline(early, early, p_units, stage0_branch)

    def act_last(t, carry):
        r = block(t, TILE)
        v = ag[r, :]
        for j in range(planes):
            i = per - 1
            c0 = j * fan + i * UNIT
            v = v + dot_nt(cot[r, c0 : c0 + UNIT], wo[j, :, i * UNIT : (i + 1) * UNIT])
        pgrad[r, :] = (v * pre[r, :]).astype(BF16)
        return carry

    lax.fori_loop(0, tiles, act_last, 0)

    up_part = dot_nt(iup_ref[...], pgrad[...])
    q_part = dot_nt(qup(0), pg[0])
    for c in range(1, 3):
        q_part = q_part + dot_nt(qup(c), pg[c])
    ar_send[1, :RANK, :] = ADAPTER_SCALE * q_part
    ar_send[1, RANK : 2 * RANK, :] = ADAPTER_SCALE * up_part
    reduce_round(1, 0)

    def rounds(n):
        for i in range(1, 4):

            @pl.when(n == p_units + 2 * i - 1)
            def _(i=i):
                reduce_round(1, i)
                if i == 2:
                    g = ADAPTER_SCALE * dot(coeff_t[RANK : 2 * RANK, :], pgrad[...])
                    for j in range(4):
                        b_msg[j, :, :256] = g[:, j * 256 : (j + 1) * 256]
                if i == 3:
                    g = dot(ar_send[1].astype(BF16), normed[:, block(s, share)])
                    for m in range(2):
                        for j in range(4):
                            b_msg[j, :, 256 + m * 128 : 384 + m * 128] = g[
                                m * RANK : (m + 1) * RANK, (j // 2) * 128 : (j // 2 + 1) * 128
                            ]
                    hop1(1, b_msg, b_h1, True)

    pipeline(early, p_units, total, stage0_back, rounds)
    hop2(1, b_h1, b_h2)
    pipeline(early, total, total + 3, None)

    first_t = ar_send[0, :, block(s, rows)].astype(BF16)
    late_t = ar_send[1, :, block(s, rows)].astype(BF16)
    out = tok_ref[...].astype(F32) + res[...] + ADAPTER_SCALE * dot_tn(first_t, ups_ref[...])
    out_ref[...] = (out + db_ref[...].astype(F32) + ob_ref[...].astype(F32)).astype(BF16)
    x = tok_ref[...].astype(F32)
    mean = jnp.mean(x, axis=-1, keepdims=True)
    centred = x - mean
    inv = lax.rsqrt(jnp.mean(centred * centred, axis=-1, keepdims=True) + EPSILON)
    xhat = centred * inv
    e = (igrad_ref[...] + dot_tn(late_t, downs_ref[...])) * gain_ref[...].astype(F32)
    igrad_ref[...] = cotown_ref[...].astype(F32) + inv * (
        e
        - jnp.mean(e, axis=-1, keepdims=True)
        - xhat * jnp.mean(e * xhat, axis=-1, keepdims=True)
    )

    landed(1, b_h1, b_h2)
    place([b_h2[g, :, :256] for g in range(planes)], 5, all_rows)
    place([b_h2[g, :, 256:384] for g in range(planes)], 0, half_rows)
    place([b_h2[g, :, 384:512] for g in range(planes)], 4, half_rows)

    hop1(0, a_msg, a_h1, False)
    hop1(1, b_msg, b_h1, False)
    qkv_hop1(False)
    for k in range(1, planes):
        adapter_copy(k).wait_send()
    for sends, _ in gathers:
        for copy in sends:
            copy.wait_send()
    for c in range(n_chunks):
        for k in range(planes - 1):
            for direction in (0, 1):

                @pl.when(zhas(direction, k))
                def _(c=c, k=k, direction=direction):
                    zcopy(c, direction, k).wait_send()


def run_layer(planes, args, shapes):
    rows, width, length, units, mine = shapes
    fan = width // planes
    vm = pl.BlockSpec(memory_space=pltpu.VMEM)
    hbm = pl.BlockSpec(memory_space=pl.ANY)
    n_chunks = 8 + 2 * (fan // UNIT)
    total = 2 * width // UNIT
    dma = pltpu.SemaphoreType.DMA
    maps = args[13:21]
    lanes = sum(2 * m.shape[0] if m.shape[0] % 128 else m.shape[0] for m in maps)

    def entry(*refs):
        layer_kernel(planes, *refs[:13], refs[13:21], *refs[21:25], refs[25:33], *refs[33:])

    return pl.pallas_call(
        entry,
        out_shape=(
            jax.ShapeDtypeStruct((rows, width), BF16),
            jax.ShapeDtypeStruct((rows, width), F32),
            *(jax.ShapeDtypeStruct(m.shape, F32) for m in maps),
        ),
        in_specs=[vm, vm, hbm, hbm, hbm, hbm]
        + [vm] * 6
        + [pl.BlockSpec(memory_space=pltpu.SMEM)]
        + [vm] * 10,
        out_specs=(vm,) * 10,
        scratch_shapes=[
            pltpu.VMEM((lanes, ADAPT * RANK), BF16),
            pltpu.VMEM((planes, RANK, lanes), BF16),
            pltpu.VMEM((8, planes, RANK, lanes), BF16),
            pltpu.VMEM((2 * RANK, width), BF16),
            pltpu.VMEM((2 * RANK, width), BF16),
            pltpu.VMEM((RANK, width), BF16),
            pltpu.VMEM((RANK, 3 * width), BF16),
            pltpu.VMEM((RANK, units), BF16),
            pltpu.VMEM((RANK, units), BF16),
            pltpu.VMEM((6, RANK, 128), F32),
            pltpu.VMEM((4, RANK, 640), F32),
            pltpu.VMEM((planes, RANK, 640), F32),
            pltpu.VMEM((planes, RANK, 640), F32),
            pltpu.VMEM((4, RANK, 512), F32),
            pltpu.VMEM((planes, RANK, 512), F32),
            pltpu.VMEM((planes, RANK, 512), F32),
            pltpu.VMEM((planes, 2, RANK, 128), F32),
            pltpu.VMEM((planes, 2, RANK, 128), F32),
            pltpu.VMEM((length, width), BF16),
            pltpu.VMEM((length, width), BF16),
            pltpu.VMEM((planes, 3, fan, mine), BF16),
            pltpu.VMEM((planes, mine, fan), BF16),
            pltpu.VMEM((planes, fan, units), BF16),
            pltpu.VMEM((planes, units, fan), BF16),
            pltpu.VMEM((3, length, mine), BF16),
            pltpu.VMEM((length, mine), BF16),
            pltpu.VMEM((length, mine), BF16),
            pltpu.VMEM((3, length, mine), BF16),
            pltpu.VMEM((BLOCK, mine), F32),
            pltpu.VMEM((BLOCK, mine), F32),
            pltpu.VMEM((length, units), F32),
            pltpu.VMEM((length, units), BF16),
            pltpu.VMEM((length, units), F32),
            pltpu.VMEM((length, units), BF16),
            pltpu.VMEM((length, 2 * RANK), BF16),
            pltpu.VMEM((length, 2 * RANK), BF16),
            pltpu.VMEM((2 * RANK, length), BF16),
            pltpu.VMEM((2 * RANK, length), BF16),
            pltpu.VMEM((rows, width), F32),
            pltpu.VMEM((4, 4, rows, UNIT), F32),
            pltpu.VMEM((2, 4, rows, UNIT), BF16),
            pltpu.VMEM((total, 4, rows, UNIT), BF16),
            pltpu.VMEM((2, 2, rows, UNIT // 2), BF16),
            pltpu.VMEM((total, 2, rows, UNIT // 2), BF16),
            pltpu.VMEM((2, 2, rows, UNIT), BF16),
            pltpu.VMEM((total, 2, rows, UNIT), BF16),
            pltpu.VMEM((2, 2 * RANK, length), F32),
            pltpu.VMEM((2, 3, 2 * RANK, length), F32),
            dma((n_chunks,)),
            dma((n_chunks, 2, planes)),
            dma((n_chunks, planes)),
            dma((3, 8)),
            dma((3, 8)),
            dma((2,)),
            dma((total,)),
            dma((2, 2)),
            dma((total, 2)),
            dma((2, 2)),
            dma((total, 2)),
            dma((2, 3)),
            dma((2, 3)),
            dma((planes,)),
            dma((planes,)),
            dma((2, 4)),
            dma((2, planes)),
            dma((2, planes)),
            dma((2, planes)),
            dma((12,)),
            dma((planes, 2)),
            dma((planes,)),
            dma((planes,)),
        ],
        compiler_params=pltpu.CompilerParams(
            collective_id=0, has_side_effects=True, vmem_limit_bytes=63 * 1024 * 1024
        ),
    )(*args)


def fits(planes, groups, shapes):
    rows, width, length, units, mine = shapes
    return (
        groups == 8
        and planes == 4
        and rows * 2 == TILE
        and length <= 1024
        and width == 2048
        and mine == 256
        and units == 1024
    )


def deliver(packed, sizes, counts, pick, planes, groups):
    s = lax.axis_index("seq")
    everyone = lax.all_gather(packed, "seq", axis=0, tiled=False)
    owned = []
    at = 0
    for i, (n, w) in enumerate(zip(counts, sizes)):
        part = everyone[:, :, at : at + w]
        at += w
        blocks = 3 if i == 1 else 1
        part = part.reshape(groups, RANK, blocks, w // blocks).transpose(1, 2, 0, 3)
        part = part.reshape(RANK, planes, groups, n)
        owned.append(lax.dynamic_index_in_dim(part, s, 2, keepdims=False))
    owned = jnp.concatenate(owned, axis=2).transpose(1, 0, 2)
    arrived = lax.all_to_all(owned, "fsdp", split_axis=0, concat_axis=0, tiled=True)
    place = pick.astype(F32).reshape(planes * RANK, ADAPT * RANK)
    spread = lax.dot_general(
        arrived.reshape(planes * RANK, -1),
        place,
        (((0,), (0,)), ((), ())),
        precision=lax.Precision.HIGHEST,
        preferred_element_type=F32,
    )
    outs = []
    at = 0
    for n in counts:
        outs.append(spread[at : at + n])
        at += n
    return outs


def on_device(
    tokens,
    cotangent,
    adapter_index,
    qkv_weight,
    dense_weight,
    inner_weight,
    outer_weight,
    qkv_bias,
    dense_bias,
    inner_bias,
    outer_bias,
    norm_gain,
    norm_bias,
    *maps,
):
    planes = lax.axis_size("fsdp")
    groups = lax.axis_size("seq")
    rows, width = tokens.shape
    length = rows * groups
    heads = H // groups
    mine = heads * HD
    units = inner_weight.shape[1]
    s = lax.axis_index("seq")

    shapes = (rows, width, length, units, mine)
    if fits(planes, groups, shapes):
        return run_layer(
            planes,
            (
                tokens,
                cotangent,
                qkv_weight,
                dense_weight,
                inner_weight,
                outer_weight,
                qkv_bias.reshape(3, width),
                dense_bias[None],
                inner_bias[None],
                outer_bias[None],
                norm_gain[None],
                norm_bias[None],
                adapter_index,
                *maps,
                *rope_constants(length),
            ),
            shapes,
        )

    counts = [m.shape[0] for m in maps]
    stacked = jnp.concatenate(maps, axis=0)
    wanted = (adapter_index[:, None] * RANK + jnp.arange(RANK)[None, :]).reshape(-1)
    pick = (wanted[:, None] == jnp.arange(ADAPT * RANK)[None, :]).astype(BF16)
    chosen = dot_nt(pick, stacked).astype(BF16).reshape(planes, RANK, -1)
    chosen = lax.all_to_all(chosen, "fsdp", split_axis=0, concat_axis=0, tiled=True)
    chosen = lax.all_gather(chosen, "seq", axis=1, tiled=False)
    full = []
    at = 0
    for n in counts:
        part = chosen[:, :, :, at : at + n]
        full.append(part.transpose(2, 0, 1, 3).reshape(RANK, -1))
        at += n
    qkv_down, qkv_up, dense_down, dense_up, inner_down, inner_up, outer_down, outer_up = full

    def own(m, n):
        return lax.dynamic_slice_in_dim(m, s * n, n, axis=1)

    qkv_up = jnp.concatenate(
        [own(qkv_up[:, c * width : (c + 1) * width], mine) for c in range(3)], axis=1
    )
    dense_down = own(dense_down, mine)
    inner_up = own(inner_up, units)
    outer_down = own(outer_down, units)

    wqkv = lax.all_gather(qkv_weight, "fsdp", axis=1, tiled=True)
    wdense = lax.all_gather(dense_weight, "fsdp", axis=1, tiled=True)
    winner = lax.all_gather(inner_weight, "fsdp", axis=0, tiled=True)
    wouter = lax.all_gather(outer_weight, "fsdp", axis=1, tiled=True)

    gain = norm_gain.astype(F32)
    shift = norm_bias.astype(F32)
    source = tokens.astype(F32)
    normed_own = norm_layer(source, gain, shift).astype(BF16)
    normed = lax.all_gather(normed_own, "seq", axis=0, tiled=True)
    cot = lax.all_gather(cotangent, "seq", axis=0, tiled=True)

    coeffs = dot_nt(normed, jnp.concatenate([qkv_down, inner_down], axis=0)).astype(BF16)
    qkv_coeff, inner_coeff = coeffs[:, :RANK], coeffs[:, RANK:]
    cgs = (
        ADAPTER_SCALE * dot_nt(cot, jnp.concatenate([dense_up, outer_up], axis=0))
    ).astype(BF16)
    dense_cg, outer_cg = cgs[:, :RANK], cgs[:, RANK:]

    bias = jnp.stack([own(qkv_bias.reshape(3, width)[c : c + 1], mine)[0] for c in range(3)])
    projected = (
        jnp.concatenate([dot(normed, wqkv[c]) for c in range(3)], axis=1)
        + bias.reshape(-1).astype(F32)
        + ADAPTER_SCALE * dot(qkv_coeff, qkv_up)
    ).reshape(length, 3, heads, HD)
    cos_table, sin_table = rope_tables(length, heads)
    query = rotate(projected[:, 0], cos_table, sin_table).astype(BF16).transpose(1, 0, 2)
    key = rotate(projected[:, 1], cos_table, sin_table).astype(BF16).transpose(1, 0, 2)
    value = projected[:, 2].astype(BF16).transpose(1, 0, 2)
    attended_grad = (dot_nt(cot, wdense) + dot(dense_cg, dense_down)).astype(BF16)
    head_grad = attended_grad.reshape(length, heads, HD).transpose(1, 0, 2)

    scale = HD ** (-0.5)

    def bmm(spec, a, b):
        return jnp.einsum(spec, a, b, preferred_element_type=F32)

    key_grad = jnp.zeros((heads, length, HD), F32)
    value_grad = jnp.zeros((heads, length, HD), F32)
    attended_parts = []
    query_parts = []
    for b in range(length // BLOCK):
        lo, hi = b * BLOCK, (b + 1) * BLOCK
        q = query[:, lo:hi]
        k = key[:, :hi]
        v = value[:, :hi]
        g = head_grad[:, lo:hi]
        scores = bmm("hqd,hkd->hqk", q, k) * scale
        row_max = jnp.max(scores, axis=-1, keepdims=True)
        exponent = jnp.exp(scores - row_max)
        prob = exponent / jnp.sum(exponent, axis=-1, keepdims=True)
        prob_low = prob.astype(BF16)
        attended_parts.append(bmm("hqk,hkd->hqd", prob_low, v).astype(BF16))
        prob_grad = bmm("hqd,hkd->hqk", g, v)
        row_dot = jnp.sum(prob_grad * prob, axis=-1, keepdims=True)
        score_grad = (prob * (prob_grad - row_dot)).astype(BF16)
        query_parts.append((bmm("hqk,hkd->hqd", score_grad, k) * scale).astype(BF16))
        key_grad = key_grad.at[:, :hi].add(bmm("hqk,hqd->hkd", score_grad, q) * scale)
        value_grad = value_grad.at[:, :hi].add(bmm("hqk,hqd->hkd", prob_low, g))

    def rows_first(x):
        return x.transpose(1, 0, 2)

    attended = rows_first(jnp.concatenate(attended_parts, axis=1)).reshape(length, mine)
    query_grad = rows_first(jnp.concatenate(query_parts, axis=1)).astype(F32)
    key_back = rows_first(key_grad.astype(BF16)).astype(F32)
    value_back = rows_first(value_grad.astype(BF16)).reshape(length, mine)
    projected_grad = jnp.concatenate(
        [
            rotate(query_grad, cos_table, -sin_table).astype(BF16).reshape(length, mine),
            rotate(key_back, cos_table, -sin_table).astype(BF16).reshape(length, mine),
            value_back,
        ],
        axis=1,
    )

    pre_act = (
        dot(normed, winner)
        + own(inner_bias[None], units).astype(F32)
        + ADAPTER_SCALE * dot(inner_coeff, inner_up)
    )
    act32, gelu_back = jax.vjp(lambda v: jax.nn.gelu(v, approximate=True), pre_act)
    activated = act32.astype(BF16)
    act_grad = dot_nt(cot, wouter) + dot(outer_cg, outer_down)
    pre_grad = gelu_back(act_grad)[0].astype(BF16)

    def scatter(x):
        return lax.psum_scatter(x, "seq", scatter_dimension=0, tiled=True)

    branch = scatter((dot(attended, wdense) + dot(activated, wouter)))
    coeff_sum = scatter(
        jnp.concatenate([dot_nt(attended, dense_down), dot_nt(activated, outer_down)], axis=1)
    )
    back = dot_nt(pre_grad, winner)
    for c in range(3):
        back = back + dot_nt(projected_grad[:, c * mine : (c + 1) * mine], wqkv[c])
    back = scatter(back)
    cg_sum = scatter(
        ADAPTER_SCALE
        * jnp.concatenate([dot_nt(projected_grad, qkv_up), dot_nt(pre_grad, inner_up)], axis=1)
    )
    late_own = jnp.concatenate([coeff_sum, cg_sum], axis=1).astype(BF16)
    late = lax.all_gather(late_own, "seq", axis=0, tiled=True)

    layer_out = (
        source
        + branch
        + dense_bias.astype(F32)
        + outer_bias.astype(F32)
        + ADAPTER_SCALE
        * dot(late_own[:, : 2 * RANK], jnp.concatenate([dense_up, outer_up], axis=0))
    ).astype(BF16)
    normed_grad = back + dot(
        late_own[:, 2 * RANK :], jnp.concatenate([qkv_down, inner_down], axis=0)
    )
    row_mean = jnp.mean(source, axis=-1, keepdims=True)
    centred = source - row_mean
    inv = lax.rsqrt(jnp.mean(centred * centred, axis=-1, keepdims=True) + EPSILON)
    xhat = centred * inv
    e = normed_grad * gain
    input_grad = cotangent.astype(F32) + inv * (
        e
        - jnp.mean(e, axis=-1, keepdims=True)
        - xhat * jnp.mean(e * xhat, axis=-1, keepdims=True)
    )

    share = width // groups
    cot_mine = own(cot, share)
    normed_mine = own(normed, share)
    qkv_up_g = ADAPTER_SCALE * dot_tn(qkv_coeff, projected_grad)
    inner_up_g = ADAPTER_SCALE * dot_tn(inner_coeff, pre_grad)
    dense_down_g = dot_tn(dense_cg, attended)
    outer_down_g = dot_tn(outer_cg, activated)
    ups = ADAPTER_SCALE * dot_tn(late[:, : 2 * RANK], cot_mine)
    downs = dot_tn(late[:, 2 * RANK :], normed_mine)
    mine_grads = [
        downs[:RANK],
        qkv_up_g,
        dense_down_g,
        ups[:RANK],
        downs[RANK:],
        inner_up_g,
        outer_down_g,
        ups[RANK:],
    ]
    packed = jnp.concatenate(mine_grads, axis=1)
    sizes = [g.shape[1] for g in mine_grads]
    outs = deliver(packed, sizes, counts, pick, planes, groups)
    return (layer_out, input_grad, *outs)


def solution(mesh):
    both = P(("fsdp", "seq"), None)
    placed = (
        both,
        both,
        P(),
        P(None, "fsdp", "seq"),
        P("seq", "fsdp"),
        P("fsdp", "seq"),
        P("seq", "fsdp"),
    ) + (P(),) * 6 + (both,) * 8
    return jax.shard_map(
        on_device, mesh=mesh, in_specs=placed, out_specs=(both,) * 10, check_vma=False
    )
```

```python
import functools

import jax
import jax.numpy as jnp
import numpy as np
from jax import lax
from jax.experimental import pallas as pl
from jax.experimental.pallas import tpu as pltpu
from jax.sharding import PartitionSpec as P

H = 32
HD = 64
ROT = 32
RANK = 16
ADAPT = 8
BLOCK = 256
EPSILON = 1e-05
ADAPTER_SCALE = 2.0
ROPE_BASE = 10000.0
MASKED = -1e30
F32 = jnp.float32
BF16 = jnp.bfloat16


def dot(a, b, dims=((1,), (0,))):
    return lax.dot_general(a, b, (dims, ((), ())), preferred_element_type=F32)


def dot_nt(a, b):
    return dot(a, b, ((1,), (1,)))


def dot_tn(a, b):
    return dot(a, b, ((0,), (0,)))


def norm_layer(values, scale_gain, offset_bias):
    row_mean = jnp.mean(values, axis=-1, keepdims=True)
    centred = values - row_mean
    spread = jnp.mean(centred * centred, axis=-1, keepdims=True)
    return centred * lax.rsqrt(spread + EPSILON) * scale_gain + offset_bias


def rope_tables(length, heads):
    frequency = ROPE_BASE ** (-2.0 * jnp.arange(ROT // 2, dtype=F32) / ROT)
    angles = jnp.arange(length).astype(F32)[:, None] * frequency[None, :]
    return jnp.cos(angles)[:, None, :], jnp.sin(angles)[:, None, :]


def rotate(values, cos_table, sin_table):
    a = values[..., : ROT // 2]
    b = values[..., ROT // 2 : ROT]
    return jnp.concatenate(
        [a * cos_table - b * sin_table, b * cos_table + a * sin_table, values[..., ROT:]], axis=-1
    )


MESH = pl.DeviceIdType.MESH
TILE = 256
UNIT = 256
PART = 128
ALL = slice(None)


def rope_constants(length):
    frequency = ROPE_BASE ** (-2.0 * np.arange(ROT // 2, dtype=np.float64) / ROT)
    angles = np.arange(length, dtype=np.float64)[:, None] * frequency[None, :]
    cos = np.ones((length, HD))
    sin = np.zeros((length, HD))
    half = ROT // 2
    cos[:, :half] = np.cos(angles)
    cos[:, half:ROT] = np.cos(angles)
    sin[:, :half] = -np.sin(angles)
    sin[:, half:ROT] = np.sin(angles)
    return (
        jnp.asarray(np.tile(cos, (1, 2)), F32),
        jnp.asarray(np.tile(sin, (1, 2)), F32),
    )


def turn(x, cos, sin, sign):
    lane = lax.broadcasted_iota(jnp.int32, x.shape, 1) % HD
    partner = jnp.where(
        lane < ROT // 2,
        pltpu.roll(x, x.shape[1] - ROT // 2, 1),
        pltpu.roll(x, ROT // 2, 1),
    )
    return x * cos + partner * (sin * sign)


def turn_all(x, cos, sin, sign):
    step = cos.shape[1]
    return jnp.concatenate(
        [turn(x[:, i : i + step], cos, sin, sign) for i in range(0, x.shape[1], step)], axis=1
    )


def layer_kernel(
    planes,
    tok_ref,
    cotown_ref,
    wq_in,
    wd_in,
    wi_in,
    wo_in,
    qb_ref,
    db_ref,
    ib_ref,
    ob_ref,
    gain_ref,
    shift_ref,
    index_ref,
    map_refs,
    cos_ref,
    sin_ref,
    out_ref,
    igrad_ref,
    grad_refs,
    stack,
    sel,
    adm,
    downs_ref,
    ups_ref,
    ddown_all,
    qup_all,
    iup_ref,
    odown_ref,
    qgrad,
    a_msg,
    a_h1,
    a_h2,
    b_msg,
    b_h1,
    b_h2,
    q_h1,
    q_h2,
    normed,
    cot,
    wq,
    wd,
    wi,
    wo,
    qkv,
    hg,
    att,
    pg,
    acc_a,
    acc_b,
    pre,
    act,
    ag,
    pgrad,
    coeff,
    cgs,
    coeff_t,
    cgs_t,
    res,
    keep,
    s1_send,
    s1_recv,
    a_send,
    a_recv,
    c_send,
    c_recv,
    ar_send,
    ar_recv,
    local_sem,
    zs_sem,
    zr_sem,
    ag_ssem,
    ag_rsem,
    s1_ssem,
    s1_rsem,
    a_ssem,
    a_rsem,
    c_ssem,
    c_rsem,
    ar_ssem,
    ar_rsem,
    adz_ssem,
    adz_rsem,
    h1_ssem,
    h1_rsem,
    h2_ssem,
    h2_rsem,
    q1_ssem,
    q1_rsem,
    q2_ssem,
    q2_rsem,
):
    z = lax.axis_index("fsdp")
    s = lax.axis_index("seq")
    core = s % 2
    chip = s // 2
    to_core = (z, chip * 2 + (1 - core))
    chip_x = chip + 1 - 2 * (chip % 2)
    chip_y = (chip + 2) % 4
    chip_d = chip_x + 2 - 4 * (chip_x // 2)
    to_x = (z, chip_x * 2 + core)
    to_y = (z, chip_y * 2 + core)
    rows, width = tok_ref.shape
    length = normed.shape[0]
    units = act.shape[1]
    fan = width // planes
    mine = wq.shape[3]
    tiles = length // TILE

    def remote(src, dst, ssem, rsem, where):
        return pltpu.make_async_remote_copy(
            src_ref=src, dst_ref=dst, send_sem=ssem, recv_sem=rsem, device_id=where,
            device_id_type=MESH,
        )

    def line(ref, cols):
        return ref[cols].astype(F32)[None, :]

    def block(i, n):
        return pl.ds(pl.multiple_of(i * n, n), n)

    bar = pltpu.get_barrier_semaphore()
    for k in range(1, 8):
        pl.semaphore_signal(bar, inc=1, device_id=(z, (s + k) % 8), device_id_type=MESH)
    for k in range(1, planes):
        pl.semaphore_signal(bar, inc=1, device_id=((z + k) % planes, s), device_id_type=MESH)
    pl.semaphore_wait(bar, 7 + planes - 1)

    chunks = []
    for c in range(3):
        chunks.append((wq_in.at[c], lambda j, c=c: wq.at[j, c]))
    chunks.append((wd_in, lambda j: wd.at[j]))
    part = fan // 4
    for i in range(4):
        chunks.append(
            (
                wi_in.at[pl.ds(i * part, part), :],
                lambda j, i=i: wi.at[j, pl.ds(i * part, part), :],
            )
        )
    for i in range(fan // PART):
        chunks.append(
            (
                wo_in.at[:, pl.ds(i * PART, PART)],
                lambda j, i=i: wo.at[j, :, pl.ds(i * PART, PART)],
            )
        )
    n_chunks = len(chunks)
    ahead = 2
    last_step = n_chunks + planes - 1

    def zcopy(c, direction, k):
        src, place = chunks[c]
        j = z - k if direction == 0 else z + k
        return remote(
            src if k == 0 else place(j),
            place(j),
            zs_sem.at[c, direction, k],
            zr_sem.at[c, j],
            (z + 1, s) if direction == 0 else (z - 1, s),
        )

    def zhas(direction, k):
        if direction == 0:
            return jnp.logical_and(z - k >= 0, z + 1 < planes)
        return jnp.logical_and(z + k < planes, z - 1 >= 0)

    def zsend(c, k):
        for direction in (0, 1):

            @pl.when(zhas(direction, k))
            def _(direction=direction):
                zcopy(c, direction, k).start()

    def zarrived(c, j):
        place = chunks[c][1](j)
        pltpu.make_async_copy(place, place, zr_sem.at[c, j]).wait()

    def zrelay(c, k):
        for direction in (0, 1):

            @pl.when(zhas(direction, k))
            def _(direction=direction):
                zarrived(c, z - k if direction == 0 else z + k)
                zcopy(c, direction, k).start()

    def zfinish(first, last):
        for c in range(first, last):
            for direction in (0, 1):
                for k in range(1, planes):
                    j = z - k if direction == 0 else z + k
                    here = z == planes - 1 if direction == 0 else z == 0

                    @pl.when(here)
                    def _(c=c, j=j):
                        zarrived(c, j)

    def zstep(t):
        if t == 0:
            for c in range(min(ahead, n_chunks - 1) + 1):
                zsend(c, 0)
        elif t + ahead < n_chunks:
            zsend(t + ahead, 0)
        for k in range(1, planes - 1):
            if 0 <= t - k < n_chunks:
                zrelay(t - k, k)

    own = []
    for c in range(n_chunks):
        src, place = chunks[c]
        own.append(pltpu.make_async_copy(src, place(z), local_sem.at[c]))
    for copy in own:
        copy.start()

    zstep(0)

    half = width // 2

    def row_view(buf, b, part):
        if part is None:
            return buf.at[block(b, rows), :]
        return buf.at[block(b, rows), pl.ds(part * half, half)]

    def lead_view(buf, b, part):
        if part is None:
            return buf.at[b]
        return buf.at[b, pl.ds(part * (planes // 2), planes // 2)]

    def gather_copies(p, buf, view):
        bx = chip_x * 2 + core
        by = chip_y * 2 + core
        bd = chip_d * 2 + core
        me = view(buf, s, None)
        blk_x = view(buf, bx, None)
        blk_y = view(buf, by, None)
        blk_d = view(buf, bd, None)
        x0 = view(buf, bx, 0)
        y1 = view(buf, by, 1)
        d0 = view(buf, bd, 0)
        d1 = view(buf, bd, 1)
        ss, rs = ag_ssem.at[p], ag_rsem.at[p]

        def same(ref, i, where):
            return remote(ref, ref, ss.at[i], rs.at[i], where)

        sends = [
            same(me, 0, to_x),
            same(me, 1, to_y),
            same(me, 2, to_core),
            same(x0, 3, to_y),
            same(blk_x, 4, to_core),
            same(y1, 5, to_x),
            same(blk_y, 6, to_core),
            same(blk_d, 7, to_core),
        ]
        other = 1 - core
        into = [
            blk_x,
            blk_y,
            view(buf, chip * 2 + other, None),
            d0,
            view(buf, chip_x * 2 + other, None),
            d1,
            view(buf, chip_y * 2 + other, None),
            view(buf, chip_d * 2 + other, None),
        ]

        def arrived(i):
            pltpu.make_async_copy(into[i], into[i], rs.at[i]).wait()

        return sends, arrived

    cot[block(s, rows), :] = cotown_ref[...]
    c_sends, c_arrived = gather_copies(0, cot, row_view)
    for i in range(3):
        c_sends[i].start()

    counts = [m.shape[0] for m in map_refs]
    spans = [2 * n if n % 128 else n for n in counts]
    bases = [sum(spans[:i]) for i in range(8)]
    stack[...] = jnp.zeros_like(stack)
    odd = s % 2
    for m, n, span, base in zip(map_refs, counts, spans, bases):
        at = base + (odd * n if span != n else 0)
        stack[pl.ds(pl.multiple_of(at, 64), n), :] = m[...]
    lane = lax.broadcasted_iota(jnp.int32, (RANK, ADAPT * RANK), 1)
    column = lax.broadcasted_iota(jnp.int32, (RANK, ADAPT * RANK), 0)
    picks = []
    for g in range(planes):
        picks.append((lane == column + index_ref[g] * RANK).astype(F32))
        sel[g] = dot_nt(picks[g].astype(BF16), stack[...]).astype(BF16)

    def adapter_copy(k):
        g = (z + k) % planes
        return remote(sel.at[g], adm.at[s, z], adz_ssem.at[k - 1], adz_rsem.at[z], (g, s))

    for k in range(1, planes):
        adapter_copy(k).start()
    adm[s, z] = sel[z]

    x = tok_ref[...].astype(F32)
    mean = jnp.mean(x, axis=-1, keepdims=True)
    centred = x - mean
    inv = lax.rsqrt(jnp.mean(centred * centred, axis=-1, keepdims=True) + EPSILON)
    normed[block(s, rows), :] = (
        centred * inv * line(gain_ref, ALL) + line(shift_ref, ALL)
    ).astype(BF16)
    n_sends, n_arrived = gather_copies(1, normed, row_view)
    for i in range(3):
        n_sends[i].start()
    for k in range(1, planes):
        g = (z + k) % planes
        pltpu.make_async_copy(adm.at[s, g], adm.at[s, g], adz_rsem.at[g]).wait()
    m_sends, m_arrived = gather_copies(2, adm, lead_view)
    for i in range(3):
        m_sends[i].start()
    gathers = ((c_sends, c_arrived), (n_sends, n_arrived), (m_sends, m_arrived))
    zstep(1)
    for m, (sends, arrived) in enumerate(gathers):
        arrived(0)
        sends[3].start()
        sends[4].start()
        arrived(1)
        sends[5].start()
        sends[6].start()
        if m == 0:
            zstep(2)
        if m == 2:
            zstep(3)
    for m, (sends, arrived) in enumerate(gathers):
        arrived(3)
        arrived(5)
        sends[7].start()
        if m == 0:
            zstep(4)
    for sends, arrived in gathers:
        for i in (2, 4, 6, 7):
            arrived(i)
    zstep(5)

    def order(f, carry):
        for pair in range(4):

            def both(i):
                cols = slice(bases[i], bases[i] + spans[i])
                return adm[2 * pair, f, :, cols] + adm[2 * pair + 1, f, :, cols]

            where = block(f * 4 + pair, 128)
            downs_ref[:RANK, where] = both(0)
            downs_ref[RANK:, where] = both(4)
            ups_ref[:RANK, where] = both(3)
            ups_ref[RANK:, where] = both(7)
            ddown_all[:, where] = both(2)
            qup_all[:, block(f * 4 + pair, spans[1])] = both(1)
        return carry

    lax.fori_loop(0, planes, order, 0)
    for j in range(4):
        q = s * 4 + j
        n = counts[5]
        iup_ref[:, j * n : (j + 1) * n] = adm[q % 8, q // 8, :, bases[5] : bases[5] + n]
        odown_ref[:, j * n : (j + 1) * n] = adm[q % 8, q // 8, :, bases[6] : bases[6] + n]

    def qup(c):
        return qup_all[:, pl.ds(pl.multiple_of(c * width + s * mine, mine), mine)]

    def ddown():
        return ddown_all[:, block(s, mine)]

    def low(t, carry):
        r = block(t, TILE)
        c = dot_nt(normed[r, :], downs_ref[...])
        coeff[r, :] = c.astype(BF16)
        g = ADAPTER_SCALE * dot_nt(cot[r, :], ups_ref[...])
        cgs[r, :] = g.astype(BF16)
        return carry

    lax.fori_loop(0, tiles, low, 0)
    for copy in own:
        copy.wait()
    zstep(6)
    zfinish(0, 4)

    def project(t, carry):
        r = block(t, TILE)
        cos = cos_ref[r, :]
        sin = sin_ref[r, :]
        for c in range(3):
            v = ADAPTER_SCALE * dot(coeff[r, :RANK], qup(c))
            v = v + line(qb_ref, pl.ds(pl.multiple_of(c * width + s * mine, mine), mine))
            for j in range(planes):
                v = v + dot(normed[r, j * fan : (j + 1) * fan], wq[j, c])
            if c < 2:
                v = turn_all(v, cos, sin, 1.0)
            v = v.astype(BF16)
            if c == 0:
                v = v * jnp.asarray(HD**-0.5, BF16)
            qkv[c, r, :] = v
        g = dot(cgs[r, :RANK], ddown())
        for j in range(planes):
            g = g + dot_nt(cot[r, j * fan : (j + 1) * fan], wd[j])
        hg[r, :] = g.astype(BF16)
        return carry

    lax.fori_loop(0, tiles, project, 0)
    zstep(7)

    dk = ag.at[:, pl.ds(0, mine)]
    dv = ag.at[:, pl.ds(mine, mine)]
    ag[:, : 2 * mine] = jnp.zeros((length, 2 * mine), F32)
    heads = mine // HD

    for b in range(length // BLOCK):
        lo, hi = b * BLOCK, (b + 1) * BLOCK
        acc_a[...] = jnp.zeros_like(acc_a)
        acc_b[...] = jnp.zeros_like(acc_b)

        def one_head(h, carry, lo=lo, hi=hi):
            lane = lax.broadcasted_iota(jnp.int32, (1, mine), 1)
            mask = (lane // HD == h).astype(BF16)
            mask32 = (lane // HD == h).astype(F32)
            q = qkv[0, lo:hi, :] * mask
            g = hg[lo:hi, :] * mask
            k = qkv[1, :hi, :]
            v = qkv[2, :hi, :]
            sc = dot_nt(q, k)
            e = jnp.exp(sc - jnp.max(sc, axis=-1, keepdims=True))
            p = e * (1.0 / jnp.sum(e, axis=-1, keepdims=True))
            pb = p.astype(BF16)
            acc_a[...] += dot(pb, v) * mask32
            dp = dot_nt(g, v)
            ds = (p * (dp - jnp.sum(dp * p, axis=-1, keepdims=True))).astype(BF16)
            acc_b[...] += dot(ds, k) * mask32
            dk[:hi, :] += dot_tn(ds, q)
            dv[:hi, :] += dot_tn(pb, g)
            return carry

        lax.fori_loop(0, heads, one_head, 0)
        att[lo:hi, :] = acc_a[...].astype(BF16)
        back = (acc_b[...] * (HD**-0.5)).astype(BF16).astype(F32)
        pg[0, lo:hi, :] = turn_all(back, cos_ref[lo:hi, :], sin_ref[lo:hi, :], -1.0).astype(BF16)
        if b == 1:
            zstep(8)
        if b == 2:
            zstep(9)
        if b == 3:
            zstep(10)

    def finish(t, carry):
        r = block(t, TILE)
        back = dk[r, :].astype(BF16).astype(F32)
        pg[1, r, :] = turn_all(back, cos_ref[r, :], sin_ref[r, :], -1.0).astype(BF16)
        pg[2, r, :] = dv[r, :].astype(BF16)
        return carry

    lax.fori_loop(0, tiles, finish, 0)

    coeff_t[...] = dot_nt(downs_ref[...], normed[...]).astype(BF16)
    cgs_t[...] = (ADAPTER_SCALE * dot_nt(ups_ref[...], cot[...])).astype(BF16)

    share = width // 8

    def wait_on(ref, sem):
        pltpu.make_async_copy(ref, ref, sem).wait()

    def hop1(w, msg, h1, start):
        for j in range(4):
            to = 4 * (s % 2) + j
            there = (z, to)

            @pl.when(to != s)
            def _(j=j, there=there):
                copy = remote(
                    msg.at[j], h1.at[s // 2], h1_ssem.at[w, j], h1_rsem.at[w, s // 2], there
                )
                if start:
                    copy.start()
                else:
                    copy.wait_send()

            if start:

                @pl.when(to == s)
                def _(j=j):
                    pltpu.make_async_copy(
                        msg.at[j], h1.at[s // 2], h1_rsem.at[w, s // 2]
                    ).start()

    def hop2_copy(w, h1, h2, k):
        g = (z + k) % planes
        return remote(h1.at[g], h2.at[z], h2_ssem.at[w, k - 1], h2_rsem.at[w, z], (g, s))

    def hop2(w, h1, h2):
        for g in range(planes):
            wait_on(h1.at[g], h1_rsem.at[w, g])
        for k in range(1, planes):
            hop2_copy(w, h1, h2, k).start()
        h2[z] = h1[z]

    def landed(w, h1, h2):
        for k in range(1, planes):
            g = (z + k) % planes
            wait_on(h2.at[g], h2_rsem.at[w, g])
        for k in range(1, planes):
            hop2_copy(w, h1, h2, k).wait_send()

    def place(parts, i, rows_of):
        full = None
        for g in range(planes):
            v = lax.dot_general(
                parts[g], picks[g], (((0,), (0,)), ((), ())),
                precision=lax.Precision.HIGHEST, preferred_element_type=F32,
            )
            full = v if full is None else full + v
        grad_refs[i][...] = rows_of(full)

    def half_rows(v):
        return jnp.where(s % 2 == 0, v[:64], v[64:])

    def all_rows(v):
        return v

    for c in range(3):
        g = ADAPTER_SCALE * dot(coeff_t[:RANK, :], pg[c])
        for i in range(2):
            qgrad[2 * c + i] = g[:, i * 128 : (i + 1) * 128]

    def qkv_hop1(start):
        for c in range(3):
            for i in range(2):
                t = 16 * c + 2 * s + i
                for o in range(2):
                    owner = 2 * (t // 3) + o
                    slot = t % 3 - o
                    ok = jnp.logical_and(slot >= 0, slot <= 1)
                    to = owner % 8
                    src = qgrad.at[2 * c + i]
                    n = 4 * c + 2 * i + o

                    @pl.when(jnp.logical_and(ok, to != s))
                    def _(src=src, owner=owner, slot=slot, to=to, n=n):
                        copy = remote(
                            src, q_h1.at[owner // 8, slot], q1_ssem.at[n],
                            q1_rsem.at[owner // 8, slot], (z, to),
                        )
                        if start:
                            copy.start()
                        else:
                            copy.wait_send()

                    if start:

                        @pl.when(jnp.logical_and(ok, to == s))
                        def _(src=src, owner=owner, slot=slot):
                            pltpu.make_async_copy(
                                src, q_h1.at[owner // 8, slot], q1_rsem.at[owner // 8, slot]
                            ).start()

    def qkv_hop2_copy(k):
        g = (z + k) % planes
        return remote(q_h1.at[g], q_h2.at[z], q2_ssem.at[k - 1], q2_rsem.at[z], (g, s))

    def qkv_hop2():
        for g in range(planes):
            for slot in range(2):
                wait_on(q_h1.at[g, slot], q1_rsem.at[g, slot])
        for k in range(1, planes):
            qkv_hop2_copy(k).start()
        q_h2[z] = q_h1[z]

    def qkv_landed():
        for k in range(1, planes):
            g = (z + k) % planes
            wait_on(q_h2.at[g], q2_rsem.at[g])
        for k in range(1, planes):
            qkv_hop2_copy(k).wait_send()

    qkv_hop1(True)
    g = dot(cgs_t[:RANK, :], att[...])
    for j in range(4):
        a_msg[j, :, 256:384] = g[:, (j // 2) * 128 : (j // 2 + 1) * 128]
    pass
    zfinish(4, 8)
    zstep(11)

    k0 = 0.7978845608028654
    k1 = 0.044715

    def inner(t, carry):
        r = block(t, TILE)
        v = ADAPTER_SCALE * dot(coeff[r, RANK : 2 * RANK], iup_ref[...])
        v = v + line(ib_ref, block(s, units))
        for j in range(planes):
            v = v + dot(normed[r, j * fan : (j + 1) * fan], wi[j])
        sq = v * v
        th = jnp.tanh(k0 * v * (1.0 + k1 * sq))
        act[r, :] = (0.5 * v * (1.0 + th)).astype(BF16)
        pre[r, :] = 0.5 * (1.0 + th) + 0.5 * v * (1.0 - th * th) * (k0 * (1.0 + 3.0 * k1 * sq))
        return carry

    lax.fori_loop(0, tiles, inner, 0)
    g = dot(cgs_t[RANK : 2 * RANK, :], act[...])
    for j in range(4):
        a_msg[j, :, :256] = g[:, j * 256 : (j + 1) * 256]
    qkv_hop2()
    zstep(12)

    partners = (to_core, to_x, to_y)

    def reduce_copy(w, i):
        return remote(
            ar_send.at[w], ar_recv.at[w, i], ar_ssem.at[w, i], ar_rsem.at[w, i], partners[i]
        )

    def reduce_round(w, i):
        if i > 0:
            reduce_copy(w, i - 1).wait()
            ar_send[w] += ar_recv[w, i - 1]
        if i < 3:
            reduce_copy(w, i).start()

    ar_send[0, :RANK, :] = dot_nt(ddown(), att[...])
    ar_send[0, RANK : 2 * RANK, :] = dot_nt(odown_ref[...], act[...])
    for i in range(4):
        reduce_round(0, i)
        pass
    coeff_dense = ar_send[0].astype(BF16)
    for i in range(2):
        g = ADAPTER_SCALE * dot(
            coeff_dense[i * RANK : (i + 1) * RANK, :], cot[:, block(s, share)]
        )
        for j in range(4):
            at = 384 + i * 128
            a_msg[j, :, at : at + 128] = g[:, (j // 2) * 128 : (j // 2 + 1) * 128]
    hop1(0, a_msg, a_h1, True)

    p_units = width // UNIT
    per = fan // UNIT
    early = p_units - planes // 2
    total = 2 * p_units

    def branch_place(n):
        return (n % (planes // 2)) * 2, n // (planes // 2)

    def back_place(n):
        return (n - p_units) // per, (n - p_units) % per

    def keep_split(n, k, r):
        slot = n % 2
        a = r[:rows, :]
        b = r[rows:, :]
        first = core == 0
        keep[n % 6, k] = jnp.where(first, a, b)
        s1_send[slot, k] = jnp.where(first, b, a).astype(BF16)

    def s1_copy(n):
        return remote(s1_send.at[n % 2], s1_recv.at[n], s1_ssem.at[n % 2], s1_rsem.at[n], to_core)

    def a_copy(n, i):
        return remote(
            a_send.at[n % 3, i], a_recv.at[n, i], a_ssem.at[n % 3, i], a_rsem.at[n, i],
            (to_x, to_y)[i],
        )

    def c_copy(n, i):
        return remote(
            c_send.at[n % 3, i], c_recv.at[n, i], c_ssem.at[n % 3, i], c_rsem.at[n, i],
            (to_x, to_y)[i],
        )

    hu = UNIT // 2

    def stage0_branch(n):
        j, i = branch_place(n)

        def tile(k, carry):
            r = block(k, TILE)
            cols = block(i, PART)
            w_o = jnp.concatenate([wo[j, :, cols], wo[j + 1, :, cols]], axis=1)
            w_d = jnp.concatenate([wd[j, :, cols], wd[j + 1, :, cols]], axis=1)
            keep_split(n, k, dot(act[r, :], w_o) + dot(att[r, :], w_d))
            return carry

        lax.fori_loop(0, tiles, tile, 0)
        s1_copy(n).start()

    def stage0_back(n):
        j, i = back_place(n)

        def tile(k, carry):
            r = block(k, TILE)
            rws = block(i, UNIT)
            v = dot_nt(pgrad[r, :], wi[j, rws, :])
            for c in range(3):
                v = v + dot_nt(pg[c, r, :], wq[j, c, rws, :])
            keep_split(n, k, v)
            return carry

        lax.fori_loop(0, tiles, tile, 0)
        s1_copy(n).start()

    def stage1(n):
        s1_copy(n).wait()
        q = n % 6
        for k in range(4):
            keep[q, k] += s1_recv[n, k].astype(F32)
        far = keep[q, chip_d]
        a_send[n % 3, 0] = far[:, :hu].astype(BF16)
        a_send[n % 3, 1] = far[:, hu:].astype(BF16)
        for i in range(2):
            a_copy(n, i).start()

    def stage2(n):
        q = n % 6
        for i in range(2):
            a_copy(n, i).wait()
        keep[q, chip_y, :, :hu] += a_recv[n, 0].astype(F32)
        keep[q, chip_x, :, hu:] += a_recv[n, 1].astype(F32)
        c_send[n % 3, 0] = keep[q, chip_x].astype(BF16)
        c_send[n % 3, 1] = keep[q, chip_y].astype(BF16)
        for i in range(2):
            c_copy(n, i).start()

    def stage3(n):
        q = n % 6
        for i in range(2):
            c_copy(n, i).wait()
        v = keep[q, chip] + c_recv[n, 0].astype(F32) + c_recv[n, 1].astype(F32)

        @pl.when(n < p_units)
        def _():
            j, i = branch_place(n)
            for m in range(2):
                res[:, pl.ds(pl.multiple_of((j + m) * fan + i * PART, PART), PART)] = v[
                    :, m * PART : (m + 1) * PART
                ]

        @pl.when(n >= p_units)
        def _():
            igrad_ref[:, block(n - p_units, UNIT)] = v

    def pipeline(first, lo, hi, stage0, extra=None):
        def body(n, carry):
            if stage0 is not None:
                stage0(n)
            for back, stage in ((1, stage1), (3, stage2), (5, stage3)):
                m = n - back
                ok = m >= first
                if stage0 is None:
                    ok = jnp.logical_and(ok, m < hi - 5)

                @pl.when(ok)
                def _(m=m, stage=stage):
                    stage(m)

            if extra is not None:
                extra(n)
            return carry

        lax.fori_loop(lo, hi, body, 0)

    zstep(13)
    zfinish(8, 10)
    pass
    per_part = planes // 2
    pipeline(0, 0, 2 * per_part, stage0_branch)

    def act_part(r, i):
        cols = [slice(j * fan + i * PART, j * fan + (i + 1) * PART) for j in range(planes)]
        g = jnp.concatenate([cot[r, c] for c in cols], axis=1)
        w = [wo[j, :, i * PART : (i + 1) * PART] for j in range(planes)]
        return dot_nt(g, jnp.concatenate(w, axis=1))

    def act_back(t, carry):
        r = block(t, TILE)
        v = dot(cgs[r, RANK : 2 * RANK], odown_ref[...])
        for i in range(2):
            v = v + act_part(r, i)
        ag[r, :] = v
        return carry

    hop2(0, a_h1, a_h2)
    lax.fori_loop(0, tiles, act_back, 0)
    qkv_landed()
    landed(0, a_h1, a_h2)
    place([a_h2[g, :, :256] for g in range(planes)], 6, all_rows)
    place([a_h2[g, :, 256:384] for g in range(planes)], 2, half_rows)
    place([a_h2[g, :, 384:512] for g in range(planes)], 3, half_rows)
    place([a_h2[g, :, 512:640] for g in range(planes)], 7, half_rows)

    def qkv_rows(v):
        return jnp.where(s % 2 == 0, v[:192], v[64:])

    place(
        [jnp.concatenate([q_h2[g, 0], q_h2[g, 1]], axis=1) for g in range(planes)], 1, qkv_rows
    )
    pass
    zfinish(10, 11)
    pipeline(0, 2 * per_part, early, stage0_branch)

    def act_more(t, carry):
        r = block(t, TILE)
        ag[r, :] += act_part(r, 2)
        return carry

    lax.fori_loop(0, tiles, act_more, 0)
    zfinish(11, 12)

    pipeline(0, early, p_units, stage0_branch)

    def act_last(t, carry):
        r = block(t, TILE)
        v = ag[r, :] + act_part(r, fan // PART - 1)
        pgrad[r, :] = (v * pre[r, :]).astype(BF16)
        return carry

    lax.fori_loop(0, tiles, act_last, 0)

    up_part = dot_nt(iup_ref[...], pgrad[...])
    q_part = dot_nt(qup(0), pg[0])
    for c in range(1, 3):
        q_part = q_part + dot_nt(qup(c), pg[c])
    ar_send[1, :RANK, :] = ADAPTER_SCALE * q_part
    ar_send[1, RANK : 2 * RANK, :] = ADAPTER_SCALE * up_part
    reduce_round(1, 0)

    def rounds(n):
        for i in range(1, 4):

            @pl.when(n == p_units + 2 * i - 1)
            def _(i=i):
                reduce_round(1, i)
                if i == 2:
                    g = ADAPTER_SCALE * dot(coeff_t[RANK : 2 * RANK, :], pgrad[...])
                    for j in range(4):
                        b_msg[j, :, :256] = g[:, j * 256 : (j + 1) * 256]
                if i == 3:
                    g = dot(ar_send[1].astype(BF16), normed[:, block(s, share)])
                    for m in range(2):
                        for j in range(4):
                            b_msg[j, :, 256 + m * 128 : 384 + m * 128] = g[
                                m * RANK : (m + 1) * RANK, (j // 2) * 128 : (j // 2 + 1) * 128
                            ]
                    hop1(1, b_msg, b_h1, True)

    pipeline(0, p_units, total, stage0_back, rounds)
    hop2(1, b_h1, b_h2)
    pipeline(0, total, total + 5, None)

    first_t = ar_send[0, :, block(s, rows)].astype(BF16)
    late_t = ar_send[1, :, block(s, rows)].astype(BF16)
    out = tok_ref[...].astype(F32) + res[...] + ADAPTER_SCALE * dot_tn(first_t, ups_ref[...])
    out_ref[...] = (out + line(db_ref, ALL) + line(ob_ref, ALL)).astype(BF16)
    x = tok_ref[...].astype(F32)
    mean = jnp.mean(x, axis=-1, keepdims=True)
    centred = x - mean
    inv = lax.rsqrt(jnp.mean(centred * centred, axis=-1, keepdims=True) + EPSILON)
    xhat = centred * inv
    e = (igrad_ref[...] + dot_tn(late_t, downs_ref[...])) * line(gain_ref, ALL)
    igrad_ref[...] = cotown_ref[...].astype(F32) + inv * (
        e
        - jnp.mean(e, axis=-1, keepdims=True)
        - xhat * jnp.mean(e * xhat, axis=-1, keepdims=True)
    )

    landed(1, b_h1, b_h2)
    place([b_h2[g, :, :256] for g in range(planes)], 5, all_rows)
    place([b_h2[g, :, 256:384] for g in range(planes)], 0, half_rows)
    place([b_h2[g, :, 384:512] for g in range(planes)], 4, half_rows)

    hop1(0, a_msg, a_h1, False)
    hop1(1, b_msg, b_h1, False)
    qkv_hop1(False)
    for k in range(1, planes):
        adapter_copy(k).wait_send()
    for sends, _ in gathers:
        for copy in sends:
            copy.wait_send()
    for c in range(n_chunks):
        for k in range(planes - 1):
            for direction in (0, 1):

                @pl.when(zhas(direction, k))
                def _(c=c, k=k, direction=direction):
                    zcopy(c, direction, k).wait_send()


def run_layer(planes, args, shapes):
    rows, width, length, units, mine = shapes
    fan = width // planes
    vm = pl.BlockSpec(memory_space=pltpu.VMEM)
    hbm = pl.BlockSpec(memory_space=pl.ANY)
    n_chunks = 8 + fan // PART
    total = 2 * width // UNIT
    dma = pltpu.SemaphoreType.DMA
    maps = args[13:21]
    lanes = sum(2 * m.shape[0] if m.shape[0] % 128 else m.shape[0] for m in maps)

    def entry(*refs):
        layer_kernel(planes, *refs[:13], refs[13:21], *refs[21:25], refs[25:33], *refs[33:])

    return pl.pallas_call(
        entry,
        out_shape=(
            jax.ShapeDtypeStruct((rows, width), BF16),
            jax.ShapeDtypeStruct((rows, width), F32),
            *(jax.ShapeDtypeStruct(m.shape, F32) for m in maps),
        ),
        in_specs=[vm, vm, hbm, hbm, hbm, hbm]
        + [vm] * 6
        + [pl.BlockSpec(memory_space=pltpu.SMEM)]
        + [vm] * 10,
        out_specs=(vm,) * 10,
        scratch_shapes=[
            pltpu.VMEM((lanes, ADAPT * RANK), BF16),
            pltpu.VMEM((planes, RANK, lanes), BF16),
            pltpu.VMEM((8, planes, RANK, lanes), BF16),
            pltpu.VMEM((2 * RANK, width), BF16),
            pltpu.VMEM((2 * RANK, width), BF16),
            pltpu.VMEM((RANK, width), BF16),
            pltpu.VMEM((RANK, 3 * width), BF16),
            pltpu.VMEM((RANK, units), BF16),
            pltpu.VMEM((RANK, units), BF16),
            pltpu.VMEM((6, RANK, 128), F32),
            pltpu.VMEM((4, RANK, 640), F32),
            pltpu.VMEM((planes, RANK, 640), F32),
            pltpu.VMEM((planes, RANK, 640), F32),
            pltpu.VMEM((4, RANK, 512), F32),
            pltpu.VMEM((planes, RANK, 512), F32),
            pltpu.VMEM((planes, RANK, 512), F32),
            pltpu.VMEM((planes, 2, RANK, 128), F32),
            pltpu.VMEM((planes, 2, RANK, 128), F32),
            pltpu.VMEM((length, width), BF16),
            pltpu.VMEM((length, width), BF16),
            pltpu.VMEM((planes, 3, fan, mine), BF16),
            pltpu.VMEM((planes, mine, fan), BF16),
            pltpu.VMEM((planes, fan, units), BF16),
            pltpu.VMEM((planes, units, fan), BF16),
            pltpu.VMEM((3, length, mine), BF16),
            pltpu.VMEM((length, mine), BF16),
            pltpu.VMEM((length, mine), BF16),
            pltpu.VMEM((3, length, mine), BF16),
            pltpu.VMEM((BLOCK, mine), F32),
            pltpu.VMEM((BLOCK, mine), F32),
            pltpu.VMEM((length, units), F32),
            pltpu.VMEM((length, units), BF16),
            pltpu.VMEM((length, units), F32),
            pltpu.VMEM((length, units), BF16),
            pltpu.VMEM((length, 2 * RANK), BF16),
            pltpu.VMEM((length, 2 * RANK), BF16),
            pltpu.VMEM((2 * RANK, length), BF16),
            pltpu.VMEM((2 * RANK, length), BF16),
            pltpu.VMEM((rows, width), F32),
            pltpu.VMEM((6, 4, rows, UNIT), F32),
            pltpu.VMEM((2, 4, rows, UNIT), BF16),
            pltpu.VMEM((total, 4, rows, UNIT), BF16),
            pltpu.VMEM((3, 2, rows, UNIT // 2), BF16),
            pltpu.VMEM((total, 2, rows, UNIT // 2), BF16),
            pltpu.VMEM((3, 2, rows, UNIT), BF16),
            pltpu.VMEM((total, 2, rows, UNIT), BF16),
            pltpu.VMEM((2, 2 * RANK, length), F32),
            pltpu.VMEM((2, 3, 2 * RANK, length), F32),
            dma((n_chunks,)),
            dma((n_chunks, 2, planes)),
            dma((n_chunks, planes)),
            dma((3, 8)),
            dma((3, 8)),
            dma((2,)),
            dma((total,)),
            dma((3, 2)),
            dma((total, 2)),
            dma((3, 2)),
            dma((total, 2)),
            dma((2, 3)),
            dma((2, 3)),
            dma((planes,)),
            dma((planes,)),
            dma((2, 4)),
            dma((2, planes)),
            dma((2, planes)),
            dma((2, planes)),
            dma((12,)),
            dma((planes, 2)),
            dma((planes,)),
            dma((planes,)),
        ],
        compiler_params=pltpu.CompilerParams(
            collective_id=0, has_side_effects=True, vmem_limit_bytes=63 * 1024 * 1024
        ),
    )(*args)


def fits(planes, groups, shapes):
    rows, width, length, units, mine = shapes
    return (
        groups == 8
        and planes == 4
        and rows * 2 == TILE
        and length <= 1024
        and width == 2048
        and mine == 256
        and units == 1024
    )


def deliver(packed, sizes, counts, pick, planes, groups):
    s = lax.axis_index("seq")
    everyone = lax.all_gather(packed, "seq", axis=0, tiled=False)
    owned = []
    at = 0
    for i, (n, w) in enumerate(zip(counts, sizes)):
        part = everyone[:, :, at : at + w]
        at += w
        blocks = 3 if i == 1 else 1
        part = part.reshape(groups, RANK, blocks, w // blocks).transpose(1, 2, 0, 3)
        part = part.reshape(RANK, planes, groups, n)
        owned.append(lax.dynamic_index_in_dim(part, s, 2, keepdims=False))
    owned = jnp.concatenate(owned, axis=2).transpose(1, 0, 2)
    arrived = lax.all_to_all(owned, "fsdp", split_axis=0, concat_axis=0, tiled=True)
    place = pick.astype(F32).reshape(planes * RANK, ADAPT * RANK)
    spread = lax.dot_general(
        arrived.reshape(planes * RANK, -1),
        place,
        (((0,), (0,)), ((), ())),
        precision=lax.Precision.HIGHEST,
        preferred_element_type=F32,
    )
    outs = []
    at = 0
    for n in counts:
        outs.append(spread[at : at + n])
        at += n
    return outs


def on_device(
    tokens,
    cotangent,
    adapter_index,
    qkv_weight,
    dense_weight,
    inner_weight,
    outer_weight,
    qkv_bias,
    dense_bias,
    inner_bias,
    outer_bias,
    norm_gain,
    norm_bias,
    *maps,
):
    planes = lax.axis_size("fsdp")
    groups = lax.axis_size("seq")
    rows, width = tokens.shape
    length = rows * groups
    heads = H // groups
    mine = heads * HD
    units = inner_weight.shape[1]
    s = lax.axis_index("seq")

    shapes = (rows, width, length, units, mine)
    if fits(planes, groups, shapes):
        return run_layer(
            planes,
            (
                tokens,
                cotangent,
                qkv_weight,
                dense_weight,
                inner_weight,
                outer_weight,
                qkv_bias,
                dense_bias,
                inner_bias,
                outer_bias,
                norm_gain,
                norm_bias,
                adapter_index,
                *maps,
                *rope_constants(length),
            ),
            shapes,
        )

    counts = [m.shape[0] for m in maps]
    stacked = jnp.concatenate(maps, axis=0)
    wanted = (adapter_index[:, None] * RANK + jnp.arange(RANK)[None, :]).reshape(-1)
    pick = (wanted[:, None] == jnp.arange(ADAPT * RANK)[None, :]).astype(BF16)
    chosen = dot_nt(pick, stacked).astype(BF16).reshape(planes, RANK, -1)
    chosen = lax.all_to_all(chosen, "fsdp", split_axis=0, concat_axis=0, tiled=True)
    chosen = lax.all_gather(chosen, "seq", axis=1, tiled=False)
    full = []
    at = 0
    for n in counts:
        part = chosen[:, :, :, at : at + n]
        full.append(part.transpose(2, 0, 1, 3).reshape(RANK, -1))
        at += n
    qkv_down, qkv_up, dense_down, dense_up, inner_down, inner_up, outer_down, outer_up = full

    def own(m, n):
        return lax.dynamic_slice_in_dim(m, s * n, n, axis=1)

    qkv_up = jnp.concatenate(
        [own(qkv_up[:, c * width : (c + 1) * width], mine) for c in range(3)], axis=1
    )
    dense_down = own(dense_down, mine)
    inner_up = own(inner_up, units)
    outer_down = own(outer_down, units)

    wqkv = lax.all_gather(qkv_weight, "fsdp", axis=1, tiled=True)
    wdense = lax.all_gather(dense_weight, "fsdp", axis=1, tiled=True)
    winner = lax.all_gather(inner_weight, "fsdp", axis=0, tiled=True)
    wouter = lax.all_gather(outer_weight, "fsdp", axis=1, tiled=True)

    gain = norm_gain.astype(F32)
    shift = norm_bias.astype(F32)
    source = tokens.astype(F32)
    normed_own = norm_layer(source, gain, shift).astype(BF16)
    normed = lax.all_gather(normed_own, "seq", axis=0, tiled=True)
    cot = lax.all_gather(cotangent, "seq", axis=0, tiled=True)

    coeffs = dot_nt(normed, jnp.concatenate([qkv_down, inner_down], axis=0)).astype(BF16)
    qkv_coeff, inner_coeff = coeffs[:, :RANK], coeffs[:, RANK:]
    cgs = (
        ADAPTER_SCALE * dot_nt(cot, jnp.concatenate([dense_up, outer_up], axis=0))
    ).astype(BF16)
    dense_cg, outer_cg = cgs[:, :RANK], cgs[:, RANK:]

    bias = jnp.stack([own(qkv_bias.reshape(3, width)[c : c + 1], mine)[0] for c in range(3)])
    projected = (
        jnp.concatenate([dot(normed, wqkv[c]) for c in range(3)], axis=1)
        + bias.reshape(-1).astype(F32)
        + ADAPTER_SCALE * dot(qkv_coeff, qkv_up)
    ).reshape(length, 3, heads, HD)
    cos_table, sin_table = rope_tables(length, heads)
    query = rotate(projected[:, 0], cos_table, sin_table).astype(BF16).transpose(1, 0, 2)
    key = rotate(projected[:, 1], cos_table, sin_table).astype(BF16).transpose(1, 0, 2)
    value = projected[:, 2].astype(BF16).transpose(1, 0, 2)
    attended_grad = (dot_nt(cot, wdense) + dot(dense_cg, dense_down)).astype(BF16)
    head_grad = attended_grad.reshape(length, heads, HD).transpose(1, 0, 2)

    scale = HD ** (-0.5)

    def bmm(spec, a, b):
        return jnp.einsum(spec, a, b, preferred_element_type=F32)

    key_grad = jnp.zeros((heads, length, HD), F32)
    value_grad = jnp.zeros((heads, length, HD), F32)
    attended_parts = []
    query_parts = []
    for b in range(length // BLOCK):
        lo, hi = b * BLOCK, (b + 1) * BLOCK
        q = query[:, lo:hi]
        k = key[:, :hi]
        v = value[:, :hi]
        g = head_grad[:, lo:hi]
        scores = bmm("hqd,hkd->hqk", q, k) * scale
        row_max = jnp.max(scores, axis=-1, keepdims=True)
        exponent = jnp.exp(scores - row_max)
        prob = exponent / jnp.sum(exponent, axis=-1, keepdims=True)
        prob_low = prob.astype(BF16)
        attended_parts.append(bmm("hqk,hkd->hqd", prob_low, v).astype(BF16))
        prob_grad = bmm("hqd,hkd->hqk", g, v)
        row_dot = jnp.sum(prob_grad * prob, axis=-1, keepdims=True)
        score_grad = (prob * (prob_grad - row_dot)).astype(BF16)
        query_parts.append((bmm("hqk,hkd->hqd", score_grad, k) * scale).astype(BF16))
        key_grad = key_grad.at[:, :hi].add(bmm("hqk,hqd->hkd", score_grad, q) * scale)
        value_grad = value_grad.at[:, :hi].add(bmm("hqk,hqd->hkd", prob_low, g))

    def rows_first(x):
        return x.transpose(1, 0, 2)

    attended = rows_first(jnp.concatenate(attended_parts, axis=1)).reshape(length, mine)
    query_grad = rows_first(jnp.concatenate(query_parts, axis=1)).astype(F32)
    key_back = rows_first(key_grad.astype(BF16)).astype(F32)
    value_back = rows_first(value_grad.astype(BF16)).reshape(length, mine)
    projected_grad = jnp.concatenate(
        [
            rotate(query_grad, cos_table, -sin_table).astype(BF16).reshape(length, mine),
            rotate(key_back, cos_table, -sin_table).astype(BF16).reshape(length, mine),
            value_back,
        ],
        axis=1,
    )

    pre_act = (
        dot(normed, winner)
        + own(inner_bias[None], units).astype(F32)
        + ADAPTER_SCALE * dot(inner_coeff, inner_up)
    )
    act32, gelu_back = jax.vjp(lambda v: jax.nn.gelu(v, approximate=True), pre_act)
    activated = act32.astype(BF16)
    act_grad = dot_nt(cot, wouter) + dot(outer_cg, outer_down)
    pre_grad = gelu_back(act_grad)[0].astype(BF16)

    def scatter(x):
        return lax.psum_scatter(x, "seq", scatter_dimension=0, tiled=True)

    branch = scatter((dot(attended, wdense) + dot(activated, wouter)))
    coeff_sum = scatter(
        jnp.concatenate([dot_nt(attended, dense_down), dot_nt(activated, outer_down)], axis=1)
    )
    back = dot_nt(pre_grad, winner)
    for c in range(3):
        back = back + dot_nt(projected_grad[:, c * mine : (c + 1) * mine], wqkv[c])
    back = scatter(back)
    cg_sum = scatter(
        ADAPTER_SCALE
        * jnp.concatenate([dot_nt(projected_grad, qkv_up), dot_nt(pre_grad, inner_up)], axis=1)
    )
    late_own = jnp.concatenate([coeff_sum, cg_sum], axis=1).astype(BF16)
    late = lax.all_gather(late_own, "seq", axis=0, tiled=True)

    layer_out = (
        source
        + branch
        + dense_bias.astype(F32)
        + outer_bias.astype(F32)
        + ADAPTER_SCALE
        * dot(late_own[:, : 2 * RANK], jnp.concatenate([dense_up, outer_up], axis=0))
    ).astype(BF16)
    normed_grad = back + dot(
        late_own[:, 2 * RANK :], jnp.concatenate([qkv_down, inner_down], axis=0)
    )
    row_mean = jnp.mean(source, axis=-1, keepdims=True)
    centred = source - row_mean
    inv = lax.rsqrt(jnp.mean(centred * centred, axis=-1, keepdims=True) + EPSILON)
    xhat = centred * inv
    e = normed_grad * gain
    input_grad = cotangent.astype(F32) + inv * (
        e
        - jnp.mean(e, axis=-1, keepdims=True)
        - xhat * jnp.mean(e * xhat, axis=-1, keepdims=True)
    )

    share = width // groups
    cot_mine = own(cot, share)
    normed_mine = own(normed, share)
    qkv_up_g = ADAPTER_SCALE * dot_tn(qkv_coeff, projected_grad)
    inner_up_g = ADAPTER_SCALE * dot_tn(inner_coeff, pre_grad)
    dense_down_g = dot_tn(dense_cg, attended)
    outer_down_g = dot_tn(outer_cg, activated)
    ups = ADAPTER_SCALE * dot_tn(late[:, : 2 * RANK], cot_mine)
    downs = dot_tn(late[:, 2 * RANK :], normed_mine)
    mine_grads = [
        downs[:RANK],
        qkv_up_g,
        dense_down_g,
        ups[:RANK],
        downs[RANK:],
        inner_up_g,
        outer_down_g,
        ups[RANK:],
    ]
    packed = jnp.concatenate(mine_grads, axis=1)
    sizes = [g.shape[1] for g in mine_grads]
    outs = deliver(packed, sizes, counts, pick, planes, groups)
    return (layer_out, input_grad, *outs)


def solution(mesh):
    both = P(("fsdp", "seq"), None)
    placed = (
        both,
        both,
        P(),
        P(None, "fsdp", "seq"),
        P("seq", "fsdp"),
        P("fsdp", "seq"),
        P("seq", "fsdp"),
    ) + (P(),) * 6 + (both,) * 8
    return jax.shard_map(
        on_device, mesh=mesh, in_specs=placed, out_specs=(both,) * 10, check_vma=False
    )
```

```python
import functools

import jax
import jax.numpy as jnp
import numpy as np
from jax import lax
from jax.experimental import pallas as pl
from jax.experimental.pallas import tpu as pltpu
from jax.sharding import PartitionSpec as P

H = 32
HD = 64
ROT = 32
RANK = 16
ADAPT = 8
BLOCK = 256
EPSILON = 1e-05
ADAPTER_SCALE = 2.0
ROPE_BASE = 10000.0
MASKED = -1e30
F32 = jnp.float32
BF16 = jnp.bfloat16


def dot(a, b, dims=((1,), (0,))):
    return lax.dot_general(a, b, (dims, ((), ())), preferred_element_type=F32)


def dot_nt(a, b):
    return dot(a, b, ((1,), (1,)))


def dot_tn(a, b):
    return dot(a, b, ((0,), (0,)))


def norm_layer(values, scale_gain, offset_bias):
    row_mean = jnp.mean(values, axis=-1, keepdims=True)
    centred = values - row_mean
    spread = jnp.mean(centred * centred, axis=-1, keepdims=True)
    return centred * lax.rsqrt(spread + EPSILON) * scale_gain + offset_bias


def rope_tables(length, heads):
    frequency = ROPE_BASE ** (-2.0 * jnp.arange(ROT // 2, dtype=F32) / ROT)
    angles = jnp.arange(length).astype(F32)[:, None] * frequency[None, :]
    return jnp.cos(angles)[:, None, :], jnp.sin(angles)[:, None, :]


def rotate(values, cos_table, sin_table):
    a = values[..., : ROT // 2]
    b = values[..., ROT // 2 : ROT]
    return jnp.concatenate(
        [a * cos_table - b * sin_table, b * cos_table + a * sin_table, values[..., ROT:]], axis=-1
    )


MESH = pl.DeviceIdType.MESH
TILE = 256
UNIT = 256
PART = 128
ALL = slice(None)


def rope_constants(length):
    frequency = ROPE_BASE ** (-2.0 * np.arange(ROT // 2, dtype=np.float64) / ROT)
    angles = np.arange(length, dtype=np.float64)[:, None] * frequency[None, :]
    cos = np.ones((length, HD))
    sin = np.zeros((length, HD))
    half = ROT // 2
    cos[:, :half] = np.cos(angles)
    cos[:, half:ROT] = np.cos(angles)
    sin[:, :half] = -np.sin(angles)
    sin[:, half:ROT] = np.sin(angles)
    return (
        jnp.asarray(np.tile(cos, (1, 2)), F32),
        jnp.asarray(np.tile(sin, (1, 2)), F32),
    )


def turn(x, cos, sin, sign):
    lane = lax.broadcasted_iota(jnp.int32, x.shape, 1) % HD
    partner = jnp.where(
        lane < ROT // 2,
        pltpu.roll(x, x.shape[1] - ROT // 2, 1),
        pltpu.roll(x, ROT // 2, 1),
    )
    return x * cos + partner * (sin * sign)


def turn_all(x, cos, sin, sign):
    step = cos.shape[1]
    return jnp.concatenate(
        [turn(x[:, i : i + step], cos, sin, sign) for i in range(0, x.shape[1], step)], axis=1
    )


def layer_kernel(
    planes,
    tok_ref,
    cotown_ref,
    wq_in,
    wd_in,
    wi_in,
    wo_in,
    qb_ref,
    db_ref,
    ib_ref,
    ob_ref,
    gain_ref,
    shift_ref,
    index_ref,
    map_refs,
    cos_ref,
    sin_ref,
    out_ref,
    igrad_ref,
    grad_refs,
    stack,
    sel,
    adm,
    downs_ref,
    ups_ref,
    ddown_all,
    qup_all,
    iup_ref,
    odown_ref,
    qgrad,
    a_msg,
    a_h1,
    a_h2,
    b_msg,
    b_h1,
    b_h2,
    q_h1,
    q_h2,
    normed,
    cot,
    wq,
    wd,
    wi,
    wo,
    qkv,
    hg,
    att,
    pg,
    acc_a,
    acc_b,
    pre,
    act,
    ag,
    pgrad,
    coeff,
    cgs,
    coeff_t,
    cgs_t,
    res,
    keep,
    s1_send,
    s1_recv,
    a_send,
    a_recv,
    c_send,
    c_recv,
    ar_send,
    ar_recv,
    ar_low,
    ar_recv_low,
    local_sem,
    zs_sem,
    zr_sem,
    ag_ssem,
    ag_rsem,
    s1_ssem,
    s1_rsem,
    a_ssem,
    a_rsem,
    c_ssem,
    c_rsem,
    ar_ssem,
    ar_rsem,
    adz_ssem,
    adz_rsem,
    h1_ssem,
    h1_rsem,
    h2_ssem,
    h2_rsem,
    q1_ssem,
    q1_rsem,
    q2_ssem,
    q2_rsem,
):
    z = lax.axis_index("fsdp")
    s = lax.axis_index("seq")
    core = s % 2
    chip = s // 2
    to_core = (z, chip * 2 + (1 - core))
    chip_x = chip + 1 - 2 * (chip % 2)
    chip_y = (chip + 2) % 4
    chip_d = chip_x + 2 - 4 * (chip_x // 2)
    to_x = (z, chip_x * 2 + core)
    to_y = (z, chip_y * 2 + core)
    rows, width = tok_ref.shape
    length = normed.shape[0]
    units = act.shape[1]
    fan = width // planes
    mine = wq.shape[3]
    tiles = length // TILE

    def remote(src, dst, ssem, rsem, where):
        return pltpu.make_async_remote_copy(
            src_ref=src, dst_ref=dst, send_sem=ssem, recv_sem=rsem, device_id=where,
            device_id_type=MESH,
        )

    def line(ref, cols):
        return ref[cols].astype(F32)[None, :]

    def block(i, n):
        return pl.ds(pl.multiple_of(i * n, n), n)

    bar = pltpu.get_barrier_semaphore()
    for k in range(1, 8):
        pl.semaphore_signal(bar, inc=1, device_id=(z, (s + k) % 8), device_id_type=MESH)
    for k in range(1, planes):
        pl.semaphore_signal(bar, inc=1, device_id=((z + k) % planes, s), device_id_type=MESH)
    pl.semaphore_wait(bar, 7 + planes - 1)

    chunks = []
    for c in range(3):
        chunks.append((wq_in.at[c], lambda j, c=c: wq.at[j, c]))
    chunks.append((wd_in, lambda j: wd.at[j]))
    part = fan // 4
    for i in range(4):
        chunks.append(
            (
                wi_in.at[pl.ds(i * part, part), :],
                lambda j, i=i: wi.at[j, pl.ds(i * part, part), :],
            )
        )
    for i in range(fan // PART):
        chunks.append(
            (
                wo_in.at[:, pl.ds(i * PART, PART)],
                lambda j, i=i: wo.at[j, :, pl.ds(i * PART, PART)],
            )
        )
    n_chunks = len(chunks)
    ahead = 2
    last_step = n_chunks + planes - 1

    def zcopy(c, direction, k):
        src, place = chunks[c]
        j = z - k if direction == 0 else z + k
        return remote(
            src if k == 0 else place(j),
            place(j),
            zs_sem.at[c, direction, k],
            zr_sem.at[c, j],
            (z + 1, s) if direction == 0 else (z - 1, s),
        )

    def zhas(direction, k):
        if direction == 0:
            return jnp.logical_and(z - k >= 0, z + 1 < planes)
        return jnp.logical_and(z + k < planes, z - 1 >= 0)

    def zsend(c, k):
        for direction in (0, 1):

            @pl.when(zhas(direction, k))
            def _(direction=direction):
                zcopy(c, direction, k).start()

    def zarrived(c, j):
        place = chunks[c][1](j)
        pltpu.make_async_copy(place, place, zr_sem.at[c, j]).wait()

    def zrelay(c, k):
        for direction in (0, 1):

            @pl.when(zhas(direction, k))
            def _(direction=direction):
                zarrived(c, z - k if direction == 0 else z + k)
                zcopy(c, direction, k).start()

    def zfinish(first, last):
        for c in range(first, last):
            for direction in (0, 1):
                for k in range(1, planes):
                    j = z - k if direction == 0 else z + k
                    here = z == planes - 1 if direction == 0 else z == 0

                    @pl.when(here)
                    def _(c=c, j=j):
                        zarrived(c, j)

    def zstep(t):
        if t == 0:
            for c in range(min(ahead, n_chunks - 1) + 1):
                zsend(c, 0)
        elif t + ahead < n_chunks:
            zsend(t + ahead, 0)
        for k in range(1, planes - 1):
            if 0 <= t - k < n_chunks:
                zrelay(t - k, k)

    own = []
    for c in range(n_chunks):
        src, place = chunks[c]
        own.append(pltpu.make_async_copy(src, place(z), local_sem.at[c]))
    zstep(0)
    for copy in own:
        copy.start()

    half = width // 2

    def row_view(buf, b, part):
        if part is None:
            return buf.at[block(b, rows), :]
        return buf.at[block(b, rows), pl.ds(part * half, half)]

    def lead_view(buf, b, part):
        if part is None:
            return buf.at[b]
        return buf.at[b, pl.ds(part * (planes // 2), planes // 2)]

    def gather_copies(p, buf, view):
        bx = chip_x * 2 + core
        by = chip_y * 2 + core
        bd = chip_d * 2 + core
        me = view(buf, s, None)
        blk_x = view(buf, bx, None)
        blk_y = view(buf, by, None)
        blk_d = view(buf, bd, None)
        x0 = view(buf, bx, 0)
        y1 = view(buf, by, 1)
        d0 = view(buf, bd, 0)
        d1 = view(buf, bd, 1)
        ss, rs = ag_ssem.at[p], ag_rsem.at[p]

        def same(ref, i, where):
            return remote(ref, ref, ss.at[i], rs.at[i], where)

        sends = [
            same(me, 0, to_x),
            same(me, 1, to_y),
            same(me, 2, to_core),
            same(x0, 3, to_y),
            same(blk_x, 4, to_core),
            same(y1, 5, to_x),
            same(blk_y, 6, to_core),
            same(blk_d, 7, to_core),
        ]
        other = 1 - core
        into = [
            blk_x,
            blk_y,
            view(buf, chip * 2 + other, None),
            d0,
            view(buf, chip_x * 2 + other, None),
            d1,
            view(buf, chip_y * 2 + other, None),
            view(buf, chip_d * 2 + other, None),
        ]

        def arrived(i):
            pltpu.make_async_copy(into[i], into[i], rs.at[i]).wait()

        return sends, arrived

    cot[block(s, rows), :] = cotown_ref[...]
    c_sends, c_arrived = gather_copies(0, cot, row_view)
    for i in range(3):
        c_sends[i].start()

    counts = [m.shape[0] for m in map_refs]
    spans = [2 * n if n % 128 else n for n in counts]
    bases = [sum(spans[:i]) for i in range(8)]
    stack[...] = jnp.zeros_like(stack)
    odd = s % 2
    for m, n, span, base in zip(map_refs, counts, spans, bases):
        at = base + (odd * n if span != n else 0)
        stack[pl.ds(pl.multiple_of(at, 64), n), :] = m[...]
    lane = lax.broadcasted_iota(jnp.int32, (RANK, ADAPT * RANK), 1)
    column = lax.broadcasted_iota(jnp.int32, (RANK, ADAPT * RANK), 0)
    picks = []
    for g in range(planes):
        picks.append((lane == column + index_ref[g] * RANK).astype(F32))
        sel[g] = dot_nt(picks[g].astype(BF16), stack[...]).astype(BF16)

    def adapter_copy(k):
        g = (z + k) % planes
        return remote(sel.at[g], adm.at[s, z], adz_ssem.at[k - 1], adz_rsem.at[z], (g, s))

    for k in range(1, planes):
        adapter_copy(k).start()
    adm[s, z] = sel[z]

    x = tok_ref[...].astype(F32)
    mean = jnp.mean(x, axis=-1, keepdims=True)
    centred = x - mean
    inv = lax.rsqrt(jnp.mean(centred * centred, axis=-1, keepdims=True) + EPSILON)
    normed[block(s, rows), :] = (
        centred * inv * line(gain_ref, ALL) + line(shift_ref, ALL)
    ).astype(BF16)
    n_sends, n_arrived = gather_copies(1, normed, row_view)
    for k in range(1, planes):
        g = (z + k) % planes
        pltpu.make_async_copy(adm.at[s, g], adm.at[s, g], adz_rsem.at[g]).wait()
    m_sends, m_arrived = gather_copies(2, adm, lead_view)
    gathers = ((c_sends, c_arrived), (n_sends, n_arrived), (m_sends, m_arrived))
    zstep(1)
    for m, (sends, arrived) in enumerate(gathers):
        arrived(0)
        sends[3].start()
        sends[4].start()
        arrived(1)
        sends[5].start()
        sends[6].start()
        if m < 2:
            for i in range(3):
                gathers[m + 1][0][i].start()
            zstep(m + 2)
    zstep(4)
    for m, (sends, arrived) in enumerate(gathers):
        arrived(3)
        arrived(5)
        sends[7].start()
    for sends, arrived in gathers:
        for i in (2, 4, 6, 7):
            arrived(i)
    zstep(5)

    def order(f, carry):
        for pair in range(4):

            def both(i):
                cols = slice(bases[i], bases[i] + spans[i])
                return adm[2 * pair, f, :, cols] + adm[2 * pair + 1, f, :, cols]

            where = block(f * 4 + pair, 128)
            downs_ref[:RANK, where] = both(0)
            downs_ref[RANK:, where] = both(4)
            ups_ref[:RANK, where] = both(3)
            ups_ref[RANK:, where] = both(7)
            ddown_all[:, where] = both(2)
            qup_all[:, block(f * 4 + pair, spans[1])] = both(1)
        return carry

    lax.fori_loop(0, planes, order, 0)
    for j in range(4):
        q = s * 4 + j
        n = counts[5]
        iup_ref[:, j * n : (j + 1) * n] = adm[q % 8, q // 8, :, bases[5] : bases[5] + n]
        odown_ref[:, j * n : (j + 1) * n] = adm[q % 8, q // 8, :, bases[6] : bases[6] + n]

    def qup(c):
        return qup_all[:, pl.ds(pl.multiple_of(c * width + s * mine, mine), mine)]

    def ddown():
        return ddown_all[:, block(s, mine)]

    def low(t, carry):
        r = block(t, TILE)
        c = dot_nt(normed[r, :], downs_ref[...])
        coeff[r, :] = c.astype(BF16)
        g = ADAPTER_SCALE * dot_nt(cot[r, :], ups_ref[...])
        cgs[r, :] = g.astype(BF16)
        return carry

    lax.fori_loop(0, tiles, low, 0)
    for copy in own:
        copy.wait()
    zstep(6)
    zfinish(0, 4)

    def project(t, carry):
        r = block(t, TILE)
        cos = cos_ref[r, :]
        sin = sin_ref[r, :]
        for c in range(3):
            v = ADAPTER_SCALE * dot(coeff[r, :RANK], qup(c))
            v = v + line(qb_ref, pl.ds(pl.multiple_of(c * width + s * mine, mine), mine))
            for j in range(planes):
                v = v + dot(normed[r, j * fan : (j + 1) * fan], wq[j, c])
            if c < 2:
                v = turn_all(v, cos, sin, 1.0)
            v = v.astype(BF16)
            if c == 0:
                v = v * jnp.asarray(HD**-0.5, BF16)
            qkv[c, r, :] = v
        g = dot(cgs[r, :RANK], ddown())
        for j in range(planes):
            g = g + dot_nt(cot[r, j * fan : (j + 1) * fan], wd[j])
        hg[r, :] = g.astype(BF16)
        return carry

    lax.fori_loop(0, tiles, project, 0)
    zstep(7)

    dk = ag.at[:, pl.ds(0, mine)]
    dv = ag.at[:, pl.ds(mine, mine)]
    ag[:, : 2 * mine] = jnp.zeros((length, 2 * mine), F32)
    heads = mine // HD

    for b in range(length // BLOCK):
        lo, hi = b * BLOCK, (b + 1) * BLOCK
        acc_a[...] = jnp.zeros_like(acc_a)
        acc_b[...] = jnp.zeros_like(acc_b)

        def one_head(h, carry, lo=lo, hi=hi):
            lane = lax.broadcasted_iota(jnp.int32, (1, mine), 1)
            mask = (lane // HD == h).astype(BF16)
            mask32 = (lane // HD == h).astype(F32)
            q = qkv[0, lo:hi, :] * mask
            g = hg[lo:hi, :] * mask
            k = qkv[1, :hi, :]
            v = qkv[2, :hi, :]
            sc = dot_nt(q, k)
            e = jnp.exp(sc - jnp.max(sc, axis=-1, keepdims=True))
            p = e * (1.0 / jnp.sum(e, axis=-1, keepdims=True))
            pb = p.astype(BF16)
            acc_a[...] += dot(pb, v) * mask32
            dp = dot_nt(g, v)
            ds = (p * (dp - jnp.sum(dp * p, axis=-1, keepdims=True))).astype(BF16)
            acc_b[...] += dot(ds, k) * mask32
            dk[:hi, :] += dot_tn(ds, q)
            dv[:hi, :] += dot_tn(pb, g)
            return carry

        lax.fori_loop(0, heads, one_head, 0)
        att[lo:hi, :] = acc_a[...].astype(BF16)
        back = (acc_b[...] * (HD**-0.5)).astype(BF16).astype(F32)
        pg[0, lo:hi, :] = turn_all(back, cos_ref[lo:hi, :], sin_ref[lo:hi, :], -1.0).astype(BF16)
        if b == 1:
            zstep(8)
        if b == 2:
            zstep(9)
        if b == 3:
            zstep(10)

    def finish(t, carry):
        r = block(t, TILE)
        back = dk[r, :].astype(BF16).astype(F32)
        pg[1, r, :] = turn_all(back, cos_ref[r, :], sin_ref[r, :], -1.0).astype(BF16)
        pg[2, r, :] = dv[r, :].astype(BF16)
        return carry

    lax.fori_loop(0, tiles, finish, 0)

    coeff_t[...] = dot_nt(downs_ref[...], normed[...]).astype(BF16)
    cgs_t[...] = (ADAPTER_SCALE * dot_nt(ups_ref[...], cot[...])).astype(BF16)

    share = width // 8

    def wait_on(ref, sem):
        pltpu.make_async_copy(ref, ref, sem).wait()

    def hop1(w, msg, h1, start):
        for j in range(4):
            to = 4 * (s % 2) + j
            there = (z, to)

            @pl.when(to != s)
            def _(j=j, there=there):
                copy = remote(
                    msg.at[j], h1.at[s // 2], h1_ssem.at[w, j], h1_rsem.at[w, s // 2], there
                )
                if start:
                    copy.start()
                else:
                    copy.wait_send()

            if start:

                @pl.when(to == s)
                def _(j=j):
                    pltpu.make_async_copy(
                        msg.at[j], h1.at[s // 2], h1_rsem.at[w, s // 2]
                    ).start()

    def hop2_copy(w, h1, h2, k):
        g = (z + k) % planes
        return remote(h1.at[g], h2.at[z], h2_ssem.at[w, k - 1], h2_rsem.at[w, z], (g, s))

    def hop2(w, h1, h2):
        for g in range(planes):
            wait_on(h1.at[g], h1_rsem.at[w, g])
        for k in range(1, planes):
            hop2_copy(w, h1, h2, k).start()
        h2[z] = h1[z]

    def landed(w, h1, h2):
        for k in range(1, planes):
            g = (z + k) % planes
            wait_on(h2.at[g], h2_rsem.at[w, g])
        for k in range(1, planes):
            hop2_copy(w, h1, h2, k).wait_send()

    pick_all = jnp.concatenate(picks, axis=0)

    def spread(h2):
        return lax.dot_general(
            h2.reshape(planes * RANK, h2.shape[-1]), pick_all, (((0,), (0,)), ((), ())),
            precision=lax.Precision.HIGHEST, preferred_element_type=F32,
        )

    def half_rows(v):
        return jnp.where(s % 2 == 0, v[:64], v[64:])

    for c in range(3):
        g = ADAPTER_SCALE * dot(coeff_t[:RANK, :], pg[c])
        for i in range(2):
            qgrad[2 * c + i] = g[:, i * 128 : (i + 1) * 128]

    def qkv_hop1(start):
        for c in range(3):
            for i in range(2):
                t = 16 * c + 2 * s + i
                for o in range(2):
                    owner = 2 * (t // 3) + o
                    slot = t % 3 - o
                    ok = jnp.logical_and(slot >= 0, slot <= 1)
                    to = owner % 8
                    src = qgrad.at[2 * c + i]
                    n = 4 * c + 2 * i + o

                    @pl.when(jnp.logical_and(ok, to != s))
                    def _(src=src, owner=owner, slot=slot, to=to, n=n):
                        copy = remote(
                            src, q_h1.at[owner // 8, slot], q1_ssem.at[n],
                            q1_rsem.at[owner // 8, slot], (z, to),
                        )
                        if start:
                            copy.start()
                        else:
                            copy.wait_send()

                    if start:

                        @pl.when(jnp.logical_and(ok, to == s))
                        def _(src=src, owner=owner, slot=slot):
                            pltpu.make_async_copy(
                                src, q_h1.at[owner // 8, slot], q1_rsem.at[owner // 8, slot]
                            ).start()

    def qkv_hop2_copy(k):
        g = (z + k) % planes
        return remote(q_h1.at[g], q_h2.at[z], q2_ssem.at[k - 1], q2_rsem.at[z], (g, s))

    def qkv_hop2():
        for g in range(planes):
            for slot in range(2):
                wait_on(q_h1.at[g, slot], q1_rsem.at[g, slot])
        for k in range(1, planes):
            qkv_hop2_copy(k).start()
        q_h2[z] = q_h1[z]

    def qkv_landed():
        for k in range(1, planes):
            g = (z + k) % planes
            wait_on(q_h2.at[g], q2_rsem.at[g])
        for k in range(1, planes):
            qkv_hop2_copy(k).wait_send()

    qkv_hop1(True)
    g = dot(cgs_t[:RANK, :], att[...])
    for j in range(4):
        a_msg[j, :, 256:384] = g[:, (j // 2) * 128 : (j // 2 + 1) * 128]
    pass
    zfinish(4, 8)
    zstep(11)

    k0 = 0.7978845608028654
    k1 = 0.044715

    def inner(t, carry):
        r = block(t, TILE)
        v = ADAPTER_SCALE * dot(coeff[r, RANK : 2 * RANK], iup_ref[...])
        v = v + line(ib_ref, block(s, units))
        for j in range(planes):
            v = v + dot(normed[r, j * fan : (j + 1) * fan], wi[j])
        sq = v * v
        th = jnp.tanh(k0 * v * (1.0 + k1 * sq))
        act[r, :] = (0.5 * v * (1.0 + th)).astype(BF16)
        pre[r, :] = 0.5 * (1.0 + th) + 0.5 * v * (1.0 - th * th) * (k0 * (1.0 + 3.0 * k1 * sq))
        return carry

    lax.fori_loop(0, tiles, inner, 0)
    for k in range(1, planes):
        adapter_copy(k).wait_send()
    for sends, _ in gathers:
        for copy in sends:
            copy.wait_send()
    spot = (8, planes, RANK, share)
    for i in range(length // (8 * planes * RANK)):
        span = 8 * planes * RANK
        adm[:, :, :, i * share : (i + 1) * share] = normed[
            i * span : (i + 1) * span, block(s, share)
        ].reshape(spot)
    g = dot(cgs_t[RANK : 2 * RANK, :], act[...])
    for j in range(4):
        a_msg[j, :, :256] = g[:, j * 256 : (j + 1) * 256]
    qkv_hop2()
    zstep(12)

    partners = (to_core, to_x, to_y)

    def reduce_copy(w, i):
        src = ar_send.at[0] if w == 0 else ar_low
        dst = ar_recv.at[i] if w == 0 else ar_recv_low.at[i]
        return remote(src, dst, ar_ssem.at[w, i], ar_rsem.at[w, i], partners[i])

    def reduce_round(w, i):
        if i > 0:
            reduce_copy(w, i - 1).wait()
            got = ar_recv[i - 1] if w == 0 else ar_recv_low[i - 1].astype(F32)
            ar_send[w] += got
        if i < 3:
            if w == 1:
                ar_low[...] = ar_send[1].astype(BF16)
            reduce_copy(w, i).start()

    ar_send[0, :RANK, :] = dot_nt(ddown(), att[...])
    ar_send[0, RANK : 2 * RANK, :] = dot_nt(odown_ref[...], act[...])
    for i in range(4):
        reduce_round(0, i)
        pass
    coeff_dense = ar_send[0].astype(BF16)
    for i in range(2):
        g = ADAPTER_SCALE * dot(
            coeff_dense[i * RANK : (i + 1) * RANK, :], cot[:, block(s, share)]
        )
        for j in range(4):
            at = 384 + i * 128
            a_msg[j, :, at : at + 128] = g[:, (j // 2) * 128 : (j // 2 + 1) * 128]
    hop1(0, a_msg, a_h1, True)

    p_units = width // UNIT
    per = fan // UNIT
    early = p_units - planes // 2
    total = 2 * p_units

    def branch_place(n):
        return (n % (planes // 2)) * 2, n // (planes // 2)

    def back_place(n):
        return (n - p_units) // per, (n - p_units) % per

    def keep_split(n, k, r):
        slot = n % 2
        a = r[:rows, :]
        b = r[rows:, :]
        first = core == 0
        keep[n % 6, k] = jnp.where(first, a, b)
        s1_send[slot, k] = jnp.where(first, b, a).astype(BF16)

    def keep_pair(n, k, v):
        keep_split(n, 2 * k, v[:TILE])
        keep_split(n, 2 * k + 1, v[TILE:])

    def s1_copy(n):
        return remote(s1_send.at[n % 2], s1_recv.at[n], s1_ssem.at[n % 2], s1_rsem.at[n], to_core)

    def a_copy(n, i):
        return remote(
            a_send.at[n % 3, i], a_recv.at[n, i], a_ssem.at[n % 3, i], a_rsem.at[n, i],
            (to_x, to_y)[i],
        )

    def c_copy(n, i):
        return remote(
            c_send.at[n % 3, i], c_recv.at[n, i], c_ssem.at[n % 3, i], c_rsem.at[n, i],
            (to_x, to_y)[i],
        )

    hu = UNIT // 2

    def stage0_branch(n):
        j, i = branch_place(n)

        def tile(k, carry):
            r = block(k, 2 * TILE)
            cols = block(i, PART)
            w_o = jnp.concatenate([wo[j, :, cols], wo[j + 1, :, cols]], axis=1)
            w_d = jnp.concatenate([wd[j, :, cols], wd[j + 1, :, cols]], axis=1)
            keep_pair(n, k, dot(act[r, :], w_o) + dot(att[r, :], w_d))
            return carry

        lax.fori_loop(0, tiles // 2, tile, 0)
        s1_copy(n).start()

    def stage0_back(n):
        j, i = back_place(n)

        def tile(k, carry):
            r = block(k, 2 * TILE)
            rws = block(i, UNIT)
            v = dot_nt(pgrad[r, :], wi[j, rws, :])
            v = v + normed[r, block(n - p_units, UNIT)].astype(F32)
            keep_pair(n, k, v)
            return carry

        lax.fori_loop(0, tiles // 2, tile, 0)
        s1_copy(n).start()

    def stage1(n):
        s1_copy(n).wait()
        q = n % 6
        for k in range(4):
            keep[q, k] += s1_recv[n, k].astype(F32)
        far = keep[q, chip_d]
        a_send[n % 3, 0] = far[:, :hu].astype(BF16)
        a_send[n % 3, 1] = far[:, hu:].astype(BF16)
        for i in range(2):
            a_copy(n, i).start()

    def stage2(n):
        q = n % 6
        for i in range(2):
            a_copy(n, i).wait()
        keep[q, chip_y, :, :hu] += a_recv[n, 0].astype(F32)
        keep[q, chip_x, :, hu:] += a_recv[n, 1].astype(F32)
        c_send[n % 3, 0] = keep[q, chip_x].astype(BF16)
        c_send[n % 3, 1] = keep[q, chip_y].astype(BF16)
        for i in range(2):
            c_copy(n, i).start()

    def stage3(n):
        q = n % 6
        for i in range(2):
            c_copy(n, i).wait()
        v = keep[q, chip] + c_recv[n, 0].astype(F32) + c_recv[n, 1].astype(F32)

        @pl.when(n < p_units)
        def _():
            j, i = branch_place(n)
            for m in range(2):
                res[:, pl.ds(pl.multiple_of((j + m) * fan + i * PART, PART), PART)] = v[
                    :, m * PART : (m + 1) * PART
                ]

        @pl.when(n >= p_units)
        def _():
            igrad_ref[:, block(n - p_units, UNIT)] = v

    def pipeline(first, lo, hi, stage0, extra=None, units_end=None):
        def body(n, carry):
            if stage0 is not None:
                stage0(n)
            for back, stage in ((1, stage1), (3, stage2), (5, stage3)):
                m = n - back
                ok = m >= first
                if stage0 is None:
                    ok = jnp.logical_and(ok, m < units_end)

                @pl.when(ok)
                def _(m=m, stage=stage):
                    stage(m)

            if extra is not None:
                extra(n)
            return carry

        lax.fori_loop(lo, hi, body, 0)

    zstep(13)
    def act_part(r, i):
        cols = [slice(j * fan + i * PART, j * fan + (i + 1) * PART) for j in range(planes)]
        g = jnp.concatenate([cot[r, c] for c in cols], axis=1)
        w = [wo[j, :, i * PART : (i + 1) * PART] for j in range(planes)]
        return dot_nt(g, jnp.concatenate(w, axis=1))

    def attention_back(u, carry):
        j = u // per
        rws = block(u % per, UNIT)
        for h in range(2):
            r = slice(h * length // 2, (h + 1) * length // 2)
            v = dot_nt(pg[0, r, :], wq[j, 0, rws, :])
            for c in range(1, 3):
                v = v + dot_nt(pg[c, r, :], wq[j, c, rws, :])
            normed[r, block(u, UNIT)] = v.astype(BF16)
        return carry

    lax.fori_loop(0, p_units, attention_back, 0)

    per_part = planes // 2
    for i in range(fan // PART - 1):
        zfinish(8 + i, 9 + i)
        pipeline(0, i * per_part, (i + 1) * per_part, stage0_branch)

        def act_back(t, carry, i=i):
            r = block(t, TILE)
            first = dot(cgs[r, RANK : 2 * RANK], odown_ref[...]) if i == 0 else ag[r, :]
            ag[r, :] = first + act_part(r, i)
            return carry

        lax.fori_loop(0, tiles, act_back, 0)
        if i == 0:
            hop2(0, a_h1, a_h2)
    pipeline(0, early, early + 5, None, None, early)
    zfinish(11, 12)

    pipeline(early, early, p_units, stage0_branch)

    def act_last(t, carry):
        r = block(t, TILE)
        v = ag[r, :] + act_part(r, fan // PART - 1)
        pgrad[r, :] = (v * pre[r, :]).astype(BF16)
        return carry

    lax.fori_loop(0, tiles, act_last, 0)

    def rounds(n):
        @pl.when(n == p_units)
        def _():
            up_part = dot_nt(iup_ref[...], pgrad[...])
            q_part = dot_nt(qup(0), pg[0])
            for c in range(1, 3):
                q_part = q_part + dot_nt(qup(c), pg[c])
            ar_send[1, :RANK, :] = ADAPTER_SCALE * q_part
            ar_send[1, RANK : 2 * RANK, :] = ADAPTER_SCALE * up_part
            reduce_round(1, 0)

        @pl.when(n == p_units + 1)
        def _():
            qkv_landed()
            full = [spread(q_h2[:, i]) for i in range(2)]
            full = jnp.concatenate(full, axis=0)
            grad_refs[1][...] = jnp.where(s % 2 == 0, full[:192], full[64:])

        @pl.when(n == p_units + 3)
        def _():
            landed(0, a_h1, a_h2)
            full = spread(a_h2[...])
            grad_refs[6][...] = full[:256]
            grad_refs[2][...] = half_rows(full[256:384])
            grad_refs[3][...] = half_rows(full[384:512])
            grad_refs[7][...] = half_rows(full[512:640])


        for i in range(1, 4):

            @pl.when(n == p_units + (1, 3, 5)[i - 1])
            def _(i=i):
                reduce_round(1, i)
                if i == 2:
                    g = ADAPTER_SCALE * dot(coeff_t[RANK : 2 * RANK, :], pgrad[...])
                    for j in range(4):
                        b_msg[j, :, :256] = g[:, j * 256 : (j + 1) * 256]
                if i == 3:
                    g = None
                    span = 8 * planes * RANK
                    for m in range(length // span):
                        part = dot(
                            ar_send[1, :, m * span : (m + 1) * span].astype(BF16),
                            adm[:, :, :, m * share : (m + 1) * share].reshape(span, share),
                        )
                        g = part if g is None else g + part
                    for m in range(2):
                        for j in range(4):
                            b_msg[j, :, 256 + m * 128 : 384 + m * 128] = g[
                                m * RANK : (m + 1) * RANK, (j // 2) * 128 : (j // 2 + 1) * 128
                            ]
                    hop1(1, b_msg, b_h1, True)

    pipeline(early, p_units, total, stage0_back, rounds)
    pipeline(early, total, total + 3, None, None, total)
    hop2(1, b_h1, b_h2)
    pipeline(early, total + 3, total + 5, None, None, total)

    first_t = ar_send[0, :, block(s, rows)].astype(BF16)
    late_t = ar_send[1, :, block(s, rows)].astype(BF16)
    out = tok_ref[...].astype(F32) + res[...] + ADAPTER_SCALE * dot_tn(first_t, ups_ref[...])
    out_ref[...] = (out + line(db_ref, ALL) + line(ob_ref, ALL)).astype(BF16)
    x = tok_ref[...].astype(F32)
    mean = jnp.mean(x, axis=-1, keepdims=True)
    centred = x - mean
    inv = lax.rsqrt(jnp.mean(centred * centred, axis=-1, keepdims=True) + EPSILON)
    xhat = centred * inv
    e = (igrad_ref[...] + dot_tn(late_t, downs_ref[...])) * line(gain_ref, ALL)
    igrad_ref[...] = cotown_ref[...].astype(F32) + inv * (
        e
        - jnp.mean(e, axis=-1, keepdims=True)
        - xhat * jnp.mean(e * xhat, axis=-1, keepdims=True)
    )

    landed(1, b_h1, b_h2)
    full = spread(b_h2[...])
    grad_refs[5][...] = full[:256]
    grad_refs[0][...] = half_rows(full[256:384])
    grad_refs[4][...] = half_rows(full[384:512])

    hop1(0, a_msg, a_h1, False)
    hop1(1, b_msg, b_h1, False)
    qkv_hop1(False)
    for c in range(n_chunks):
        for k in range(planes - 1):
            for direction in (0, 1):

                @pl.when(zhas(direction, k))
                def _(c=c, k=k, direction=direction):
                    zcopy(c, direction, k).wait_send()


def run_layer(planes, args, shapes):
    rows, width, length, units, mine = shapes
    fan = width // planes
    vm = pl.BlockSpec(memory_space=pltpu.VMEM)
    hbm = pl.BlockSpec(memory_space=pl.ANY)
    n_chunks = 8 + fan // PART
    total = 2 * width // UNIT
    dma = pltpu.SemaphoreType.DMA
    maps = args[13:21]
    lanes = sum(2 * m.shape[0] if m.shape[0] % 128 else m.shape[0] for m in maps)

    def entry(*refs):
        layer_kernel(planes, *refs[:13], refs[13:21], *refs[21:25], refs[25:33], *refs[33:])

    outs = pl.pallas_call(
        entry,
        out_shape=(
            jax.ShapeDtypeStruct((rows, width), BF16),
            jax.ShapeDtypeStruct((rows, width), F32),
            *(jax.ShapeDtypeStruct(m.shape, F32) for m in maps),
        ),
        in_specs=[vm, vm, hbm, hbm, hbm, hbm]
        + [vm] * 6
        + [pl.BlockSpec(memory_space=pltpu.SMEM)]
        + [vm] * 10,
        out_specs=(vm,) * 10,
        scratch_shapes=[
            pltpu.VMEM((lanes, ADAPT * RANK), BF16),
            pltpu.VMEM((planes, RANK, lanes), BF16),
            pltpu.VMEM((8, planes, RANK, lanes), BF16),
            pltpu.VMEM((2 * RANK, width), BF16),
            pltpu.VMEM((2 * RANK, width), BF16),
            pltpu.VMEM((RANK, width), BF16),
            pltpu.VMEM((RANK, 3 * width), BF16),
            pltpu.VMEM((RANK, units), BF16),
            pltpu.VMEM((RANK, units), BF16),
            pltpu.VMEM((6, RANK, 128), F32),
            pltpu.VMEM((4, RANK, 640), F32),
            pltpu.VMEM((planes, RANK, 640), F32),
            pltpu.VMEM((planes, RANK, 640), F32),
            pltpu.VMEM((4, RANK, 512), F32),
            pltpu.VMEM((planes, RANK, 512), F32),
            pltpu.VMEM((planes, RANK, 512), F32),
            pltpu.VMEM((planes, 2, RANK, 128), F32),
            pltpu.VMEM((planes, 2, RANK, 128), F32),
            pltpu.VMEM((length, width), BF16),
            pltpu.VMEM((length, width), BF16),
            pltpu.VMEM((planes, 3, fan, mine), BF16),
            pltpu.VMEM((planes, mine, fan), BF16),
            pltpu.VMEM((planes, fan, units), BF16),
            pltpu.VMEM((planes, units, fan), BF16),
            pltpu.VMEM((3, length, mine), BF16),
            pltpu.VMEM((length, mine), BF16),
            pltpu.VMEM((length, mine), BF16),
            pltpu.VMEM((3, length, mine), BF16),
            pltpu.VMEM((BLOCK, mine), F32),
            pltpu.VMEM((BLOCK, mine), F32),
            pltpu.VMEM((length, units), F32),
            pltpu.VMEM((length, units), BF16),
            pltpu.VMEM((length, units), F32),
            pltpu.VMEM((length, units), BF16),
            pltpu.VMEM((length, 2 * RANK), BF16),
            pltpu.VMEM((length, 2 * RANK), BF16),
            pltpu.VMEM((2 * RANK, length), BF16),
            pltpu.VMEM((2 * RANK, length), BF16),
            pltpu.VMEM((rows, width), F32),
            pltpu.VMEM((6, 4, rows, UNIT), F32),
            pltpu.VMEM((2, 4, rows, UNIT), BF16),
            pltpu.VMEM((total, 4, rows, UNIT), BF16),
            pltpu.VMEM((3, 2, rows, UNIT // 2), BF16),
            pltpu.VMEM((total, 2, rows, UNIT // 2), BF16),
            pltpu.VMEM((3, 2, rows, UNIT), BF16),
            pltpu.VMEM((total, 2, rows, UNIT), BF16),
            pltpu.VMEM((2, 2 * RANK, length), F32),
            pltpu.VMEM((3, 2 * RANK, length), F32),
            pltpu.VMEM((2 * RANK, length), BF16),
            pltpu.VMEM((3, 2 * RANK, length), BF16),
            dma((n_chunks,)),
            dma((n_chunks, 2, planes)),
            dma((n_chunks, planes)),
            dma((3, 8)),
            dma((3, 8)),
            dma((2,)),
            dma((total,)),
            dma((3, 2)),
            dma((total, 2)),
            dma((3, 2)),
            dma((total, 2)),
            dma((2, 3)),
            dma((2, 3)),
            dma((planes,)),
            dma((planes,)),
            dma((2, 4)),
            dma((2, planes)),
            dma((2, planes)),
            dma((2, planes)),
            dma((12,)),
            dma((planes, 2)),
            dma((planes,)),
            dma((planes,)),
        ],
        compiler_params=pltpu.CompilerParams(
            collective_id=0, has_side_effects=True, vmem_limit_bytes=63 * 1024 * 1024
        ),
    )(*args)
    return pl.pallas_call(
        hand_over,
        out_shape=tuple(jax.ShapeDtypeStruct(o.shape, o.dtype) for o in outs),
        in_specs=[vm] * 10,
        out_specs=(vm,) * 10,
    )(*outs)


def hand_over(*refs):
    for i in range(10):
        refs[10 + i][...] = refs[i][...]


def fits(planes, groups, shapes):
    rows, width, length, units, mine = shapes
    return (
        groups == 8
        and planes == 4
        and rows * 2 == TILE
        and length <= 1024
        and width == 2048
        and mine == 256
        and units == 1024
    )


def deliver(packed, sizes, counts, pick, planes, groups):
    s = lax.axis_index("seq")
    everyone = lax.all_gather(packed, "seq", axis=0, tiled=False)
    owned = []
    at = 0
    for i, (n, w) in enumerate(zip(counts, sizes)):
        part = everyone[:, :, at : at + w]
        at += w
        blocks = 3 if i == 1 else 1
        part = part.reshape(groups, RANK, blocks, w // blocks).transpose(1, 2, 0, 3)
        part = part.reshape(RANK, planes, groups, n)
        owned.append(lax.dynamic_index_in_dim(part, s, 2, keepdims=False))
    owned = jnp.concatenate(owned, axis=2).transpose(1, 0, 2)
    arrived = lax.all_to_all(owned, "fsdp", split_axis=0, concat_axis=0, tiled=True)
    place = pick.astype(F32).reshape(planes * RANK, ADAPT * RANK)
    spread = lax.dot_general(
        arrived.reshape(planes * RANK, -1),
        place,
        (((0,), (0,)), ((), ())),
        precision=lax.Precision.HIGHEST,
        preferred_element_type=F32,
    )
    outs = []
    at = 0
    for n in counts:
        outs.append(spread[at : at + n])
        at += n
    return outs


def on_device(
    tokens,
    cotangent,
    adapter_index,
    qkv_weight,
    dense_weight,
    inner_weight,
    outer_weight,
    qkv_bias,
    dense_bias,
    inner_bias,
    outer_bias,
    norm_gain,
    norm_bias,
    *maps,
):
    planes = lax.axis_size("fsdp")
    groups = lax.axis_size("seq")
    rows, width = tokens.shape
    length = rows * groups
    heads = H // groups
    mine = heads * HD
    units = inner_weight.shape[1]
    s = lax.axis_index("seq")

    shapes = (rows, width, length, units, mine)
    if fits(planes, groups, shapes):
        return run_layer(
            planes,
            (
                tokens,
                cotangent,
                qkv_weight,
                dense_weight,
                inner_weight,
                outer_weight,
                qkv_bias,
                dense_bias,
                inner_bias,
                outer_bias,
                norm_gain,
                norm_bias,
                adapter_index,
                *maps,
                *rope_constants(length),
            ),
            shapes,
        )

    counts = [m.shape[0] for m in maps]
    stacked = jnp.concatenate(maps, axis=0)
    wanted = (adapter_index[:, None] * RANK + jnp.arange(RANK)[None, :]).reshape(-1)
    pick = (wanted[:, None] == jnp.arange(ADAPT * RANK)[None, :]).astype(BF16)
    chosen = dot_nt(pick, stacked).astype(BF16).reshape(planes, RANK, -1)
    chosen = lax.all_to_all(chosen, "fsdp", split_axis=0, concat_axis=0, tiled=True)
    chosen = lax.all_gather(chosen, "seq", axis=1, tiled=False)
    full = []
    at = 0
    for n in counts:
        part = chosen[:, :, :, at : at + n]
        full.append(part.transpose(2, 0, 1, 3).reshape(RANK, -1))
        at += n
    qkv_down, qkv_up, dense_down, dense_up, inner_down, inner_up, outer_down, outer_up = full

    def own(m, n):
        return lax.dynamic_slice_in_dim(m, s * n, n, axis=1)

    qkv_up = jnp.concatenate(
        [own(qkv_up[:, c * width : (c + 1) * width], mine) for c in range(3)], axis=1
    )
    dense_down = own(dense_down, mine)
    inner_up = own(inner_up, units)
    outer_down = own(outer_down, units)

    wqkv = lax.all_gather(qkv_weight, "fsdp", axis=1, tiled=True)
    wdense = lax.all_gather(dense_weight, "fsdp", axis=1, tiled=True)
    winner = lax.all_gather(inner_weight, "fsdp", axis=0, tiled=True)
    wouter = lax.all_gather(outer_weight, "fsdp", axis=1, tiled=True)

    gain = norm_gain.astype(F32)
    shift = norm_bias.astype(F32)
    source = tokens.astype(F32)
    normed_own = norm_layer(source, gain, shift).astype(BF16)
    normed = lax.all_gather(normed_own, "seq", axis=0, tiled=True)
    cot = lax.all_gather(cotangent, "seq", axis=0, tiled=True)

    coeffs = dot_nt(normed, jnp.concatenate([qkv_down, inner_down], axis=0)).astype(BF16)
    qkv_coeff, inner_coeff = coeffs[:, :RANK], coeffs[:, RANK:]
    cgs = (
        ADAPTER_SCALE * dot_nt(cot, jnp.concatenate([dense_up, outer_up], axis=0))
    ).astype(BF16)
    dense_cg, outer_cg = cgs[:, :RANK], cgs[:, RANK:]

    bias = jnp.stack([own(qkv_bias.reshape(3, width)[c : c + 1], mine)[0] for c in range(3)])
    projected = (
        jnp.concatenate([dot(normed, wqkv[c]) for c in range(3)], axis=1)
        + bias.reshape(-1).astype(F32)
        + ADAPTER_SCALE * dot(qkv_coeff, qkv_up)
    ).reshape(length, 3, heads, HD)
    cos_table, sin_table = rope_tables(length, heads)
    query = rotate(projected[:, 0], cos_table, sin_table).astype(BF16).transpose(1, 0, 2)
    key = rotate(projected[:, 1], cos_table, sin_table).astype(BF16).transpose(1, 0, 2)
    value = projected[:, 2].astype(BF16).transpose(1, 0, 2)
    attended_grad = (dot_nt(cot, wdense) + dot(dense_cg, dense_down)).astype(BF16)
    head_grad = attended_grad.reshape(length, heads, HD).transpose(1, 0, 2)

    scale = HD ** (-0.5)

    def bmm(spec, a, b):
        return jnp.einsum(spec, a, b, preferred_element_type=F32)

    key_grad = jnp.zeros((heads, length, HD), F32)
    value_grad = jnp.zeros((heads, length, HD), F32)
    attended_parts = []
    query_parts = []
    for b in range(length // BLOCK):
        lo, hi = b * BLOCK, (b + 1) * BLOCK
        q = query[:, lo:hi]
        k = key[:, :hi]
        v = value[:, :hi]
        g = head_grad[:, lo:hi]
        scores = bmm("hqd,hkd->hqk", q, k) * scale
        row_max = jnp.max(scores, axis=-1, keepdims=True)
        exponent = jnp.exp(scores - row_max)
        prob = exponent / jnp.sum(exponent, axis=-1, keepdims=True)
        prob_low = prob.astype(BF16)
        attended_parts.append(bmm("hqk,hkd->hqd", prob_low, v).astype(BF16))
        prob_grad = bmm("hqd,hkd->hqk", g, v)
        row_dot = jnp.sum(prob_grad * prob, axis=-1, keepdims=True)
        score_grad = (prob * (prob_grad - row_dot)).astype(BF16)
        query_parts.append((bmm("hqk,hkd->hqd", score_grad, k) * scale).astype(BF16))
        key_grad = key_grad.at[:, :hi].add(bmm("hqk,hqd->hkd", score_grad, q) * scale)
        value_grad = value_grad.at[:, :hi].add(bmm("hqk,hqd->hkd", prob_low, g))

    def rows_first(x):
        return x.transpose(1, 0, 2)

    attended = rows_first(jnp.concatenate(attended_parts, axis=1)).reshape(length, mine)
    query_grad = rows_first(jnp.concatenate(query_parts, axis=1)).astype(F32)
    key_back = rows_first(key_grad.astype(BF16)).astype(F32)
    value_back = rows_first(value_grad.astype(BF16)).reshape(length, mine)
    projected_grad = jnp.concatenate(
        [
            rotate(query_grad, cos_table, -sin_table).astype(BF16).reshape(length, mine),
            rotate(key_back, cos_table, -sin_table).astype(BF16).reshape(length, mine),
            value_back,
        ],
        axis=1,
    )

    pre_act = (
        dot(normed, winner)
        + own(inner_bias[None], units).astype(F32)
        + ADAPTER_SCALE * dot(inner_coeff, inner_up)
    )
    act32, gelu_back = jax.vjp(lambda v: jax.nn.gelu(v, approximate=True), pre_act)
    activated = act32.astype(BF16)
    act_grad = dot_nt(cot, wouter) + dot(outer_cg, outer_down)
    pre_grad = gelu_back(act_grad)[0].astype(BF16)

    def scatter(x):
        return lax.psum_scatter(x, "seq", scatter_dimension=0, tiled=True)

    branch = scatter((dot(attended, wdense) + dot(activated, wouter)))
    coeff_sum = scatter(
        jnp.concatenate([dot_nt(attended, dense_down), dot_nt(activated, outer_down)], axis=1)
    )
    back = dot_nt(pre_grad, winner)
    for c in range(3):
        back = back + dot_nt(projected_grad[:, c * mine : (c + 1) * mine], wqkv[c])
    back = scatter(back)
    cg_sum = scatter(
        ADAPTER_SCALE
        * jnp.concatenate([dot_nt(projected_grad, qkv_up), dot_nt(pre_grad, inner_up)], axis=1)
    )
    late_own = jnp.concatenate([coeff_sum, cg_sum], axis=1).astype(BF16)
    late = lax.all_gather(late_own, "seq", axis=0, tiled=True)

    layer_out = (
        source
        + branch
        + dense_bias.astype(F32)
        + outer_bias.astype(F32)
        + ADAPTER_SCALE
        * dot(late_own[:, : 2 * RANK], jnp.concatenate([dense_up, outer_up], axis=0))
    ).astype(BF16)
    normed_grad = back + dot(
        late_own[:, 2 * RANK :], jnp.concatenate([qkv_down, inner_down], axis=0)
    )
    row_mean = jnp.mean(source, axis=-1, keepdims=True)
    centred = source - row_mean
    inv = lax.rsqrt(jnp.mean(centred * centred, axis=-1, keepdims=True) + EPSILON)
    xhat = centred * inv
    e = normed_grad * gain
    input_grad = cotangent.astype(F32) + inv * (
        e
        - jnp.mean(e, axis=-1, keepdims=True)
        - xhat * jnp.mean(e * xhat, axis=-1, keepdims=True)
    )

    share = width // groups
    cot_mine = own(cot, share)
    normed_mine = own(normed, share)
    qkv_up_g = ADAPTER_SCALE * dot_tn(qkv_coeff, projected_grad)
    inner_up_g = ADAPTER_SCALE * dot_tn(inner_coeff, pre_grad)
    dense_down_g = dot_tn(dense_cg, attended)
    outer_down_g = dot_tn(outer_cg, activated)
    ups = ADAPTER_SCALE * dot_tn(late[:, : 2 * RANK], cot_mine)
    downs = dot_tn(late[:, 2 * RANK :], normed_mine)
    mine_grads = [
        downs[:RANK],
        qkv_up_g,
        dense_down_g,
        ups[:RANK],
        downs[RANK:],
        inner_up_g,
        outer_down_g,
        ups[RANK:],
    ]
    packed = jnp.concatenate(mine_grads, axis=1)
    sizes = [g.shape[1] for g in mine_grads]
    outs = deliver(packed, sizes, counts, pick, planes, groups)
    return (layer_out, input_grad, *outs)


def solution(mesh):
    both = P(("fsdp", "seq"), None)
    placed = (
        both,
        both,
        P(),
        P(None, "fsdp", "seq"),
        P("seq", "fsdp"),
        P("fsdp", "seq"),
        P("seq", "fsdp"),
    ) + (P(),) * 6 + (both,) * 8
    return jax.shard_map(
        on_device, mesh=mesh, in_specs=placed, out_specs=(both,) * 10, check_vma=False
    )
```

```python
import functools

import jax
import jax.numpy as jnp
import numpy as np
from jax import lax
from jax.experimental import pallas as pl
from jax.experimental.pallas import tpu as pltpu
from jax.sharding import PartitionSpec as P

H = 32
HD = 64
ROT = 32
RANK = 16
ADAPT = 8
BLOCK = 256
EPSILON = 1e-05
ADAPTER_SCALE = 2.0
ROPE_BASE = 10000.0
MASKED = -1e30
F32 = jnp.float32
BF16 = jnp.bfloat16


def dot(a, b, dims=((1,), (0,))):
    return lax.dot_general(a, b, (dims, ((), ())), preferred_element_type=F32)


def dot_nt(a, b):
    return dot(a, b, ((1,), (1,)))


def dot_tn(a, b):
    return dot(a, b, ((0,), (0,)))


def norm_layer(values, scale_gain, offset_bias):
    row_mean = jnp.mean(values, axis=-1, keepdims=True)
    centred = values - row_mean
    spread = jnp.mean(centred * centred, axis=-1, keepdims=True)
    return centred * lax.rsqrt(spread + EPSILON) * scale_gain + offset_bias


def rope_tables(length, heads):
    frequency = ROPE_BASE ** (-2.0 * jnp.arange(ROT // 2, dtype=F32) / ROT)
    angles = jnp.arange(length).astype(F32)[:, None] * frequency[None, :]
    return jnp.cos(angles)[:, None, :], jnp.sin(angles)[:, None, :]


def rotate(values, cos_table, sin_table):
    a = values[..., : ROT // 2]
    b = values[..., ROT // 2 : ROT]
    return jnp.concatenate(
        [a * cos_table - b * sin_table, b * cos_table + a * sin_table, values[..., ROT:]], axis=-1
    )


MESH = pl.DeviceIdType.MESH
TILE = 256
UNIT = 256
PART = 128
ALL = slice(None)


def rope_constants(length):
    frequency = ROPE_BASE ** (-2.0 * np.arange(ROT // 2, dtype=np.float64) / ROT)
    angles = np.arange(length, dtype=np.float64)[:, None] * frequency[None, :]
    cos = np.ones((length, HD))
    sin = np.zeros((length, HD))
    half = ROT // 2
    cos[:, :half] = np.cos(angles)
    cos[:, half:ROT] = np.cos(angles)
    sin[:, :half] = -np.sin(angles)
    sin[:, half:ROT] = np.sin(angles)
    return (
        jnp.asarray(np.tile(cos, (1, 2)), F32),
        jnp.asarray(np.tile(sin, (1, 2)), F32),
    )


def turn(x, cos, sin, sign):
    lane = lax.broadcasted_iota(jnp.int32, x.shape, 1) % HD
    partner = jnp.where(
        lane < ROT // 2,
        pltpu.roll(x, x.shape[1] - ROT // 2, 1),
        pltpu.roll(x, ROT // 2, 1),
    )
    return x * cos + partner * (sin * sign)


def turn_all(x, cos, sin, sign):
    step = cos.shape[1]
    return jnp.concatenate(
        [turn(x[:, i : i + step], cos, sin, sign) for i in range(0, x.shape[1], step)], axis=1
    )


def layer_kernel(
    planes,
    tok_ref,
    cotown_ref,
    wq_in,
    wd_in,
    wi_in,
    wo_in,
    qb_ref,
    db_ref,
    ib_ref,
    ob_ref,
    gain_ref,
    shift_ref,
    index_ref,
    map_refs,
    cos_ref,
    sin_ref,
    out_ref,
    igrad_ref,
    grad_refs,
    stack,
    sel,
    adm,
    downs_ref,
    ups_ref,
    ddown_all,
    qup_all,
    iup_ref,
    odown_ref,
    qgrad,
    a_msg,
    a_h1,
    a_h2,
    b_msg,
    b_h1,
    b_h2,
    q_h1,
    q_h2,
    normed,
    cot,
    wq,
    wd,
    wi,
    wo,
    qkv,
    hg,
    att,
    pg,
    acc_a,
    acc_b,
    pre,
    act,
    ag,
    pgrad,
    coeff,
    cgs,
    coeff_t,
    cgs_t,
    res,
    keep,
    s1_send,
    s1_recv,
    a_send,
    a_recv,
    c_send,
    c_recv,
    ar_send,
    ar_recv,
    ar_low,
    ar_recv_low,
    local_sem,
    zs_sem,
    zr_sem,
    ag_ssem,
    ag_rsem,
    s1_ssem,
    s1_rsem,
    a_ssem,
    a_rsem,
    c_ssem,
    c_rsem,
    ar_ssem,
    ar_rsem,
    adz_ssem,
    adz_rsem,
    h1_ssem,
    h1_rsem,
    h2_ssem,
    h2_rsem,
    q1_ssem,
    q1_rsem,
    q2_ssem,
    q2_rsem,
):
    z = lax.axis_index("fsdp")
    s = lax.axis_index("seq")
    core = s % 2
    chip = s // 2
    to_core = (z, chip * 2 + (1 - core))
    chip_x = chip + 1 - 2 * (chip % 2)
    chip_y = (chip + 2) % 4
    chip_d = chip_x + 2 - 4 * (chip_x // 2)
    to_x = (z, chip_x * 2 + core)
    to_y = (z, chip_y * 2 + core)
    rows, width = tok_ref.shape
    length = normed.shape[0]
    units = act.shape[1]
    fan = width // planes
    mine = wq.shape[3]
    tiles = length // TILE

    def remote(src, dst, ssem, rsem, where):
        return pltpu.make_async_remote_copy(
            src_ref=src, dst_ref=dst, send_sem=ssem, recv_sem=rsem, device_id=where,
            device_id_type=MESH,
        )

    def line(ref, cols):
        return ref[cols].astype(F32)[None, :]

    def block(i, n):
        return pl.ds(pl.multiple_of(i * n, n), n)

    bar = pltpu.get_barrier_semaphore()
    for k in range(1, 8):
        pl.semaphore_signal(bar, inc=1, device_id=(z, (s + k) % 8), device_id_type=MESH)
    for k in range(1, planes):
        pl.semaphore_signal(bar, inc=1, device_id=((z + k) % planes, s), device_id_type=MESH)
    pl.semaphore_wait(bar, 7 + planes - 1)

    chunks = []
    for c in range(3):
        chunks.append((wq_in.at[c], lambda j, c=c: wq.at[j, c]))
    chunks.append((wd_in, lambda j: wd.at[j]))
    part = fan // 4
    for i in range(4):
        chunks.append(
            (
                wi_in.at[pl.ds(i * part, part), :],
                lambda j, i=i: wi.at[j, pl.ds(i * part, part), :],
            )
        )
    for i in range(fan // PART):
        chunks.append(
            (
                wo_in.at[:, pl.ds(i * PART, PART)],
                lambda j, i=i: wo.at[j, :, pl.ds(i * PART, PART)],
            )
        )
    n_chunks = len(chunks)
    ahead = 2
    last_step = n_chunks + planes - 1

    def zcopy(c, direction, k):
        src, place = chunks[c]
        j = z - k if direction == 0 else z + k
        return remote(
            src if k == 0 else place(j),
            place(j),
            zs_sem.at[c, direction, k],
            zr_sem.at[c, j],
            (z + 1, s) if direction == 0 else (z - 1, s),
        )

    def zhas(direction, k):
        if direction == 0:
            return jnp.logical_and(z - k >= 0, z + 1 < planes)
        return jnp.logical_and(z + k < planes, z - 1 >= 0)

    def zsend(c, k):
        for direction in (0, 1):

            @pl.when(zhas(direction, k))
            def _(direction=direction):
                zcopy(c, direction, k).start()

    def zarrived(c, j):
        place = chunks[c][1](j)
        pltpu.make_async_copy(place, place, zr_sem.at[c, j]).wait()

    def zrelay(c, k):
        for direction in (0, 1):

            @pl.when(zhas(direction, k))
            def _(direction=direction):
                zarrived(c, z - k if direction == 0 else z + k)
                zcopy(c, direction, k).start()

    def zfinish(first, last):
        for c in range(first, last):
            for direction in (0, 1):
                for k in range(1, planes):
                    j = z - k if direction == 0 else z + k
                    here = z == planes - 1 if direction == 0 else z == 0

                    @pl.when(here)
                    def _(c=c, j=j):
                        zarrived(c, j)

    def zstep(t):
        if t == 0:
            for c in range(min(ahead, n_chunks - 1) + 1):
                zsend(c, 0)
        elif t + ahead < n_chunks:
            zsend(t + ahead, 0)
        for k in range(1, planes - 1):
            if 0 <= t - k < n_chunks:
                zrelay(t - k, k)

    own = []
    for c in range(n_chunks):
        src, place = chunks[c]
        own.append(pltpu.make_async_copy(src, place(z), local_sem.at[c]))
    zstep(0)
    for copy in own:
        copy.start()

    half = width // 2

    def row_view(buf, b, part):
        if part is None:
            return buf.at[block(b, rows), :]
        return buf.at[block(b, rows), pl.ds(part * half, half)]

    def lead_view(buf, b, part):
        if part is None:
            return buf.at[b]
        return buf.at[b, pl.ds(part * (planes // 2), planes // 2)]

    def gather_copies(p, buf, view):
        bx = chip_x * 2 + core
        by = chip_y * 2 + core
        bd = chip_d * 2 + core
        me = view(buf, s, None)
        blk_x = view(buf, bx, None)
        blk_y = view(buf, by, None)
        blk_d = view(buf, bd, None)
        x0 = view(buf, bx, 0)
        y1 = view(buf, by, 1)
        d0 = view(buf, bd, 0)
        d1 = view(buf, bd, 1)
        ss, rs = ag_ssem.at[p], ag_rsem.at[p]

        def same(ref, i, where):
            return remote(ref, ref, ss.at[i], rs.at[i], where)

        sends = [
            same(me, 0, to_x),
            same(me, 1, to_y),
            same(me, 2, to_core),
            same(x0, 3, to_y),
            same(blk_x, 4, to_core),
            same(y1, 5, to_x),
            same(blk_y, 6, to_core),
            same(blk_d, 7, to_core),
        ]
        other = 1 - core
        into = [
            blk_x,
            blk_y,
            view(buf, chip * 2 + other, None),
            d0,
            view(buf, chip_x * 2 + other, None),
            d1,
            view(buf, chip_y * 2 + other, None),
            view(buf, chip_d * 2 + other, None),
        ]

        def arrived(i):
            pltpu.make_async_copy(into[i], into[i], rs.at[i]).wait()

        return sends, arrived

    cot[block(s, rows), :] = cotown_ref[...]
    c_sends, c_arrived = gather_copies(0, cot, row_view)
    for i in range(3):
        c_sends[i].start()

    counts = [m.shape[0] for m in map_refs]
    spans = [2 * n if n % 128 else n for n in counts]
    bases = [sum(spans[:i]) for i in range(8)]
    stack[...] = jnp.zeros_like(stack)
    odd = s % 2
    for m, n, span, base in zip(map_refs, counts, spans, bases):
        at = base + (odd * n if span != n else 0)
        stack[pl.ds(pl.multiple_of(at, 64), n), :] = m[...]
    lane = lax.broadcasted_iota(jnp.int32, (RANK, ADAPT * RANK), 1)
    column = lax.broadcasted_iota(jnp.int32, (RANK, ADAPT * RANK), 0)
    picks = []
    for g in range(planes):
        picks.append((lane == column + index_ref[g] * RANK).astype(F32).astype(BF16))
        sel[g] = dot_nt(picks[g], stack[...]).astype(BF16)

    def adapter_copy(k):
        g = (z + k) % planes
        return remote(sel.at[g], adm.at[s, z], adz_ssem.at[k - 1], adz_rsem.at[z], (g, s))

    for k in range(1, planes):
        adapter_copy(k).start()
    adm[s, z] = sel[z]

    x = tok_ref[...].astype(F32)
    mean = jnp.mean(x, axis=-1, keepdims=True)
    centred = x - mean
    inv = lax.rsqrt(jnp.mean(centred * centred, axis=-1, keepdims=True) + EPSILON)
    normed[block(s, rows), :] = (
        centred * inv * line(gain_ref, ALL) + line(shift_ref, ALL)
    ).astype(BF16)
    n_sends, n_arrived = gather_copies(1, normed, row_view)
    for k in range(1, planes):
        g = (z + k) % planes
        pltpu.make_async_copy(adm.at[s, g], adm.at[s, g], adz_rsem.at[g]).wait()
    m_sends, m_arrived = gather_copies(2, adm, lead_view)
    gathers = ((c_sends, c_arrived), (n_sends, n_arrived), (m_sends, m_arrived))
    zstep(1)
    for m, (sends, arrived) in enumerate(gathers):
        arrived(0)
        sends[3].start()
        sends[4].start()
        arrived(1)
        sends[5].start()
        sends[6].start()
        if m < 2:
            for i in range(3):
                gathers[m + 1][0][i].start()
            zstep(m + 2)
    zstep(4)
    for m, (sends, arrived) in enumerate(gathers):
        arrived(3)
        arrived(5)
        sends[7].start()
    for sends, arrived in gathers:
        for i in (2, 4, 6, 7):
            arrived(i)
    zstep(5)

    def order(f, carry):
        for pair in range(4):

            def both(i):
                cols = slice(bases[i], bases[i] + spans[i])
                return adm[2 * pair, f, :, cols] + adm[2 * pair + 1, f, :, cols]

            where = block(f * 4 + pair, 128)
            downs_ref[:RANK, where] = both(0)
            downs_ref[RANK:, where] = both(4)
            ups_ref[:RANK, where] = both(3)
            ups_ref[RANK:, where] = both(7)
            ddown_all[:, where] = both(2)
            qup_all[:, block(f * 4 + pair, spans[1])] = both(1)
        return carry

    lax.fori_loop(0, planes, order, 0)
    for j in range(4):
        q = s * 4 + j
        n = counts[5]
        iup_ref[:, j * n : (j + 1) * n] = adm[q % 8, q // 8, :, bases[5] : bases[5] + n]
        odown_ref[:, j * n : (j + 1) * n] = adm[q % 8, q // 8, :, bases[6] : bases[6] + n]

    def qup(c):
        return qup_all[:, pl.ds(pl.multiple_of(c * width + s * mine, mine), mine)]

    def ddown():
        return ddown_all[:, block(s, mine)]

    def low(t, carry):
        r = block(t, TILE)
        c = dot_nt(normed[r, :], downs_ref[...])
        coeff[r, :] = c.astype(BF16)
        g = ADAPTER_SCALE * dot_nt(cot[r, :], ups_ref[...])
        cgs[r, :] = g.astype(BF16)
        return carry

    lax.fori_loop(0, tiles, low, 0)
    for copy in own:
        copy.wait()
    zstep(6)
    zfinish(0, 4)

    def project(t, carry):
        r = block(t, TILE)
        cos = cos_ref[r, :]
        sin = sin_ref[r, :]
        for c in range(3):
            v = ADAPTER_SCALE * dot(coeff[r, :RANK], qup(c))
            v = v + line(qb_ref, pl.ds(pl.multiple_of(c * width + s * mine, mine), mine))
            for j in range(planes):
                v = v + dot(normed[r, j * fan : (j + 1) * fan], wq[j, c])
            if c < 2:
                v = turn_all(v, cos, sin, 1.0)
            v = v.astype(BF16)
            if c == 0:
                v = v * jnp.asarray(HD**-0.5, BF16)
            qkv[c, r, :] = v
        g = dot(cgs[r, :RANK], ddown())
        for j in range(planes):
            g = g + dot_nt(cot[r, j * fan : (j + 1) * fan], wd[j])
        hg[r, :] = g.astype(BF16)
        return carry

    lax.fori_loop(0, tiles, project, 0)
    zstep(7)

    dk = ag.at[:, pl.ds(0, mine)]
    dv = ag.at[:, pl.ds(mine, mine)]
    ag[:, : 2 * mine] = jnp.zeros((length, 2 * mine), F32)
    heads = mine // HD

    for b in range(length // BLOCK):
        lo, hi = b * BLOCK, (b + 1) * BLOCK
        acc_a[...] = jnp.zeros_like(acc_a)
        acc_b[...] = jnp.zeros_like(acc_b)

        def one_head(h, carry, lo=lo, hi=hi):
            lane = lax.broadcasted_iota(jnp.int32, (1, mine), 1)
            mask = (lane // HD == h).astype(BF16)
            mask32 = (lane // HD == h).astype(F32)
            q = qkv[0, lo:hi, :] * mask
            g = hg[lo:hi, :] * mask
            k = qkv[1, :hi, :]
            v = qkv[2, :hi, :]
            sc = dot_nt(q, k)
            e = jnp.exp(sc - jnp.max(sc, axis=-1, keepdims=True))
            p = e * (1.0 / jnp.sum(e, axis=-1, keepdims=True))
            pb = p.astype(BF16)
            acc_a[...] += dot(pb, v) * mask32
            dp = dot_nt(g, v)
            ds = (p * (dp - jnp.sum(dp * p, axis=-1, keepdims=True))).astype(BF16)
            acc_b[...] += dot(ds, k) * mask32
            dk[:hi, :] += dot_tn(ds, q)
            dv[:hi, :] += dot_tn(pb, g)
            return carry

        lax.fori_loop(0, heads, one_head, 0)
        att[lo:hi, :] = acc_a[...].astype(BF16)
        back = (acc_b[...] * (HD**-0.5)).astype(BF16).astype(F32)
        pg[0, lo:hi, :] = turn_all(back, cos_ref[lo:hi, :], sin_ref[lo:hi, :], -1.0).astype(BF16)
        if b == 1:
            zstep(8)
        if b == 2:
            zstep(9)
        if b == 3:
            zstep(10)

    def finish(t, carry):
        r = block(t, TILE)
        back = dk[r, :].astype(BF16).astype(F32)
        pg[1, r, :] = turn_all(back, cos_ref[r, :], sin_ref[r, :], -1.0).astype(BF16)
        pg[2, r, :] = dv[r, :].astype(BF16)
        return carry

    lax.fori_loop(0, tiles, finish, 0)

    coeff_t[...] = dot_nt(downs_ref[...], normed[...]).astype(BF16)
    cgs_t[...] = (ADAPTER_SCALE * dot_nt(ups_ref[...], cot[...])).astype(BF16)

    share = width // 8

    def wait_on(ref, sem):
        pltpu.make_async_copy(ref, ref, sem).wait()

    def hop1(w, msg, h1, start):
        for j in range(4):
            to = 4 * (s % 2) + j
            there = (z, to)

            @pl.when(to != s)
            def _(j=j, there=there):
                copy = remote(
                    msg.at[j], h1.at[s // 2], h1_ssem.at[w, j], h1_rsem.at[w, s // 2], there
                )
                if start:
                    copy.start()
                else:
                    copy.wait_send()

            if start:

                @pl.when(to == s)
                def _(j=j):
                    pltpu.make_async_copy(
                        msg.at[j], h1.at[s // 2], h1_rsem.at[w, s // 2]
                    ).start()

    def hop2_copy(w, h1, h2, k):
        g = (z + k) % planes
        return remote(h1.at[g], h2.at[z], h2_ssem.at[w, k - 1], h2_rsem.at[w, z], (g, s))

    def hop2(w, h1, h2):
        for g in range(planes):
            wait_on(h1.at[g], h1_rsem.at[w, g])
        for k in range(1, planes):
            hop2_copy(w, h1, h2, k).start()
        h2[z] = h1[z]

    def landed(w, h1, h2):
        for k in range(1, planes):
            g = (z + k) % planes
            wait_on(h2.at[g], h2_rsem.at[w, g])
        for k in range(1, planes):
            hop2_copy(w, h1, h2, k).wait_send()

    pick_all = jnp.concatenate(picks, axis=0)

    def spread(h2):
        return dot_tn(h2.reshape(planes * RANK, h2.shape[-1]), pick_all)

    def half_rows(v):
        return jnp.where(s % 2 == 0, v[:64], v[64:])

    for c in range(3):
        g = ADAPTER_SCALE * dot(coeff_t[:RANK, :], pg[c])
        for i in range(2):
            qgrad[2 * c + i] = g[:, i * 128 : (i + 1) * 128].astype(BF16)

    def qkv_hop1(start):
        for c in range(3):
            for i in range(2):
                t = 16 * c + 2 * s + i
                for o in range(2):
                    owner = 2 * (t // 3) + o
                    slot = t % 3 - o
                    ok = jnp.logical_and(slot >= 0, slot <= 1)
                    to = owner % 8
                    src = qgrad.at[2 * c + i]
                    n = 4 * c + 2 * i + o

                    @pl.when(jnp.logical_and(ok, to != s))
                    def _(src=src, owner=owner, slot=slot, to=to, n=n):
                        copy = remote(
                            src, q_h1.at[owner // 8, slot], q1_ssem.at[n],
                            q1_rsem.at[owner // 8, slot], (z, to),
                        )
                        if start:
                            copy.start()
                        else:
                            copy.wait_send()

                    if start:

                        @pl.when(jnp.logical_and(ok, to == s))
                        def _(src=src, owner=owner, slot=slot):
                            pltpu.make_async_copy(
                                src, q_h1.at[owner // 8, slot], q1_rsem.at[owner // 8, slot]
                            ).start()

    def qkv_hop2_copy(k):
        g = (z + k) % planes
        return remote(q_h1.at[g], q_h2.at[z], q2_ssem.at[k - 1], q2_rsem.at[z], (g, s))

    def qkv_hop2():
        for g in range(planes):
            for slot in range(2):
                wait_on(q_h1.at[g, slot], q1_rsem.at[g, slot])
        for k in range(1, planes):
            qkv_hop2_copy(k).start()
        q_h2[z] = q_h1[z]

    def qkv_landed():
        for k in range(1, planes):
            g = (z + k) % planes
            wait_on(q_h2.at[g], q2_rsem.at[g])
        for k in range(1, planes):
            qkv_hop2_copy(k).wait_send()

    qkv_hop1(True)
    g = dot(cgs_t[:RANK, :], att[...])
    for j in range(4):
        a_msg[j, :, 256:384] = g[:, (j // 2) * 128 : (j // 2 + 1) * 128].astype(BF16)
    pass
    zfinish(4, 8)
    zstep(11)

    k0 = 0.7978845608028654
    k1 = 0.044715

    def inner(t, carry):
        r = block(t, TILE)
        v = ADAPTER_SCALE * dot(coeff[r, RANK : 2 * RANK], iup_ref[...])
        v = v + line(ib_ref, block(s, units))
        for j in range(planes):
            v = v + dot(normed[r, j * fan : (j + 1) * fan], wi[j])
        sq = v * v
        th = jnp.tanh(k0 * v * (1.0 + k1 * sq))
        act[r, :] = (0.5 * v * (1.0 + th)).astype(BF16)
        pre[r, :] = 0.5 * (1.0 + th) + 0.5 * v * (1.0 - th * th) * (k0 * (1.0 + 3.0 * k1 * sq))
        return carry

    lax.fori_loop(0, tiles, inner, 0)
    for k in range(1, planes):
        adapter_copy(k).wait_send()
    for sends, _ in gathers:
        for copy in sends:
            copy.wait_send()
    spot = (8, planes, RANK, share)
    for i in range(length // (8 * planes * RANK)):
        span = 8 * planes * RANK
        adm[:, :, :, i * share : (i + 1) * share] = normed[
            i * span : (i + 1) * span, block(s, share)
        ].reshape(spot)
    g = dot(cgs_t[RANK : 2 * RANK, :], act[...])
    for j in range(4):
        a_msg[j, :, :256] = g[:, j * 256 : (j + 1) * 256].astype(BF16)
    qkv_hop2()
    zstep(12)

    partners = (to_core, to_x, to_y)

    def reduce_copy(w, i):
        src = ar_send.at[0] if w == 0 else ar_low
        dst = ar_recv.at[i] if w == 0 else ar_recv_low.at[i]
        return remote(src, dst, ar_ssem.at[w, i], ar_rsem.at[w, i], partners[i])

    def reduce_round(w, i):
        if i > 0:
            reduce_copy(w, i - 1).wait()
            got = ar_recv[i - 1] if w == 0 else ar_recv_low[i - 1].astype(F32)
            ar_send[w] += got
        if i < 3:
            if w == 1:
                ar_low[...] = ar_send[1].astype(BF16)
            reduce_copy(w, i).start()

    ar_send[0, :RANK, :] = dot_nt(ddown(), att[...])
    ar_send[0, RANK : 2 * RANK, :] = dot_nt(odown_ref[...], act[...])
    for i in range(4):
        reduce_round(0, i)
        pass
    coeff_dense = ar_send[0].astype(BF16)
    for i in range(2):
        g = ADAPTER_SCALE * dot(
            coeff_dense[i * RANK : (i + 1) * RANK, :], cot[:, block(s, share)]
        )
        for j in range(4):
            at = 384 + i * 128
            a_msg[j, :, at : at + 128] = g[:, (j // 2) * 128 : (j // 2 + 1) * 128].astype(BF16)
    hop1(0, a_msg, a_h1, True)

    p_units = width // UNIT
    per = fan // UNIT
    early = p_units - planes // 2
    total = 2 * p_units

    def branch_place(n):
        return (n % (planes // 2)) * 2, n // (planes // 2)

    def back_place(n):
        return (n - p_units) // per, (n - p_units) % per

    def keep_split(n, k, r):
        slot = n % 2
        a = r[:rows, :]
        b = r[rows:, :]
        first = core == 0
        keep[n % 6, k] = jnp.where(first, a, b)
        s1_send[slot, k] = jnp.where(first, b, a).astype(BF16)

    def keep_pair(n, k, v):
        keep_split(n, 2 * k, v[:TILE])
        keep_split(n, 2 * k + 1, v[TILE:])

    def s1_copy(n):
        return remote(s1_send.at[n % 2], s1_recv.at[n], s1_ssem.at[n % 2], s1_rsem.at[n], to_core)

    def a_copy(n, i):
        return remote(
            a_send.at[n % 3, i], a_recv.at[n, i], a_ssem.at[n % 3, i], a_rsem.at[n, i],
            (to_x, to_y)[i],
        )

    def c_copy(n, i):
        return remote(
            c_send.at[n % 3, i], c_recv.at[n, i], c_ssem.at[n % 3, i], c_rsem.at[n, i],
            (to_x, to_y)[i],
        )

    hu = UNIT // 2

    def stage0_branch(n):
        j, i = branch_place(n)

        def tile(k, carry):
            r = block(k, 2 * TILE)
            cols = block(i, PART)
            w_o = jnp.concatenate([wo[j, :, cols], wo[j + 1, :, cols]], axis=1)
            w_d = jnp.concatenate([wd[j, :, cols], wd[j + 1, :, cols]], axis=1)
            keep_pair(n, k, dot(act[r, :], w_o) + dot(att[r, :], w_d))
            return carry

        lax.fori_loop(0, tiles // 2, tile, 0)
        s1_copy(n).start()

    def stage0_back(n):
        j, i = back_place(n)

        def tile(k, carry):
            r = block(k, 2 * TILE)
            rws = block(i, UNIT)
            v = dot_nt(pgrad[r, :], wi[j, rws, :])
            v = v + normed[r, block(n - p_units, UNIT)].astype(F32)
            keep_pair(n, k, v)
            return carry

        lax.fori_loop(0, tiles // 2, tile, 0)
        s1_copy(n).start()

    def stage1(n):
        s1_copy(n).wait()
        q = n % 6
        for k in range(4):
            keep[q, k] += s1_recv[n, k].astype(F32)
        far = keep[q, chip_d]
        a_send[n % 3, 0] = far[:, :hu].astype(BF16)
        a_send[n % 3, 1] = far[:, hu:].astype(BF16)
        for i in range(2):
            a_copy(n, i).start()

    def stage2(n):
        q = n % 6
        for i in range(2):
            a_copy(n, i).wait()
        keep[q, chip_y, :, :hu] += a_recv[n, 0].astype(F32)
        keep[q, chip_x, :, hu:] += a_recv[n, 1].astype(F32)
        c_send[n % 3, 0] = keep[q, chip_x].astype(BF16)
        c_send[n % 3, 1] = keep[q, chip_y].astype(BF16)
        for i in range(2):
            c_copy(n, i).start()

    def stage3(n):
        q = n % 6
        for i in range(2):
            c_copy(n, i).wait()
        v = keep[q, chip] + c_recv[n, 0].astype(F32) + c_recv[n, 1].astype(F32)

        @pl.when(n < p_units)
        def _():
            j, i = branch_place(n)
            for m in range(2):
                res[:, pl.ds(pl.multiple_of((j + m) * fan + i * PART, PART), PART)] = v[
                    :, m * PART : (m + 1) * PART
                ]

        @pl.when(n >= p_units)
        def _():
            igrad_ref[:, block(n - p_units, UNIT)] = v

    def pipeline(first, lo, hi, stage0, extra=None, units_end=None):
        def body(n, carry):
            if stage0 is not None:
                stage0(n)
            for back, stage in ((1, stage1), (3, stage2), (5, stage3)):
                m = n - back
                ok = m >= first
                if stage0 is None:
                    ok = jnp.logical_and(ok, m < units_end)

                @pl.when(ok)
                def _(m=m, stage=stage):
                    stage(m)

            if extra is not None:
                extra(n)
            return carry

        lax.fori_loop(lo, hi, body, 0)

    zstep(13)
    def act_part(r, i):
        cols = [slice(j * fan + i * PART, j * fan + (i + 1) * PART) for j in range(planes)]
        g = jnp.concatenate([cot[r, c] for c in cols], axis=1)
        w = [wo[j, :, i * PART : (i + 1) * PART] for j in range(planes)]
        return dot_nt(g, jnp.concatenate(w, axis=1))

    def attention_back(u, carry):
        j = u // per
        rws = block(u % per, UNIT)
        for h in range(2):
            r = slice(h * length // 2, (h + 1) * length // 2)
            v = dot_nt(pg[0, r, :], wq[j, 0, rws, :])
            for c in range(1, 3):
                v = v + dot_nt(pg[c, r, :], wq[j, c, rws, :])
            normed[r, block(u, UNIT)] = v.astype(BF16)
        return carry

    lax.fori_loop(0, p_units, attention_back, 0)

    per_part = planes // 2
    for i in range(fan // PART - 1):
        zfinish(8 + i, 9 + i)
        pipeline(0, i * per_part, (i + 1) * per_part, stage0_branch)

        def act_back(t, carry, i=i):
            r = block(t, TILE)
            if i == 1:
                v = dot(cgs[r, RANK : 2 * RANK], odown_ref[...]) + act_part(r, 0)
                ag[r, :] = v + act_part(r, 1)
            else:
                ag[r, :] += act_part(r, i)
            return carry

        if i > 0:
            lax.fori_loop(0, tiles, act_back, 0)
        if i == 1:
            hop2(0, a_h1, a_h2)
    zfinish(11, 12)

    pipeline(0, early, p_units, stage0_branch)

    def act_last(t, carry):
        r = block(t, TILE)
        v = ag[r, :] + act_part(r, fan // PART - 1)
        pgrad[r, :] = (v * pre[r, :]).astype(BF16)
        return carry

    lax.fori_loop(0, tiles, act_last, 0)

    def rounds(n):
        @pl.when(n == p_units)
        def _():
            up_part = dot_nt(iup_ref[...], pgrad[...])
            q_part = dot_nt(qup(0), pg[0])
            for c in range(1, 3):
                q_part = q_part + dot_nt(qup(c), pg[c])
            ar_send[1, :RANK, :] = ADAPTER_SCALE * q_part
            ar_send[1, RANK : 2 * RANK, :] = ADAPTER_SCALE * up_part
            reduce_round(1, 0)

        @pl.when(n == p_units + 1)
        def _():
            qkv_landed()
            full = [spread(q_h2[:, i]) for i in range(2)]
            full = jnp.concatenate(full, axis=0)
            grad_refs[1][...] = jnp.where(s % 2 == 0, full[:192], full[64:])

        @pl.when(n == p_units + 3)
        def _():
            landed(0, a_h1, a_h2)
            full = spread(a_h2[...])
            grad_refs[6][...] = full[:256]
            grad_refs[2][...] = half_rows(full[256:384])
            grad_refs[3][...] = half_rows(full[384:512])
            grad_refs[7][...] = half_rows(full[512:640])


        for i in range(1, 4):

            @pl.when(n == p_units + (1, 3, 5)[i - 1])
            def _(i=i):
                reduce_round(1, i)
                if i == 2:
                    g = ADAPTER_SCALE * dot(coeff_t[RANK : 2 * RANK, :], pgrad[...])
                    for j in range(4):
                        b_msg[j, :, :256] = g[:, j * 256 : (j + 1) * 256].astype(BF16)
                if i == 3:
                    g = None
                    span = 8 * planes * RANK
                    for m in range(length // span):
                        part = dot(
                            ar_send[1, :, m * span : (m + 1) * span].astype(BF16),
                            adm[:, :, :, m * share : (m + 1) * share].reshape(span, share),
                        )
                        g = part if g is None else g + part
                    for m in range(2):
                        for j in range(4):
                            b_msg[j, :, 256 + m * 128 : 384 + m * 128] = g[
                                m * RANK : (m + 1) * RANK, (j // 2) * 128 : (j // 2 + 1) * 128
                            ].astype(BF16)
                    hop1(1, b_msg, b_h1, True)

    pipeline(0, p_units, total, stage0_back, rounds)
    pipeline(0, total, total + 3, None, None, total)
    hop2(1, b_h1, b_h2)
    pipeline(0, total + 3, total + 5, None, None, total)

    first_t = ar_send[0, :, block(s, rows)].astype(BF16)
    late_t = ar_send[1, :, block(s, rows)].astype(BF16)
    out = tok_ref[...].astype(F32) + res[...] + ADAPTER_SCALE * dot_tn(first_t, ups_ref[...])
    out_ref[...] = (out + line(db_ref, ALL) + line(ob_ref, ALL)).astype(BF16)
    x = tok_ref[...].astype(F32)
    mean = jnp.mean(x, axis=-1, keepdims=True)
    centred = x - mean
    inv = lax.rsqrt(jnp.mean(centred * centred, axis=-1, keepdims=True) + EPSILON)
    xhat = centred * inv
    e = (igrad_ref[...] + dot_tn(late_t, downs_ref[...])) * line(gain_ref, ALL)
    igrad_ref[...] = cotown_ref[...].astype(F32) + inv * (
        e
        - jnp.mean(e, axis=-1, keepdims=True)
        - xhat * jnp.mean(e * xhat, axis=-1, keepdims=True)
    )

    landed(1, b_h1, b_h2)
    full = spread(b_h2[...])
    grad_refs[5][...] = full[:256]
    grad_refs[0][...] = half_rows(full[256:384])
    grad_refs[4][...] = half_rows(full[384:512])

    hop1(0, a_msg, a_h1, False)
    hop1(1, b_msg, b_h1, False)
    qkv_hop1(False)
    for c in range(n_chunks):
        for k in range(planes - 1):
            for direction in (0, 1):

                @pl.when(zhas(direction, k))
                def _(c=c, k=k, direction=direction):
                    zcopy(c, direction, k).wait_send()


def run_layer(planes, args, shapes):
    rows, width, length, units, mine = shapes
    fan = width // planes
    vm = pl.BlockSpec(memory_space=pltpu.VMEM)
    hbm = pl.BlockSpec(memory_space=pl.ANY)
    n_chunks = 8 + fan // PART
    total = 2 * width // UNIT
    dma = pltpu.SemaphoreType.DMA
    maps = args[13:21]
    lanes = sum(2 * m.shape[0] if m.shape[0] % 128 else m.shape[0] for m in maps)

    def entry(*refs):
        layer_kernel(planes, *refs[:13], refs[13:21], *refs[21:25], refs[25:33], *refs[33:])

    outs = pl.pallas_call(
        entry,
        out_shape=(
            jax.ShapeDtypeStruct((rows, width), BF16),
            jax.ShapeDtypeStruct((rows, width), F32),
            *(jax.ShapeDtypeStruct(m.shape, F32) for m in maps),
        ),
        in_specs=[vm, vm, hbm, hbm, hbm, hbm]
        + [vm] * 6
        + [pl.BlockSpec(memory_space=pltpu.SMEM)]
        + [vm] * 10,
        out_specs=(vm,) * 10,
        scratch_shapes=[
            pltpu.VMEM((lanes, ADAPT * RANK), BF16),
            pltpu.VMEM((planes, RANK, lanes), BF16),
            pltpu.VMEM((8, planes, RANK, lanes), BF16),
            pltpu.VMEM((2 * RANK, width), BF16),
            pltpu.VMEM((2 * RANK, width), BF16),
            pltpu.VMEM((RANK, width), BF16),
            pltpu.VMEM((RANK, 3 * width), BF16),
            pltpu.VMEM((RANK, units), BF16),
            pltpu.VMEM((RANK, units), BF16),
            pltpu.VMEM((6, RANK, 128), BF16),
            pltpu.VMEM((4, RANK, 640), BF16),
            pltpu.VMEM((planes, RANK, 640), BF16),
            pltpu.VMEM((planes, RANK, 640), BF16),
            pltpu.VMEM((4, RANK, 512), BF16),
            pltpu.VMEM((planes, RANK, 512), BF16),
            pltpu.VMEM((planes, RANK, 512), BF16),
            pltpu.VMEM((planes, 2, RANK, 128), BF16),
            pltpu.VMEM((planes, 2, RANK, 128), BF16),
            pltpu.VMEM((length, width), BF16),
            pltpu.VMEM((length, width), BF16),
            pltpu.VMEM((planes, 3, fan, mine), BF16),
            pltpu.VMEM((planes, mine, fan), BF16),
            pltpu.VMEM((planes, fan, units), BF16),
            pltpu.VMEM((planes, units, fan), BF16),
            pltpu.VMEM((3, length, mine), BF16),
            pltpu.VMEM((length, mine), BF16),
            pltpu.VMEM((length, mine), BF16),
            pltpu.VMEM((3, length, mine), BF16),
            pltpu.VMEM((BLOCK, mine), F32),
            pltpu.VMEM((BLOCK, mine), F32),
            pltpu.VMEM((length, units), F32),
            pltpu.VMEM((length, units), BF16),
            pltpu.VMEM((length, units), F32),
            pltpu.VMEM((length, units), BF16),
            pltpu.VMEM((length, 2 * RANK), BF16),
            pltpu.VMEM((length, 2 * RANK), BF16),
            pltpu.VMEM((2 * RANK, length), BF16),
            pltpu.VMEM((2 * RANK, length), BF16),
            pltpu.VMEM((rows, width), F32),
            pltpu.VMEM((6, 4, rows, UNIT), F32),
            pltpu.VMEM((2, 4, rows, UNIT), BF16),
            pltpu.VMEM((total, 4, rows, UNIT), BF16),
            pltpu.VMEM((3, 2, rows, UNIT // 2), BF16),
            pltpu.VMEM((total, 2, rows, UNIT // 2), BF16),
            pltpu.VMEM((3, 2, rows, UNIT), BF16),
            pltpu.VMEM((total, 2, rows, UNIT), BF16),
            pltpu.VMEM((2, 2 * RANK, length), F32),
            pltpu.VMEM((3, 2 * RANK, length), F32),
            pltpu.VMEM((2 * RANK, length), BF16),
            pltpu.VMEM((3, 2 * RANK, length), BF16),
            dma((n_chunks,)),
            dma((n_chunks, 2, planes)),
            dma((n_chunks, planes)),
            dma((3, 8)),
            dma((3, 8)),
            dma((2,)),
            dma((total,)),
            dma((3, 2)),
            dma((total, 2)),
            dma((3, 2)),
            dma((total, 2)),
            dma((2, 3)),
            dma((2, 3)),
            dma((planes,)),
            dma((planes,)),
            dma((2, 4)),
            dma((2, planes)),
            dma((2, planes)),
            dma((2, planes)),
            dma((12,)),
            dma((planes, 2)),
            dma((planes,)),
            dma((planes,)),
        ],
        compiler_params=pltpu.CompilerParams(
            collective_id=0, has_side_effects=True, vmem_limit_bytes=63 * 1024 * 1024
        ),
    )(*args)
    return pl.pallas_call(
        hand_over,
        out_shape=tuple(jax.ShapeDtypeStruct(o.shape, o.dtype) for o in outs),
        in_specs=[vm] * 10,
        out_specs=(vm,) * 10,
    )(*outs)


def hand_over(*refs):
    for i in range(10):
        refs[10 + i][...] = refs[i][...]


def fits(planes, groups, shapes):
    rows, width, length, units, mine = shapes
    return (
        groups == 8
        and planes == 4
        and rows * 2 == TILE
        and length <= 1024
        and width == 2048
        and mine == 256
        and units == 1024
    )


def deliver(packed, sizes, counts, pick, planes, groups):
    s = lax.axis_index("seq")
    everyone = lax.all_gather(packed, "seq", axis=0, tiled=False)
    owned = []
    at = 0
    for i, (n, w) in enumerate(zip(counts, sizes)):
        part = everyone[:, :, at : at + w]
        at += w
        blocks = 3 if i == 1 else 1
        part = part.reshape(groups, RANK, blocks, w // blocks).transpose(1, 2, 0, 3)
        part = part.reshape(RANK, planes, groups, n)
        owned.append(lax.dynamic_index_in_dim(part, s, 2, keepdims=False))
    owned = jnp.concatenate(owned, axis=2).transpose(1, 0, 2)
    arrived = lax.all_to_all(owned, "fsdp", split_axis=0, concat_axis=0, tiled=True)
    place = pick.astype(F32).reshape(planes * RANK, ADAPT * RANK)
    spread = lax.dot_general(
        arrived.reshape(planes * RANK, -1),
        place,
        (((0,), (0,)), ((), ())),
        precision=lax.Precision.HIGHEST,
        preferred_element_type=F32,
    )
    outs = []
    at = 0
    for n in counts:
        outs.append(spread[at : at + n])
        at += n
    return outs


def on_device(
    tokens,
    cotangent,
    adapter_index,
    qkv_weight,
    dense_weight,
    inner_weight,
    outer_weight,
    qkv_bias,
    dense_bias,
    inner_bias,
    outer_bias,
    norm_gain,
    norm_bias,
    *maps,
):
    planes = lax.axis_size("fsdp")
    groups = lax.axis_size("seq")
    rows, width = tokens.shape
    length = rows * groups
    heads = H // groups
    mine = heads * HD
    units = inner_weight.shape[1]
    s = lax.axis_index("seq")

    shapes = (rows, width, length, units, mine)
    if fits(planes, groups, shapes):
        return run_layer(
            planes,
            (
                tokens,
                cotangent,
                qkv_weight,
                dense_weight,
                inner_weight,
                outer_weight,
                qkv_bias,
                dense_bias,
                inner_bias,
                outer_bias,
                norm_gain,
                norm_bias,
                adapter_index,
                *maps,
                *rope_constants(length),
            ),
            shapes,
        )

    counts = [m.shape[0] for m in maps]
    stacked = jnp.concatenate(maps, axis=0)
    wanted = (adapter_index[:, None] * RANK + jnp.arange(RANK)[None, :]).reshape(-1)
    pick = (wanted[:, None] == jnp.arange(ADAPT * RANK)[None, :]).astype(BF16)
    chosen = dot_nt(pick, stacked).astype(BF16).reshape(planes, RANK, -1)
    chosen = lax.all_to_all(chosen, "fsdp", split_axis=0, concat_axis=0, tiled=True)
    chosen = lax.all_gather(chosen, "seq", axis=1, tiled=False)
    full = []
    at = 0
    for n in counts:
        part = chosen[:, :, :, at : at + n]
        full.append(part.transpose(2, 0, 1, 3).reshape(RANK, -1))
        at += n
    qkv_down, qkv_up, dense_down, dense_up, inner_down, inner_up, outer_down, outer_up = full

    def own(m, n):
        return lax.dynamic_slice_in_dim(m, s * n, n, axis=1)

    qkv_up = jnp.concatenate(
        [own(qkv_up[:, c * width : (c + 1) * width], mine) for c in range(3)], axis=1
    )
    dense_down = own(dense_down, mine)
    inner_up = own(inner_up, units)
    outer_down = own(outer_down, units)

    wqkv = lax.all_gather(qkv_weight, "fsdp", axis=1, tiled=True)
    wdense = lax.all_gather(dense_weight, "fsdp", axis=1, tiled=True)
    winner = lax.all_gather(inner_weight, "fsdp", axis=0, tiled=True)
    wouter = lax.all_gather(outer_weight, "fsdp", axis=1, tiled=True)

    gain = norm_gain.astype(F32)
    shift = norm_bias.astype(F32)
    source = tokens.astype(F32)
    normed_own = norm_layer(source, gain, shift).astype(BF16)
    normed = lax.all_gather(normed_own, "seq", axis=0, tiled=True)
    cot = lax.all_gather(cotangent, "seq", axis=0, tiled=True)

    coeffs = dot_nt(normed, jnp.concatenate([qkv_down, inner_down], axis=0)).astype(BF16)
    qkv_coeff, inner_coeff = coeffs[:, :RANK], coeffs[:, RANK:]
    cgs = (
        ADAPTER_SCALE * dot_nt(cot, jnp.concatenate([dense_up, outer_up], axis=0))
    ).astype(BF16)
    dense_cg, outer_cg = cgs[:, :RANK], cgs[:, RANK:]

    bias = jnp.stack([own(qkv_bias.reshape(3, width)[c : c + 1], mine)[0] for c in range(3)])
    projected = (
        jnp.concatenate([dot(normed, wqkv[c]) for c in range(3)], axis=1)
        + bias.reshape(-1).astype(F32)
        + ADAPTER_SCALE * dot(qkv_coeff, qkv_up)
    ).reshape(length, 3, heads, HD)
    cos_table, sin_table = rope_tables(length, heads)
    query = rotate(projected[:, 0], cos_table, sin_table).astype(BF16).transpose(1, 0, 2)
    key = rotate(projected[:, 1], cos_table, sin_table).astype(BF16).transpose(1, 0, 2)
    value = projected[:, 2].astype(BF16).transpose(1, 0, 2)
    attended_grad = (dot_nt(cot, wdense) + dot(dense_cg, dense_down)).astype(BF16)
    head_grad = attended_grad.reshape(length, heads, HD).transpose(1, 0, 2)

    scale = HD ** (-0.5)

    def bmm(spec, a, b):
        return jnp.einsum(spec, a, b, preferred_element_type=F32)

    key_grad = jnp.zeros((heads, length, HD), F32)
    value_grad = jnp.zeros((heads, length, HD), F32)
    attended_parts = []
    query_parts = []
    for b in range(length // BLOCK):
        lo, hi = b * BLOCK, (b + 1) * BLOCK
        q = query[:, lo:hi]
        k = key[:, :hi]
        v = value[:, :hi]
        g = head_grad[:, lo:hi]
        scores = bmm("hqd,hkd->hqk", q, k) * scale
        row_max = jnp.max(scores, axis=-1, keepdims=True)
        exponent = jnp.exp(scores - row_max)
        prob = exponent / jnp.sum(exponent, axis=-1, keepdims=True)
        prob_low = prob.astype(BF16)
        attended_parts.append(bmm("hqk,hkd->hqd", prob_low, v).astype(BF16))
        prob_grad = bmm("hqd,hkd->hqk", g, v)
        row_dot = jnp.sum(prob_grad * prob, axis=-1, keepdims=True)
        score_grad = (prob * (prob_grad - row_dot)).astype(BF16)
        query_parts.append((bmm("hqk,hkd->hqd", score_grad, k) * scale).astype(BF16))
        key_grad = key_grad.at[:, :hi].add(bmm("hqk,hqd->hkd", score_grad, q) * scale)
        value_grad = value_grad.at[:, :hi].add(bmm("hqk,hqd->hkd", prob_low, g))

    def rows_first(x):
        return x.transpose(1, 0, 2)

    attended = rows_first(jnp.concatenate(attended_parts, axis=1)).reshape(length, mine)
    query_grad = rows_first(jnp.concatenate(query_parts, axis=1)).astype(F32)
    key_back = rows_first(key_grad.astype(BF16)).astype(F32)
    value_back = rows_first(value_grad.astype(BF16)).reshape(length, mine)
    projected_grad = jnp.concatenate(
        [
            rotate(query_grad, cos_table, -sin_table).astype(BF16).reshape(length, mine),
            rotate(key_back, cos_table, -sin_table).astype(BF16).reshape(length, mine),
            value_back,
        ],
        axis=1,
    )

    pre_act = (
        dot(normed, winner)
        + own(inner_bias[None], units).astype(F32)
        + ADAPTER_SCALE * dot(inner_coeff, inner_up)
    )
    act32, gelu_back = jax.vjp(lambda v: jax.nn.gelu(v, approximate=True), pre_act)
    activated = act32.astype(BF16)
    act_grad = dot_nt(cot, wouter) + dot(outer_cg, outer_down)
    pre_grad = gelu_back(act_grad)[0].astype(BF16)

    def scatter(x):
        return lax.psum_scatter(x, "seq", scatter_dimension=0, tiled=True)

    branch = scatter((dot(attended, wdense) + dot(activated, wouter)))
    coeff_sum = scatter(
        jnp.concatenate([dot_nt(attended, dense_down), dot_nt(activated, outer_down)], axis=1)
    )
    back = dot_nt(pre_grad, winner)
    for c in range(3):
        back = back + dot_nt(projected_grad[:, c * mine : (c + 1) * mine], wqkv[c])
    back = scatter(back)
    cg_sum = scatter(
        ADAPTER_SCALE
        * jnp.concatenate([dot_nt(projected_grad, qkv_up), dot_nt(pre_grad, inner_up)], axis=1)
    )
    late_own = jnp.concatenate([coeff_sum, cg_sum], axis=1).astype(BF16)
    late = lax.all_gather(late_own, "seq", axis=0, tiled=True)

    layer_out = (
        source
        + branch
        + dense_bias.astype(F32)
        + outer_bias.astype(F32)
        + ADAPTER_SCALE
        * dot(late_own[:, : 2 * RANK], jnp.concatenate([dense_up, outer_up], axis=0))
    ).astype(BF16)
    normed_grad = back + dot(
        late_own[:, 2 * RANK :], jnp.concatenate([qkv_down, inner_down], axis=0)
    )
    row_mean = jnp.mean(source, axis=-1, keepdims=True)
    centred = source - row_mean
    inv = lax.rsqrt(jnp.mean(centred * centred, axis=-1, keepdims=True) + EPSILON)
    xhat = centred * inv
    e = normed_grad * gain
    input_grad = cotangent.astype(F32) + inv * (
        e
        - jnp.mean(e, axis=-1, keepdims=True)
        - xhat * jnp.mean(e * xhat, axis=-1, keepdims=True)
    )

    share = width // groups
    cot_mine = own(cot, share)
    normed_mine = own(normed, share)
    qkv_up_g = ADAPTER_SCALE * dot_tn(qkv_coeff, projected_grad)
    inner_up_g = ADAPTER_SCALE * dot_tn(inner_coeff, pre_grad)
    dense_down_g = dot_tn(dense_cg, attended)
    outer_down_g = dot_tn(outer_cg, activated)
    ups = ADAPTER_SCALE * dot_tn(late[:, : 2 * RANK], cot_mine)
    downs = dot_tn(late[:, 2 * RANK :], normed_mine)
    mine_grads = [
        downs[:RANK],
        qkv_up_g,
        dense_down_g,
        ups[:RANK],
        downs[RANK:],
        inner_up_g,
        outer_down_g,
        ups[RANK:],
    ]
    packed = jnp.concatenate(mine_grads, axis=1)
    sizes = [g.shape[1] for g in mine_grads]
    outs = deliver(packed, sizes, counts, pick, planes, groups)
    return (layer_out, input_grad, *outs)


def solution(mesh):
    both = P(("fsdp", "seq"), None)
    placed = (
        both,
        both,
        P(),
        P(None, "fsdp", "seq"),
        P("seq", "fsdp"),
        P("fsdp", "seq"),
        P("seq", "fsdp"),
    ) + (P(),) * 6 + (both,) * 8
    return jax.shard_map(
        on_device, mesh=mesh, in_specs=placed, out_specs=(both,) * 10, check_vma=False
    )
```

```python
import functools

import jax
import jax.numpy as jnp
import numpy as np
from jax import lax
from jax.experimental import pallas as pl
from jax.experimental.pallas import tpu as pltpu
from jax.sharding import PartitionSpec as P

H = 32
HD = 64
ROT = 32
RANK = 16
ADAPT = 8
BLOCK = 256
EPSILON = 1e-05
ADAPTER_SCALE = 2.0
ROPE_BASE = 10000.0
MASKED = -1e30
F32 = jnp.float32
BF16 = jnp.bfloat16


def dot(a, b, dims=((1,), (0,))):
    return lax.dot_general(a, b, (dims, ((), ())), preferred_element_type=F32)


def dot_nt(a, b):
    return dot(a, b, ((1,), (1,)))


def dot_tn(a, b):
    return dot(a, b, ((0,), (0,)))


def norm_layer(values, scale_gain, offset_bias):
    row_mean = jnp.mean(values, axis=-1, keepdims=True)
    centred = values - row_mean
    spread = jnp.mean(centred * centred, axis=-1, keepdims=True)
    return centred * lax.rsqrt(spread + EPSILON) * scale_gain + offset_bias


def rope_tables(length, heads):
    frequency = ROPE_BASE ** (-2.0 * jnp.arange(ROT // 2, dtype=F32) / ROT)
    angles = jnp.arange(length).astype(F32)[:, None] * frequency[None, :]
    return jnp.cos(angles)[:, None, :], jnp.sin(angles)[:, None, :]


def rotate(values, cos_table, sin_table):
    a = values[..., : ROT // 2]
    b = values[..., ROT // 2 : ROT]
    return jnp.concatenate(
        [a * cos_table - b * sin_table, b * cos_table + a * sin_table, values[..., ROT:]], axis=-1
    )


MESH = pl.DeviceIdType.MESH
TILE = 256
UNIT = 256
PART = 128
ALL = slice(None)


def rope_constants(length):
    frequency = ROPE_BASE ** (-2.0 * np.arange(ROT // 2, dtype=np.float64) / ROT)
    angles = np.arange(length, dtype=np.float64)[:, None] * frequency[None, :]
    cos = np.ones((length, HD))
    sin = np.zeros((length, HD))
    half = ROT // 2
    cos[:, :half] = np.cos(angles)
    cos[:, half:ROT] = np.cos(angles)
    sin[:, :half] = -np.sin(angles)
    sin[:, half:ROT] = np.sin(angles)
    return (
        jnp.asarray(np.tile(cos, (1, 2)), F32),
        jnp.asarray(np.tile(sin, (1, 2)), F32),
    )


def turn(x, cos, sin, sign):
    lane = lax.broadcasted_iota(jnp.int32, x.shape, 1) % HD
    partner = jnp.where(
        lane < ROT // 2,
        pltpu.roll(x, x.shape[1] - ROT // 2, 1),
        pltpu.roll(x, ROT // 2, 1),
    )
    return x * cos + partner * (sin * sign)


def turn_all(x, cos, sin, sign):
    step = cos.shape[1]
    return jnp.concatenate(
        [turn(x[:, i : i + step], cos, sin, sign) for i in range(0, x.shape[1], step)], axis=1
    )


def layer_kernel(
    planes,
    tok_ref,
    cotown_ref,
    wq_in,
    wd_in,
    wi_in,
    wo_in,
    qb_ref,
    db_ref,
    ib_ref,
    ob_ref,
    gain_ref,
    shift_ref,
    index_ref,
    map_refs,
    cos_ref,
    sin_ref,
    out_ref,
    igrad_ref,
    grad_refs,
    stack,
    sel,
    adm,
    downs_ref,
    ups_ref,
    ddown_all,
    qup_all,
    iup_ref,
    odown_ref,
    qgrad,
    a_msg,
    a_h1,
    a_h2,
    b_msg,
    b_h1,
    b_h2,
    q_h1,
    q_h2,
    normed,
    cot,
    wq,
    wd,
    wi,
    wo,
    qkv,
    hg,
    att,
    pg,
    acc_a,
    acc_b,
    pre,
    act,
    ag,
    pgrad,
    coeff,
    cgs,
    coeff_t,
    cgs_t,
    res,
    keep,
    s1_send,
    s1_recv,
    a_send,
    a_recv,
    c_send,
    c_recv,
    ar_send,
    ar_recv,
    ar_low,
    ar_recv_low,
    local_sem,
    zs_sem,
    zr_sem,
    ag_ssem,
    ag_rsem,
    s1_ssem,
    s1_rsem,
    a_ssem,
    a_rsem,
    c_ssem,
    c_rsem,
    ar_ssem,
    ar_rsem,
    adz_ssem,
    adz_rsem,
    h1_ssem,
    h1_rsem,
    h2_ssem,
    h2_rsem,
    q1_ssem,
    q1_rsem,
    q2_ssem,
    q2_rsem,
):
    z = lax.axis_index("fsdp")
    s = lax.axis_index("seq")
    core = s % 2
    chip = s // 2
    to_core = (z, chip * 2 + (1 - core))
    chip_x = chip + 1 - 2 * (chip % 2)
    chip_y = (chip + 2) % 4
    chip_d = chip_x + 2 - 4 * (chip_x // 2)
    to_x = (z, chip_x * 2 + core)
    to_y = (z, chip_y * 2 + core)
    rows, width = tok_ref.shape
    length = normed.shape[0]
    units = act.shape[1]
    fan = width // planes
    mine = wq.shape[3]
    tiles = length // TILE

    def remote(src, dst, ssem, rsem, where):
        return pltpu.make_async_remote_copy(
            src_ref=src, dst_ref=dst, send_sem=ssem, recv_sem=rsem, device_id=where,
            device_id_type=MESH,
        )

    def line(ref, cols):
        return ref[cols].astype(F32)[None, :]

    def block(i, n):
        return pl.ds(pl.multiple_of(i * n, n), n)

    bar = pltpu.get_barrier_semaphore()
    for k in range(1, 8):
        pl.semaphore_signal(bar, inc=1, device_id=(z, (s + k) % 8), device_id_type=MESH)
    for k in range(1, planes):
        pl.semaphore_signal(bar, inc=1, device_id=((z + k) % planes, s), device_id_type=MESH)
    pl.semaphore_wait(bar, 7 + planes - 1)

    chunks = []
    for c in range(3):
        chunks.append((wq_in.at[c], lambda j, c=c: wq.at[j, c]))
    chunks.append((wd_in, lambda j: wd.at[j]))
    part = fan // 4
    for i in range(4):
        chunks.append(
            (
                wi_in.at[pl.ds(i * part, part), :],
                lambda j, i=i: wi.at[j, pl.ds(i * part, part), :],
            )
        )
    for i in range(fan // PART):
        chunks.append(
            (
                wo_in.at[:, pl.ds(i * PART, PART)],
                lambda j, i=i: wo.at[j, :, pl.ds(i * PART, PART)],
            )
        )
    n_chunks = len(chunks)
    ahead = 2
    last_step = n_chunks + planes - 1

    def zcopy(c, direction, k):
        src, place = chunks[c]
        j = z - k if direction == 0 else z + k
        return remote(
            src if k == 0 else place(j),
            place(j),
            zs_sem.at[c, direction, k],
            zr_sem.at[c, j],
            (z + 1, s) if direction == 0 else (z - 1, s),
        )

    def zhas(direction, k):
        if direction == 0:
            return jnp.logical_and(z - k >= 0, z + 1 < planes)
        return jnp.logical_and(z + k < planes, z - 1 >= 0)

    def zsend(c, k):
        for direction in (0, 1):

            @pl.when(zhas(direction, k))
            def _(direction=direction):
                zcopy(c, direction, k).start()

    def zarrived(c, j):
        place = chunks[c][1](j)
        pltpu.make_async_copy(place, place, zr_sem.at[c, j]).wait()

    def zrelay(c, k):
        for direction in (0, 1):

            @pl.when(zhas(direction, k))
            def _(direction=direction):
                zarrived(c, z - k if direction == 0 else z + k)
                zcopy(c, direction, k).start()

    def zfinish(first, last):
        for c in range(first, last):
            for direction in (0, 1):
                for k in range(1, planes):
                    j = z - k if direction == 0 else z + k
                    here = z == planes - 1 if direction == 0 else z == 0

                    @pl.when(here)
                    def _(c=c, j=j):
                        zarrived(c, j)

    def zstep(t):
        if t == 0:
            for c in range(min(ahead, n_chunks - 1) + 1):
                zsend(c, 0)
        elif t + ahead < n_chunks:
            zsend(t + ahead, 0)
        for k in range(1, planes - 1):
            if 0 <= t - k < n_chunks:
                zrelay(t - k, k)

    own = []
    for c in range(n_chunks):
        src, place = chunks[c]
        own.append(pltpu.make_async_copy(src, place(z), local_sem.at[c]))
    zstep(0)
    for copy in own:
        copy.start()

    half = width // 2

    def row_view(buf, b, part):
        if part is None:
            return buf.at[block(b, rows), :]
        return buf.at[block(b, rows), pl.ds(part * half, half)]

    def lead_view(buf, b, part):
        if part is None:
            return buf.at[b]
        return buf.at[b, pl.ds(part * (planes // 2), planes // 2)]

    def gather_copies(p, buf, view):
        bx = chip_x * 2 + core
        by = chip_y * 2 + core
        bd = chip_d * 2 + core
        me = view(buf, s, None)
        blk_x = view(buf, bx, None)
        blk_y = view(buf, by, None)
        blk_d = view(buf, bd, None)
        x0 = view(buf, bx, 0)
        y1 = view(buf, by, 1)
        d0 = view(buf, bd, 0)
        d1 = view(buf, bd, 1)
        ss, rs = ag_ssem.at[p], ag_rsem.at[p]

        def same(ref, i, where):
            return remote(ref, ref, ss.at[i], rs.at[i], where)

        sends = [
            same(me, 0, to_x),
            same(me, 1, to_y),
            same(me, 2, to_core),
            same(x0, 3, to_y),
            same(blk_x, 4, to_core),
            same(y1, 5, to_x),
            same(blk_y, 6, to_core),
            same(blk_d, 7, to_core),
        ]
        other = 1 - core
        into = [
            blk_x,
            blk_y,
            view(buf, chip * 2 + other, None),
            d0,
            view(buf, chip_x * 2 + other, None),
            d1,
            view(buf, chip_y * 2 + other, None),
            view(buf, chip_d * 2 + other, None),
        ]

        def arrived(i):
            pltpu.make_async_copy(into[i], into[i], rs.at[i]).wait()

        return sends, arrived

    cot[block(s, rows), :] = cotown_ref[...]
    c_sends, c_arrived = gather_copies(0, cot, row_view)
    for i in range(3):
        c_sends[i].start()

    n_in = map_refs[5].shape[0]
    spots = ((0, 0), (4, 64), (3, 128), (7, 192), (2, 256))
    for m, at in spots:
        stack[at : at + 64, :] = map_refs[m][...]
    stack[320:384, :] = map_refs[1][128:, :]
    stack[384:512, :] = map_refs[1][:128, :]
    base_in, base_out = 512, 512 + n_in
    stack[base_in : base_in + n_in, :] = map_refs[5][...]
    stack[base_out : base_out + n_in, :] = map_refs[6][...]
    lane = lax.broadcasted_iota(jnp.int32, (RANK, ADAPT * RANK), 1)
    column = lax.broadcasted_iota(jnp.int32, (RANK, ADAPT * RANK), 0)
    picks = []
    for g in range(planes):
        picks.append((lane == column + index_ref[g] * RANK).astype(F32).astype(BF16))
        sel[g] = dot_nt(picks[g], stack[...]).astype(BF16)

    def adapter_copy(k):
        g = (z + k) % planes
        return remote(sel.at[g], adm.at[s, z], adz_ssem.at[k - 1], adz_rsem.at[z], (g, s))

    for k in range(1, planes):
        adapter_copy(k).start()
    adm[s, z] = sel[z]

    x = tok_ref[...].astype(F32)
    mean = jnp.mean(x, axis=-1, keepdims=True)
    centred = x - mean
    inv = lax.rsqrt(jnp.mean(centred * centred, axis=-1, keepdims=True) + EPSILON)
    normed[block(s, rows), :] = (
        centred * inv * line(gain_ref, ALL) + line(shift_ref, ALL)
    ).astype(BF16)
    n_sends, n_arrived = gather_copies(1, normed, row_view)
    for k in range(1, planes):
        g = (z + k) % planes
        pltpu.make_async_copy(adm.at[s, g], adm.at[s, g], adz_rsem.at[g]).wait()
    m_sends, m_arrived = gather_copies(2, adm, lead_view)
    gathers = ((c_sends, c_arrived), (n_sends, n_arrived), (m_sends, m_arrived))
    zstep(1)
    for m, (sends, arrived) in enumerate(gathers):
        arrived(0)
        sends[3].start()
        sends[4].start()
        arrived(1)
        sends[5].start()
        sends[6].start()
        if m < 2:
            for i in range(3):
                gathers[m + 1][0][i].start()
            zstep(m + 2)
    zstep(4)
    for m, (sends, arrived) in enumerate(gathers):
        arrived(3)
        arrived(5)
        sends[7].start()
    for sends, arrived in gathers:
        for i in (2, 4, 6, 7):
            arrived(i)
    zstep(5)

    def order(f, carry):
        low_half = lax.broadcasted_iota(jnp.int32, (RANK, 128), 1) < 64

        def swap(v):
            return pltpu.roll(v, 64, 1)

        for pair in range(4):

            def tile(odd, i):
                return adm[2 * pair + odd, f, :, i * 128 : (i + 1) * 128].astype(F32)

            def first(i):
                return jnp.where(low_half, tile(0, i), swap(tile(1, i))).astype(BF16)

            def second(i):
                return jnp.where(low_half, swap(tile(0, i)), tile(1, i)).astype(BF16)

            where = block(f * 4 + pair, 128)
            downs_ref[:RANK, where] = first(0)
            downs_ref[RANK:, where] = second(0)
            ups_ref[:RANK, where] = first(1)
            ups_ref[RANK:, where] = second(1)
            ddown_all[:, where] = first(2)
            turned = swap(tile(1, 3))
            at = (f * 4 + pair) * 3
            qup_all[:, block(at, 128)] = tile(0, 3).astype(BF16)
            qup_all[:, block(at + 1, 128)] = jnp.where(
                low_half, swap(tile(0, 2)), turned
            ).astype(BF16)
            qup_all[:, block(at + 2, 128)] = jnp.where(low_half, turned, tile(1, 2)).astype(BF16)
        return carry

    lax.fori_loop(0, planes, order, 0)
    for j in range(4):
        q = s * 4 + j
        n = n_in
        iup_ref[:, j * n : (j + 1) * n] = adm[q % 8, q // 8, :, base_in : base_in + n]
        odown_ref[:, j * n : (j + 1) * n] = adm[q % 8, q // 8, :, base_out : base_out + n]

    def qup(c):
        return qup_all[:, pl.ds(pl.multiple_of(c * width + s * mine, mine), mine)]

    def ddown():
        return ddown_all[:, block(s, mine)]

    def low(t, carry):
        r = block(t, TILE)
        c = dot_nt(normed[r, :], downs_ref[...])
        coeff[r, :] = c.astype(BF16)
        g = ADAPTER_SCALE * dot_nt(cot[r, :], ups_ref[...])
        cgs[r, :] = g.astype(BF16)
        return carry

    lax.fori_loop(0, tiles, low, 0)
    for copy in own:
        copy.wait()
    zstep(6)
    zfinish(0, 4)

    def project(t, carry):
        r = block(t, TILE)
        cos = cos_ref[r, :]
        sin = sin_ref[r, :]
        for c in range(3):
            v = ADAPTER_SCALE * dot(coeff[r, :RANK], qup(c))
            v = v + line(qb_ref, pl.ds(pl.multiple_of(c * width + s * mine, mine), mine))
            for j in range(planes):
                v = v + dot(normed[r, j * fan : (j + 1) * fan], wq[j, c])
            if c < 2:
                v = turn_all(v, cos, sin, 1.0)
            v = v.astype(BF16)
            if c == 0:
                v = v * jnp.asarray(HD**-0.5, BF16)
            qkv[c, r, :] = v
        g = dot(cgs[r, :RANK], ddown())
        for j in range(planes):
            g = g + dot_nt(cot[r, j * fan : (j + 1) * fan], wd[j])
        hg[r, :] = g.astype(BF16)
        return carry

    lax.fori_loop(0, tiles, project, 0)
    zstep(7)

    dk = ag.at[:, pl.ds(0, mine)]
    dv = ag.at[:, pl.ds(mine, mine)]
    ag[:, : 2 * mine] = jnp.zeros((length, 2 * mine), F32)
    heads = mine // HD

    for b in range(length // BLOCK):
        lo, hi = b * BLOCK, (b + 1) * BLOCK
        acc_a[...] = jnp.zeros_like(acc_a)
        acc_b[...] = jnp.zeros_like(acc_b)

        def one_head(h, carry, lo=lo, hi=hi):
            lane = lax.broadcasted_iota(jnp.int32, (1, mine), 1)
            mask = (lane // HD == h).astype(BF16)
            mask32 = (lane // HD == h).astype(F32)
            q = qkv[0, lo:hi, :] * mask
            g = hg[lo:hi, :] * mask
            k = qkv[1, :hi, :]
            v = qkv[2, :hi, :]
            sc = dot_nt(q, k)
            e = jnp.exp(sc - jnp.max(sc, axis=-1, keepdims=True))
            p = e * (1.0 / jnp.sum(e, axis=-1, keepdims=True))
            pb = p.astype(BF16)
            acc_a[...] += dot(pb, v) * mask32
            dp = dot_nt(g, v)
            ds = (p * (dp - jnp.sum(dp * p, axis=-1, keepdims=True))).astype(BF16)
            acc_b[...] += dot(ds, k) * mask32
            dk[:hi, :] += dot_tn(ds, q)
            dv[:hi, :] += dot_tn(pb, g)
            return carry

        lax.fori_loop(0, heads, one_head, 0)
        att[lo:hi, :] = acc_a[...].astype(BF16)
        back = (acc_b[...] * (HD**-0.5)).astype(BF16).astype(F32)
        pg[0, lo:hi, :] = turn_all(back, cos_ref[lo:hi, :], sin_ref[lo:hi, :], -1.0).astype(BF16)
        if b == 1:
            zstep(8)
        if b == 2:
            zstep(9)
        if b == 3:
            zstep(10)

    def finish(t, carry):
        r = block(t, TILE)
        back = dk[r, :].astype(BF16).astype(F32)
        pg[1, r, :] = turn_all(back, cos_ref[r, :], sin_ref[r, :], -1.0).astype(BF16)
        pg[2, r, :] = dv[r, :].astype(BF16)
        return carry

    lax.fori_loop(0, tiles, finish, 0)

    coeff_t[...] = dot_nt(downs_ref[...], normed[...]).astype(BF16)
    cgs_t[...] = (ADAPTER_SCALE * dot_nt(ups_ref[...], cot[...])).astype(BF16)

    share = width // 8

    def wait_on(ref, sem):
        pltpu.make_async_copy(ref, ref, sem).wait()

    def hop1(w, msg, h1, start):
        for j in range(4):
            to = 4 * (s % 2) + j
            there = (z, to)

            @pl.when(to != s)
            def _(j=j, there=there):
                copy = remote(
                    msg.at[j], h1.at[s // 2], h1_ssem.at[w, j], h1_rsem.at[w, s // 2], there
                )
                if start:
                    copy.start()
                else:
                    copy.wait_send()

            if start:

                @pl.when(to == s)
                def _(j=j):
                    pltpu.make_async_copy(
                        msg.at[j], h1.at[s // 2], h1_rsem.at[w, s // 2]
                    ).start()

    def hop2_copy(w, h1, h2, k):
        g = (z + k) % planes
        return remote(h1.at[g], h2.at[z], h2_ssem.at[w, k - 1], h2_rsem.at[w, z], (g, s))

    def hop2(w, h1, h2):
        for g in range(planes):
            wait_on(h1.at[g], h1_rsem.at[w, g])
        for k in range(1, planes):
            hop2_copy(w, h1, h2, k).start()
        h2[z] = h1[z]

    def landed(w, h1, h2):
        for k in range(1, planes):
            g = (z + k) % planes
            wait_on(h2.at[g], h2_rsem.at[w, g])
        for k in range(1, planes):
            hop2_copy(w, h1, h2, k).wait_send()

    pick_all = jnp.concatenate(picks, axis=0)

    def spread(h2):
        return dot_tn(h2.reshape(planes * RANK, h2.shape[-1]), pick_all)

    def half_rows(v):
        return jnp.where(s % 2 == 0, v[:64], v[64:])

    for c in range(3):
        g = ADAPTER_SCALE * dot(coeff_t[:RANK, :], pg[c])
        for i in range(2):
            qgrad[2 * c + i] = g[:, i * 128 : (i + 1) * 128].astype(BF16)

    def qkv_hop1(start):
        for c in range(3):
            for i in range(2):
                t = 16 * c + 2 * s + i
                for o in range(2):
                    owner = 2 * (t // 3) + o
                    slot = t % 3 - o
                    ok = jnp.logical_and(slot >= 0, slot <= 1)
                    to = owner % 8
                    src = qgrad.at[2 * c + i]
                    n = 4 * c + 2 * i + o

                    @pl.when(jnp.logical_and(ok, to != s))
                    def _(src=src, owner=owner, slot=slot, to=to, n=n):
                        copy = remote(
                            src, q_h1.at[owner // 8, slot], q1_ssem.at[n],
                            q1_rsem.at[owner // 8, slot], (z, to),
                        )
                        if start:
                            copy.start()
                        else:
                            copy.wait_send()

                    if start:

                        @pl.when(jnp.logical_and(ok, to == s))
                        def _(src=src, owner=owner, slot=slot):
                            pltpu.make_async_copy(
                                src, q_h1.at[owner // 8, slot], q1_rsem.at[owner // 8, slot]
                            ).start()

    def qkv_hop2_copy(k):
        g = (z + k) % planes
        return remote(q_h1.at[g], q_h2.at[z], q2_ssem.at[k - 1], q2_rsem.at[z], (g, s))

    def qkv_hop2():
        for g in range(planes):
            for slot in range(2):
                wait_on(q_h1.at[g, slot], q1_rsem.at[g, slot])
        for k in range(1, planes):
            qkv_hop2_copy(k).start()
        q_h2[z] = q_h1[z]

    def qkv_landed():
        for k in range(1, planes):
            g = (z + k) % planes
            wait_on(q_h2.at[g], q2_rsem.at[g])
        for k in range(1, planes):
            qkv_hop2_copy(k).wait_send()

    qkv_hop1(True)
    g = dot(cgs_t[:RANK, :], att[...])
    for j in range(4):
        a_msg[j, :, 256:384] = g[:, (j // 2) * 128 : (j // 2 + 1) * 128].astype(BF16)
    pass
    zfinish(4, 8)
    zstep(11)

    k0 = 0.7978845608028654
    k1 = 0.044715

    def inner(t, carry):
        r = block(t, TILE)
        v = ADAPTER_SCALE * dot(coeff[r, RANK : 2 * RANK], iup_ref[...])
        v = v + line(ib_ref, block(s, units))
        for j in range(planes):
            v = v + dot(normed[r, j * fan : (j + 1) * fan], wi[j])
        sq = v * v
        th = jnp.tanh(k0 * v * (1.0 + k1 * sq))
        act[r, :] = (0.5 * v * (1.0 + th)).astype(BF16)
        pre[r, :] = 0.5 * (1.0 + th) + 0.5 * v * (1.0 - th * th) * (k0 * (1.0 + 3.0 * k1 * sq))
        return carry

    lax.fori_loop(0, tiles, inner, 0)
    for k in range(1, planes):
        adapter_copy(k).wait_send()
    for sends, _ in gathers:
        for copy in sends:
            copy.wait_send()
    spot = (8, planes, RANK, share)
    for i in range(length // (8 * planes * RANK)):
        span = 8 * planes * RANK
        adm[:, :, :, i * share : (i + 1) * share] = normed[
            i * span : (i + 1) * span, block(s, share)
        ].reshape(spot)
    g = dot(cgs_t[RANK : 2 * RANK, :], act[...])
    for j in range(4):
        a_msg[j, :, :256] = g[:, j * 256 : (j + 1) * 256].astype(BF16)
    zstep(12)

    partners = (to_core, to_x, to_y)

    def reduce_copy(w, i):
        src = ar_send.at[0] if w == 0 else ar_low
        dst = ar_recv.at[i] if w == 0 else ar_recv_low.at[i]
        return remote(src, dst, ar_ssem.at[w, i], ar_rsem.at[w, i], partners[i])

    def reduce_round(w, i):
        if i > 0:
            reduce_copy(w, i - 1).wait()
            got = ar_recv[i - 1] if w == 0 else ar_recv_low[i - 1].astype(F32)
            ar_send[w] += got
        if i < 3:
            if w == 1:
                ar_low[...] = ar_send[1].astype(BF16)
            reduce_copy(w, i).start()

    ar_send[0, :RANK, :] = dot_nt(ddown(), att[...])
    ar_send[0, RANK : 2 * RANK, :] = dot_nt(odown_ref[...], act[...])
    p_units = width // UNIT
    per = fan // UNIT
    def attention_back(u, carry):
        j = u // per
        rws = block(u % per, UNIT)
        for h in range(2):
            r = slice(h * length // 2, (h + 1) * length // 2)
            v = dot_nt(pg[0, r, :], wq[j, 0, rws, :])
            for c in range(1, 3):
                v = v + dot_nt(pg[c, r, :], wq[j, c, rws, :])
            normed[r, block(u, UNIT)] = v.astype(BF16)
        return carry

    for i in range(4):
        reduce_round(0, i)
        lax.fori_loop(2 * i, 2 * i + 2, attention_back, 0)
    coeff_dense = ar_send[0].astype(BF16)
    for i in range(2):
        g = ADAPTER_SCALE * dot(
            coeff_dense[i * RANK : (i + 1) * RANK, :], cot[:, block(s, share)]
        )
        for j in range(4):
            at = 384 + i * 128
            a_msg[j, :, at : at + 128] = g[:, (j // 2) * 128 : (j // 2 + 1) * 128].astype(BF16)
    hop1(0, a_msg, a_h1, True)

    p_units = width // UNIT
    per = fan // UNIT
    early = p_units - planes // 2
    total = 2 * p_units

    def branch_place(n):
        return (n % (planes // 2)) * 2, n // (planes // 2)

    def back_place(n):
        return (n - p_units) // per, (n - p_units) % per

    def keep_split(n, k, r):
        slot = n % 2
        a = r[:rows, :]
        b = r[rows:, :]
        first = core == 0
        keep[n % 6, k] = jnp.where(first, a, b)
        s1_send[slot, k] = jnp.where(first, b, a).astype(BF16)

    def keep_pair(n, k, v):
        keep_split(n, 2 * k, v[:TILE])
        keep_split(n, 2 * k + 1, v[TILE:])

    def s1_copy(n):
        return remote(s1_send.at[n % 2], s1_recv.at[n], s1_ssem.at[n % 2], s1_rsem.at[n], to_core)

    def a_copy(n, i):
        return remote(
            a_send.at[n % 3, i], a_recv.at[n, i], a_ssem.at[n % 3, i], a_rsem.at[n, i],
            (to_x, to_y)[i],
        )

    def c_copy(n, i):
        return remote(
            c_send.at[n % 3, i], c_recv.at[n, i], c_ssem.at[n % 3, i], c_rsem.at[n, i],
            (to_x, to_y)[i],
        )

    hu = UNIT // 2

    def stage0_branch(n):
        j, i = branch_place(n)

        def tile(k, carry):
            r = block(k, 2 * TILE)
            cols = block(i, PART)
            w_o = jnp.concatenate([wo[j, :, cols], wo[j + 1, :, cols]], axis=1)
            w_d = jnp.concatenate([wd[j, :, cols], wd[j + 1, :, cols]], axis=1)
            keep_pair(n, k, dot(act[r, :], w_o) + dot(att[r, :], w_d))
            return carry

        lax.fori_loop(0, tiles // 2, tile, 0)
        s1_copy(n).start()

    def stage0_back(n):
        j, i = back_place(n)

        def tile(k, carry):
            r = block(k, 2 * TILE)
            rws = block(i, UNIT)
            v = dot_nt(pgrad[r, :], wi[j, rws, :])
            v = v + normed[r, block(n - p_units, UNIT)].astype(F32)
            keep_pair(n, k, v)
            return carry

        lax.fori_loop(0, tiles // 2, tile, 0)
        s1_copy(n).start()

    def stage1(n):
        s1_copy(n).wait()
        q = n % 6
        for k in range(4):
            keep[q, k] += s1_recv[n, k].astype(F32)
        far = keep[q, chip_d]
        a_send[n % 3, 0] = far[:, :hu].astype(BF16)
        a_send[n % 3, 1] = far[:, hu:].astype(BF16)
        for i in range(2):
            a_copy(n, i).start()

    def stage2(n):
        q = n % 6
        for i in range(2):
            a_copy(n, i).wait()
        keep[q, chip_y, :, :hu] += a_recv[n, 0].astype(F32)
        keep[q, chip_x, :, hu:] += a_recv[n, 1].astype(F32)
        c_send[n % 3, 0] = keep[q, chip_x].astype(BF16)
        c_send[n % 3, 1] = keep[q, chip_y].astype(BF16)
        for i in range(2):
            c_copy(n, i).start()

    def stage3(n):
        q = n % 6
        for i in range(2):
            c_copy(n, i).wait()
        v = keep[q, chip] + c_recv[n, 0].astype(F32) + c_recv[n, 1].astype(F32)

        @pl.when(n < p_units)
        def _():
            j, i = branch_place(n)
            for m in range(2):
                res[:, pl.ds(pl.multiple_of((j + m) * fan + i * PART, PART), PART)] = v[
                    :, m * PART : (m + 1) * PART
                ]

        @pl.when(n >= p_units)
        def _():
            igrad_ref[:, block(n - p_units, UNIT)] = v

    def pipeline(first, lo, hi, stage0, extra=None, units_end=None):
        def body(n, carry):
            if stage0 is not None:
                stage0(n)
            for back, stage in ((1, stage1), (3, stage2), (5, stage3)):
                m = n - back
                ok = m >= first
                if stage0 is None:
                    ok = jnp.logical_and(ok, m < units_end)

                @pl.when(ok)
                def _(m=m, stage=stage):
                    stage(m)

            if extra is not None:
                extra(n)
            return carry

        lax.fori_loop(lo, hi, body, 0)

    zstep(13)
    def act_part(r, i):
        cols = [slice(j * fan + i * PART, j * fan + (i + 1) * PART) for j in range(planes)]
        g = jnp.concatenate([cot[r, c] for c in cols], axis=1)
        w = [wo[j, :, i * PART : (i + 1) * PART] for j in range(planes)]
        return dot_nt(g, jnp.concatenate(w, axis=1))

    per_part = planes // 2
    for i in range(fan // PART - 1):
        zfinish(8 + i, 9 + i)
        pipeline(0, i * per_part, (i + 1) * per_part, stage0_branch)

        def act_back(t, carry, i=i):
            r = block(t, TILE)
            if i == 1:
                v = dot(cgs[r, RANK : 2 * RANK], odown_ref[...]) + act_part(r, 0)
                ag[r, :] = v + act_part(r, 1)
            else:
                ag[r, :] += act_part(r, i)
            return carry

        if i > 0:
            lax.fori_loop(0, tiles, act_back, 0)
    zfinish(11, 12)

    pipeline(0, early, p_units, stage0_branch)

    def act_last(t, carry):
        r = block(t, TILE)
        v = ag[r, :] + act_part(r, fan // PART - 1)
        pgrad[r, :] = (v * pre[r, :]).astype(BF16)
        return carry

    lax.fori_loop(0, tiles, act_last, 0)

    def rounds(n):
        @pl.when(n == p_units)
        def _():
            up_part = dot_nt(iup_ref[...], pgrad[...])
            q_part = dot_nt(qup(0), pg[0])
            for c in range(1, 3):
                q_part = q_part + dot_nt(qup(c), pg[c])
            ar_send[1, :RANK, :] = ADAPTER_SCALE * q_part
            ar_send[1, RANK : 2 * RANK, :] = ADAPTER_SCALE * up_part
            reduce_round(1, 0)
            qkv_hop2()
            hop2(0, a_h1, a_h2)

        @pl.when(n == p_units + 4)
        def _():
            qkv_landed()
            full = [spread(q_h2[:, i]) for i in range(2)]
            full = jnp.concatenate(full, axis=0)
            grad_refs[1][...] = jnp.where(s % 2 == 0, full[:192], full[64:])

        @pl.when(n == p_units + 3)
        def _():
            landed(0, a_h1, a_h2)
            full = spread(a_h2[...])
            grad_refs[6][...] = full[:256]
            grad_refs[2][...] = half_rows(full[256:384])
            grad_refs[3][...] = half_rows(full[384:512])
            grad_refs[7][...] = half_rows(full[512:640])


        for i in range(1, 4):

            @pl.when(n == p_units + (1, 3, 5)[i - 1])
            def _(i=i):
                reduce_round(1, i)
                if i == 2:
                    g = ADAPTER_SCALE * dot(coeff_t[RANK : 2 * RANK, :], pgrad[...])
                    for j in range(4):
                        b_msg[j, :, :256] = g[:, j * 256 : (j + 1) * 256].astype(BF16)
                if i == 3:
                    g = None
                    span = 8 * planes * RANK
                    for m in range(length // span):
                        part = dot(
                            ar_send[1, :, m * span : (m + 1) * span].astype(BF16),
                            adm[:, :, :, m * share : (m + 1) * share].reshape(span, share),
                        )
                        g = part if g is None else g + part
                    for m in range(2):
                        for j in range(4):
                            b_msg[j, :, 256 + m * 128 : 384 + m * 128] = g[
                                m * RANK : (m + 1) * RANK, (j // 2) * 128 : (j // 2 + 1) * 128
                            ].astype(BF16)
                    hop1(1, b_msg, b_h1, True)

    pipeline(0, p_units, total, stage0_back, rounds)
    pipeline(0, total, total + 3, None, None, total)
    hop2(1, b_h1, b_h2)
    pipeline(0, total + 3, total + 5, None, None, total)

    first_t = ar_send[0, :, block(s, rows)].astype(BF16)
    late_t = ar_send[1, :, block(s, rows)].astype(BF16)
    out = tok_ref[...].astype(F32) + res[...] + ADAPTER_SCALE * dot_tn(first_t, ups_ref[...])
    out_ref[...] = (out + line(db_ref, ALL) + line(ob_ref, ALL)).astype(BF16)
    x = tok_ref[...].astype(F32)
    mean = jnp.mean(x, axis=-1, keepdims=True)
    centred = x - mean
    inv = lax.rsqrt(jnp.mean(centred * centred, axis=-1, keepdims=True) + EPSILON)
    xhat = centred * inv
    e = (igrad_ref[...] + dot_tn(late_t, downs_ref[...])) * line(gain_ref, ALL)
    igrad_ref[...] = cotown_ref[...].astype(F32) + inv * (
        e
        - jnp.mean(e, axis=-1, keepdims=True)
        - xhat * jnp.mean(e * xhat, axis=-1, keepdims=True)
    )

    landed(1, b_h1, b_h2)
    full = spread(b_h2[...])
    grad_refs[5][...] = full[:256]
    grad_refs[0][...] = half_rows(full[256:384])
    grad_refs[4][...] = half_rows(full[384:512])

    hop1(0, a_msg, a_h1, False)
    hop1(1, b_msg, b_h1, False)
    qkv_hop1(False)
    for c in range(n_chunks):
        for k in range(planes - 1):
            for direction in (0, 1):

                @pl.when(zhas(direction, k))
                def _(c=c, k=k, direction=direction):
                    zcopy(c, direction, k).wait_send()


def run_layer(planes, args, shapes):
    rows, width, length, units, mine = shapes
    fan = width // planes
    vm = pl.BlockSpec(memory_space=pltpu.VMEM)
    hbm = pl.BlockSpec(memory_space=pl.ANY)
    n_chunks = 8 + fan // PART
    total = 2 * width // UNIT
    dma = pltpu.SemaphoreType.DMA
    maps = args[13:21]
    lanes = sum(m.shape[0] for m in maps)

    def entry(*refs):
        layer_kernel(planes, *refs[:13], refs[13:21], *refs[21:25], refs[25:33], *refs[33:])

    outs = pl.pallas_call(
        entry,
        out_shape=(
            jax.ShapeDtypeStruct((rows, width), BF16),
            jax.ShapeDtypeStruct((rows, width), F32),
            *(jax.ShapeDtypeStruct(m.shape, F32) for m in maps),
        ),
        in_specs=[vm, vm, hbm, hbm, hbm, hbm]
        + [vm] * 6
        + [pl.BlockSpec(memory_space=pltpu.SMEM)]
        + [vm] * 10,
        out_specs=(vm,) * 10,
        scratch_shapes=[
            pltpu.VMEM((lanes, ADAPT * RANK), BF16),
            pltpu.VMEM((planes, RANK, lanes), BF16),
            pltpu.VMEM((8, planes, RANK, lanes), BF16),
            pltpu.VMEM((2 * RANK, width), BF16),
            pltpu.VMEM((2 * RANK, width), BF16),
            pltpu.VMEM((RANK, width), BF16),
            pltpu.VMEM((RANK, 3 * width), BF16),
            pltpu.VMEM((RANK, units), BF16),
            pltpu.VMEM((RANK, units), BF16),
            pltpu.VMEM((6, RANK, 128), BF16),
            pltpu.VMEM((4, RANK, 640), BF16),
            pltpu.VMEM((planes, RANK, 640), BF16),
            pltpu.VMEM((planes, RANK, 640), BF16),
            pltpu.VMEM((4, RANK, 512), BF16),
            pltpu.VMEM((planes, RANK, 512), BF16),
            pltpu.VMEM((planes, RANK, 512), BF16),
            pltpu.VMEM((planes, 2, RANK, 128), BF16),
            pltpu.VMEM((planes, 2, RANK, 128), BF16),
            pltpu.VMEM((length, width), BF16),
            pltpu.VMEM((length, width), BF16),
            pltpu.VMEM((planes, 3, fan, mine), BF16),
            pltpu.VMEM((planes, mine, fan), BF16),
            pltpu.VMEM((planes, fan, units), BF16),
            pltpu.VMEM((planes, units, fan), BF16),
            pltpu.VMEM((3, length, mine), BF16),
            pltpu.VMEM((length, mine), BF16),
            pltpu.VMEM((length, mine), BF16),
            pltpu.VMEM((3, length, mine), BF16),
            pltpu.VMEM((BLOCK, mine), F32),
            pltpu.VMEM((BLOCK, mine), F32),
            pltpu.VMEM((length, units), F32),
            pltpu.VMEM((length, units), BF16),
            pltpu.VMEM((length, units), F32),
            pltpu.VMEM((length, units), BF16),
            pltpu.VMEM((length, 2 * RANK), BF16),
            pltpu.VMEM((length, 2 * RANK), BF16),
            pltpu.VMEM((2 * RANK, length), BF16),
            pltpu.VMEM((2 * RANK, length), BF16),
            pltpu.VMEM((rows, width), F32),
            pltpu.VMEM((6, 4, rows, UNIT), F32),
            pltpu.VMEM((2, 4, rows, UNIT), BF16),
            pltpu.VMEM((total, 4, rows, UNIT), BF16),
            pltpu.VMEM((3, 2, rows, UNIT // 2), BF16),
            pltpu.VMEM((total, 2, rows, UNIT // 2), BF16),
            pltpu.VMEM((3, 2, rows, UNIT), BF16),
            pltpu.VMEM((total, 2, rows, UNIT), BF16),
            pltpu.VMEM((2, 2 * RANK, length), F32),
            pltpu.VMEM((3, 2 * RANK, length), F32),
            pltpu.VMEM((2 * RANK, length), BF16),
            pltpu.VMEM((3, 2 * RANK, length), BF16),
            dma((n_chunks,)),
            dma((n_chunks, 2, planes)),
            dma((n_chunks, planes)),
            dma((3, 8)),
            dma((3, 8)),
            dma((2,)),
            dma((total,)),
            dma((3, 2)),
            dma((total, 2)),
            dma((3, 2)),
            dma((total, 2)),
            dma((2, 3)),
            dma((2, 3)),
            dma((planes,)),
            dma((planes,)),
            dma((2, 4)),
            dma((2, planes)),
            dma((2, planes)),
            dma((2, planes)),
            dma((12,)),
            dma((planes, 2)),
            dma((planes,)),
            dma((planes,)),
        ],
        compiler_params=pltpu.CompilerParams(
            collective_id=0, has_side_effects=True, vmem_limit_bytes=63 * 1024 * 1024
        ),
    )(*args)
    return pl.pallas_call(
        hand_over,
        out_shape=tuple(jax.ShapeDtypeStruct(o.shape, o.dtype) for o in outs),
        in_specs=[vm] * 10,
        out_specs=(vm,) * 10,
    )(*outs)


def hand_over(*refs):
    for i in range(10):
        refs[10 + i][...] = refs[i][...]


def fits(planes, groups, shapes):
    rows, width, length, units, mine = shapes
    return (
        groups == 8
        and planes == 4
        and rows * 2 == TILE
        and length <= 1024
        and width == 2048
        and mine == 256
        and units == 1024
    )


def deliver(packed, sizes, counts, pick, planes, groups):
    s = lax.axis_index("seq")
    everyone = lax.all_gather(packed, "seq", axis=0, tiled=False)
    owned = []
    at = 0
    for i, (n, w) in enumerate(zip(counts, sizes)):
        part = everyone[:, :, at : at + w]
        at += w
        blocks = 3 if i == 1 else 1
        part = part.reshape(groups, RANK, blocks, w // blocks).transpose(1, 2, 0, 3)
        part = part.reshape(RANK, planes, groups, n)
        owned.append(lax.dynamic_index_in_dim(part, s, 2, keepdims=False))
    owned = jnp.concatenate(owned, axis=2).transpose(1, 0, 2)
    arrived = lax.all_to_all(owned, "fsdp", split_axis=0, concat_axis=0, tiled=True)
    place = pick.astype(F32).reshape(planes * RANK, ADAPT * RANK)
    spread = lax.dot_general(
        arrived.reshape(planes * RANK, -1),
        place,
        (((0,), (0,)), ((), ())),
        precision=lax.Precision.HIGHEST,
        preferred_element_type=F32,
    )
    outs = []
    at = 0
    for n in counts:
        outs.append(spread[at : at + n])
        at += n
    return outs


def on_device(
    tokens,
    cotangent,
    adapter_index,
    qkv_weight,
    dense_weight,
    inner_weight,
    outer_weight,
    qkv_bias,
    dense_bias,
    inner_bias,
    outer_bias,
    norm_gain,
    norm_bias,
    *maps,
):
    planes = lax.axis_size("fsdp")
    groups = lax.axis_size("seq")
    rows, width = tokens.shape
    length = rows * groups
    heads = H // groups
    mine = heads * HD
    units = inner_weight.shape[1]
    s = lax.axis_index("seq")

    shapes = (rows, width, length, units, mine)
    if fits(planes, groups, shapes):
        return run_layer(
            planes,
            (
                tokens,
                cotangent,
                qkv_weight,
                dense_weight,
                inner_weight,
                outer_weight,
                qkv_bias,
                dense_bias,
                inner_bias,
                outer_bias,
                norm_gain,
                norm_bias,
                adapter_index,
                *maps,
                *rope_constants(length),
            ),
            shapes,
        )

    counts = [m.shape[0] for m in maps]
    stacked = jnp.concatenate(maps, axis=0)
    wanted = (adapter_index[:, None] * RANK + jnp.arange(RANK)[None, :]).reshape(-1)
    pick = (wanted[:, None] == jnp.arange(ADAPT * RANK)[None, :]).astype(BF16)
    chosen = dot_nt(pick, stacked).astype(BF16).reshape(planes, RANK, -1)
    chosen = lax.all_to_all(chosen, "fsdp", split_axis=0, concat_axis=0, tiled=True)
    chosen = lax.all_gather(chosen, "seq", axis=1, tiled=False)
    full = []
    at = 0
    for n in counts:
        part = chosen[:, :, :, at : at + n]
        full.append(part.transpose(2, 0, 1, 3).reshape(RANK, -1))
        at += n
    qkv_down, qkv_up, dense_down, dense_up, inner_down, inner_up, outer_down, outer_up = full

    def own(m, n):
        return lax.dynamic_slice_in_dim(m, s * n, n, axis=1)

    qkv_up = jnp.concatenate(
        [own(qkv_up[:, c * width : (c + 1) * width], mine) for c in range(3)], axis=1
    )
    dense_down = own(dense_down, mine)
    inner_up = own(inner_up, units)
    outer_down = own(outer_down, units)

    wqkv = lax.all_gather(qkv_weight, "fsdp", axis=1, tiled=True)
    wdense = lax.all_gather(dense_weight, "fsdp", axis=1, tiled=True)
    winner = lax.all_gather(inner_weight, "fsdp", axis=0, tiled=True)
    wouter = lax.all_gather(outer_weight, "fsdp", axis=1, tiled=True)

    gain = norm_gain.astype(F32)
    shift = norm_bias.astype(F32)
    source = tokens.astype(F32)
    normed_own = norm_layer(source, gain, shift).astype(BF16)
    normed = lax.all_gather(normed_own, "seq", axis=0, tiled=True)
    cot = lax.all_gather(cotangent, "seq", axis=0, tiled=True)

    coeffs = dot_nt(normed, jnp.concatenate([qkv_down, inner_down], axis=0)).astype(BF16)
    qkv_coeff, inner_coeff = coeffs[:, :RANK], coeffs[:, RANK:]
    cgs = (
        ADAPTER_SCALE * dot_nt(cot, jnp.concatenate([dense_up, outer_up], axis=0))
    ).astype(BF16)
    dense_cg, outer_cg = cgs[:, :RANK], cgs[:, RANK:]

    bias = jnp.stack([own(qkv_bias.reshape(3, width)[c : c + 1], mine)[0] for c in range(3)])
    projected = (
        jnp.concatenate([dot(normed, wqkv[c]) for c in range(3)], axis=1)
        + bias.reshape(-1).astype(F32)
        + ADAPTER_SCALE * dot(qkv_coeff, qkv_up)
    ).reshape(length, 3, heads, HD)
    cos_table, sin_table = rope_tables(length, heads)
    query = rotate(projected[:, 0], cos_table, sin_table).astype(BF16).transpose(1, 0, 2)
    key = rotate(projected[:, 1], cos_table, sin_table).astype(BF16).transpose(1, 0, 2)
    value = projected[:, 2].astype(BF16).transpose(1, 0, 2)
    attended_grad = (dot_nt(cot, wdense) + dot(dense_cg, dense_down)).astype(BF16)
    head_grad = attended_grad.reshape(length, heads, HD).transpose(1, 0, 2)

    scale = HD ** (-0.5)

    def bmm(spec, a, b):
        return jnp.einsum(spec, a, b, preferred_element_type=F32)

    key_grad = jnp.zeros((heads, length, HD), F32)
    value_grad = jnp.zeros((heads, length, HD), F32)
    attended_parts = []
    query_parts = []
    for b in range(length // BLOCK):
        lo, hi = b * BLOCK, (b + 1) * BLOCK
        q = query[:, lo:hi]
        k = key[:, :hi]
        v = value[:, :hi]
        g = head_grad[:, lo:hi]
        scores = bmm("hqd,hkd->hqk", q, k) * scale
        row_max = jnp.max(scores, axis=-1, keepdims=True)
        exponent = jnp.exp(scores - row_max)
        prob = exponent / jnp.sum(exponent, axis=-1, keepdims=True)
        prob_low = prob.astype(BF16)
        attended_parts.append(bmm("hqk,hkd->hqd", prob_low, v).astype(BF16))
        prob_grad = bmm("hqd,hkd->hqk", g, v)
        row_dot = jnp.sum(prob_grad * prob, axis=-1, keepdims=True)
        score_grad = (prob * (prob_grad - row_dot)).astype(BF16)
        query_parts.append((bmm("hqk,hkd->hqd", score_grad, k) * scale).astype(BF16))
        key_grad = key_grad.at[:, :hi].add(bmm("hqk,hqd->hkd", score_grad, q) * scale)
        value_grad = value_grad.at[:, :hi].add(bmm("hqk,hqd->hkd", prob_low, g))

    def rows_first(x):
        return x.transpose(1, 0, 2)

    attended = rows_first(jnp.concatenate(attended_parts, axis=1)).reshape(length, mine)
    query_grad = rows_first(jnp.concatenate(query_parts, axis=1)).astype(F32)
    key_back = rows_first(key_grad.astype(BF16)).astype(F32)
    value_back = rows_first(value_grad.astype(BF16)).reshape(length, mine)
    projected_grad = jnp.concatenate(
        [
            rotate(query_grad, cos_table, -sin_table).astype(BF16).reshape(length, mine),
            rotate(key_back, cos_table, -sin_table).astype(BF16).reshape(length, mine),
            value_back,
        ],
        axis=1,
    )

    pre_act = (
        dot(normed, winner)
        + own(inner_bias[None], units).astype(F32)
        + ADAPTER_SCALE * dot(inner_coeff, inner_up)
    )
    act32, gelu_back = jax.vjp(lambda v: jax.nn.gelu(v, approximate=True), pre_act)
    activated = act32.astype(BF16)
    act_grad = dot_nt(cot, wouter) + dot(outer_cg, outer_down)
    pre_grad = gelu_back(act_grad)[0].astype(BF16)

    def scatter(x):
        return lax.psum_scatter(x, "seq", scatter_dimension=0, tiled=True)

    branch = scatter((dot(attended, wdense) + dot(activated, wouter)))
    coeff_sum = scatter(
        jnp.concatenate([dot_nt(attended, dense_down), dot_nt(activated, outer_down)], axis=1)
    )
    back = dot_nt(pre_grad, winner)
    for c in range(3):
        back = back + dot_nt(projected_grad[:, c * mine : (c + 1) * mine], wqkv[c])
    back = scatter(back)
    cg_sum = scatter(
        ADAPTER_SCALE
        * jnp.concatenate([dot_nt(projected_grad, qkv_up), dot_nt(pre_grad, inner_up)], axis=1)
    )
    late_own = jnp.concatenate([coeff_sum, cg_sum], axis=1).astype(BF16)
    late = lax.all_gather(late_own, "seq", axis=0, tiled=True)

    layer_out = (
        source
        + branch
        + dense_bias.astype(F32)
        + outer_bias.astype(F32)
        + ADAPTER_SCALE
        * dot(late_own[:, : 2 * RANK], jnp.concatenate([dense_up, outer_up], axis=0))
    ).astype(BF16)
    normed_grad = back + dot(
        late_own[:, 2 * RANK :], jnp.concatenate([qkv_down, inner_down], axis=0)
    )
    row_mean = jnp.mean(source, axis=-1, keepdims=True)
    centred = source - row_mean
    inv = lax.rsqrt(jnp.mean(centred * centred, axis=-1, keepdims=True) + EPSILON)
    xhat = centred * inv
    e = normed_grad * gain
    input_grad = cotangent.astype(F32) + inv * (
        e
        - jnp.mean(e, axis=-1, keepdims=True)
        - xhat * jnp.mean(e * xhat, axis=-1, keepdims=True)
    )

    share = width // groups
    cot_mine = own(cot, share)
    normed_mine = own(normed, share)
    qkv_up_g = ADAPTER_SCALE * dot_tn(qkv_coeff, projected_grad)
    inner_up_g = ADAPTER_SCALE * dot_tn(inner_coeff, pre_grad)
    dense_down_g = dot_tn(dense_cg, attended)
    outer_down_g = dot_tn(outer_cg, activated)
    ups = ADAPTER_SCALE * dot_tn(late[:, : 2 * RANK], cot_mine)
    downs = dot_tn(late[:, 2 * RANK :], normed_mine)
    mine_grads = [
        downs[:RANK],
        qkv_up_g,
        dense_down_g,
        ups[:RANK],
        downs[RANK:],
        inner_up_g,
        outer_down_g,
        ups[RANK:],
    ]
    packed = jnp.concatenate(mine_grads, axis=1)
    sizes = [g.shape[1] for g in mine_grads]
    outs = deliver(packed, sizes, counts, pick, planes, groups)
    return (layer_out, input_grad, *outs)


def solution(mesh):
    both = P(("fsdp", "seq"), None)
    placed = (
        both,
        both,
        P(),
        P(None, "fsdp", "seq"),
        P("seq", "fsdp"),
        P("fsdp", "seq"),
        P("seq", "fsdp"),
    ) + (P(),) * 6 + (both,) * 8
    return jax.shard_map(
        on_device, mesh=mesh, in_specs=placed, out_specs=(both,) * 10, check_vma=False
    )
```

```python
import functools

import jax
import jax.numpy as jnp
import numpy as np
from jax import lax
from jax.experimental import pallas as pl
from jax.experimental.pallas import tpu as pltpu
from jax.sharding import PartitionSpec as P

H = 32
HD = 64
ROT = 32
RANK = 16
ADAPT = 8
BLOCK = 256
EPSILON = 1e-05
ADAPTER_SCALE = 2.0
ROPE_BASE = 10000.0
MASKED = -1e30
F32 = jnp.float32
BF16 = jnp.bfloat16


def dot(a, b, dims=((1,), (0,))):
    return lax.dot_general(a, b, (dims, ((), ())), preferred_element_type=F32)


def dot_nt(a, b):
    return dot(a, b, ((1,), (1,)))


def dot_tn(a, b):
    return dot(a, b, ((0,), (0,)))


def norm_layer(values, scale_gain, offset_bias):
    row_mean = jnp.mean(values, axis=-1, keepdims=True)
    centred = values - row_mean
    spread = jnp.mean(centred * centred, axis=-1, keepdims=True)
    return centred * lax.rsqrt(spread + EPSILON) * scale_gain + offset_bias


def rope_tables(length, heads):
    frequency = ROPE_BASE ** (-2.0 * jnp.arange(ROT // 2, dtype=F32) / ROT)
    angles = jnp.arange(length).astype(F32)[:, None] * frequency[None, :]
    return jnp.cos(angles)[:, None, :], jnp.sin(angles)[:, None, :]


def rotate(values, cos_table, sin_table):
    a = values[..., : ROT // 2]
    b = values[..., ROT // 2 : ROT]
    return jnp.concatenate(
        [a * cos_table - b * sin_table, b * cos_table + a * sin_table, values[..., ROT:]], axis=-1
    )


MESH = pl.DeviceIdType.MESH
TILE = 256
UNIT = 256
PART = 128
ALL = slice(None)


def rope_constants(length):
    frequency = ROPE_BASE ** (-2.0 * np.arange(ROT // 2, dtype=np.float64) / ROT)
    angles = np.arange(length, dtype=np.float64)[:, None] * frequency[None, :]
    cos = np.ones((length, HD))
    sin = np.zeros((length, HD))
    half = ROT // 2
    cos[:, :half] = np.cos(angles)
    cos[:, half:ROT] = np.cos(angles)
    sin[:, :half] = -np.sin(angles)
    sin[:, half:ROT] = np.sin(angles)
    return (
        jnp.asarray(np.tile(cos, (1, 2)), F32),
        jnp.asarray(np.tile(sin, (1, 2)), F32),
    )


def turn(x, cos, sin, sign):
    lane = lax.broadcasted_iota(jnp.int32, x.shape, 1) % HD
    partner = jnp.where(
        lane < ROT // 2,
        pltpu.roll(x, x.shape[1] - ROT // 2, 1),
        pltpu.roll(x, ROT // 2, 1),
    )
    return x * cos + partner * (sin * sign)


def turn_all(x, cos, sin, sign):
    step = cos.shape[1]
    return jnp.concatenate(
        [turn(x[:, i : i + step], cos, sin, sign) for i in range(0, x.shape[1], step)], axis=1
    )


def layer_kernel(
    planes,
    tok_ref,
    cotown_ref,
    wq_in,
    wd_in,
    wi_in,
    wo_in,
    qb_ref,
    db_ref,
    ib_ref,
    ob_ref,
    gain_ref,
    shift_ref,
    index_ref,
    map_refs,
    cos_ref,
    sin_ref,
    out_ref,
    igrad_ref,
    grad_refs,
    stack,
    sel,
    adm,
    downs_ref,
    ups_ref,
    ddown_all,
    qup_all,
    iup_ref,
    odown_ref,
    qgrad,
    a_msg,
    a_h1,
    a_h2,
    b_msg,
    b_h1,
    b_h2,
    q_h1,
    q_h2,
    normed,
    cot,
    wq,
    wd,
    wi,
    wo,
    qkv,
    hg,
    att,
    pg,
    acc_a,
    acc_b,
    pre,
    act,
    ag,
    pgrad,
    coeff,
    cgs,
    coeff_t,
    cgs_t,
    res,
    keep,
    s1_send,
    s1_recv,
    a_send,
    a_recv,
    c_send,
    c_recv,
    ar_send,
    ar_recv,
    ar_low,
    ar_recv_low,
    local_sem,
    zs_sem,
    zr_sem,
    ag_ssem,
    ag_rsem,
    s1_ssem,
    s1_rsem,
    a_ssem,
    a_rsem,
    c_ssem,
    c_rsem,
    ar_ssem,
    ar_rsem,
    adz_ssem,
    adz_rsem,
    h1_ssem,
    h1_rsem,
    h2_ssem,
    h2_rsem,
    q1_ssem,
    q1_rsem,
    q2_ssem,
    q2_rsem,
):
    z = lax.axis_index("fsdp")
    s = lax.axis_index("seq")
    core = s % 2
    chip = s // 2
    to_core = (z, chip * 2 + (1 - core))
    chip_x = chip + 1 - 2 * (chip % 2)
    chip_y = (chip + 2) % 4
    chip_d = chip_x + 2 - 4 * (chip_x // 2)
    to_x = (z, chip_x * 2 + core)
    to_y = (z, chip_y * 2 + core)
    rows, width = tok_ref.shape
    length = normed.shape[0]
    units = act.shape[1]
    fan = width // planes
    mine = wq.shape[3]
    tiles = length // TILE

    def remote(src, dst, ssem, rsem, where):
        return pltpu.make_async_remote_copy(
            src_ref=src, dst_ref=dst, send_sem=ssem, recv_sem=rsem, device_id=where,
            device_id_type=MESH,
        )

    def line(ref, cols):
        return ref[cols].astype(F32)[None, :]

    def block(i, n):
        return pl.ds(pl.multiple_of(i * n, n), n)

    bar = pltpu.get_barrier_semaphore()
    for k in range(1, 8):
        pl.semaphore_signal(bar, inc=1, device_id=(z, (s + k) % 8), device_id_type=MESH)
    for k in range(1, planes):
        pl.semaphore_signal(bar, inc=1, device_id=((z + k) % planes, s), device_id_type=MESH)
    pl.semaphore_wait(bar, 7 + planes - 1)

    chunks = []
    for c in range(3):
        chunks.append((wq_in.at[c], lambda j, c=c: wq.at[j, c]))
    chunks.append((wd_in, lambda j: wd.at[j]))
    part = fan // 4
    for i in range(4):
        chunks.append(
            (
                wi_in.at[pl.ds(i * part, part), :],
                lambda j, i=i: wi.at[j, pl.ds(i * part, part), :],
            )
        )
    for i in range(fan // PART):
        chunks.append(
            (
                wo_in.at[:, pl.ds(i * PART, PART)],
                lambda j, i=i: wo.at[j, :, pl.ds(i * PART, PART)],
            )
        )
    n_chunks = len(chunks)
    ahead = 2
    last_step = n_chunks + planes - 1

    def zcopy(c, direction, k):
        src, place = chunks[c]
        j = z - k if direction == 0 else z + k
        return remote(
            src if k == 0 else place(j),
            place(j),
            zs_sem.at[c, direction, k],
            zr_sem.at[c, j],
            (z + 1, s) if direction == 0 else (z - 1, s),
        )

    def zhas(direction, k):
        if direction == 0:
            return jnp.logical_and(z - k >= 0, z + 1 < planes)
        return jnp.logical_and(z + k < planes, z - 1 >= 0)

    def zsend(c, k):
        for direction in (0, 1):

            @pl.when(zhas(direction, k))
            def _(direction=direction):
                zcopy(c, direction, k).start()

    def zarrived(c, j):
        place = chunks[c][1](j)
        pltpu.make_async_copy(place, place, zr_sem.at[c, j]).wait()

    def zrelay(c, k):
        for direction in (0, 1):

            @pl.when(zhas(direction, k))
            def _(direction=direction):
                zarrived(c, z - k if direction == 0 else z + k)
                zcopy(c, direction, k).start()

    def zfinish(first, last):
        for c in range(first, last):
            for direction in (0, 1):
                for k in range(1, planes):
                    j = z - k if direction == 0 else z + k
                    here = z == planes - 1 if direction == 0 else z == 0

                    @pl.when(here)
                    def _(c=c, j=j):
                        zarrived(c, j)

    def zstep(t):
        if t == 0:
            for c in range(min(ahead, n_chunks - 1) + 1):
                zsend(c, 0)
        elif t + ahead < n_chunks:
            zsend(t + ahead, 0)
        for k in range(1, planes - 1):
            if 0 <= t - k < n_chunks:
                zrelay(t - k, k)

    own = []
    for c in range(n_chunks):
        src, place = chunks[c]
        own.append(pltpu.make_async_copy(src, place(z), local_sem.at[c]))
    zstep(0)
    for copy in own:
        copy.start()

    half = width // 2

    def row_view(buf, b, part):
        if part is None:
            return buf.at[block(b, rows), :]
        return buf.at[block(b, rows), pl.ds(part * half, half)]

    def lead_view(buf, b, part):
        if part is None:
            return buf.at[b]
        return buf.at[b, pl.ds(part * (planes // 2), planes // 2)]

    def gather_copies(p, buf, view):
        bx = chip_x * 2 + core
        by = chip_y * 2 + core
        bd = chip_d * 2 + core
        me = view(buf, s, None)
        blk_x = view(buf, bx, None)
        blk_y = view(buf, by, None)
        blk_d = view(buf, bd, None)
        x0 = view(buf, bx, 0)
        y1 = view(buf, by, 1)
        d0 = view(buf, bd, 0)
        d1 = view(buf, bd, 1)
        ss, rs = ag_ssem.at[p], ag_rsem.at[p]

        def same(ref, i, where):
            return remote(ref, ref, ss.at[i], rs.at[i], where)

        sends = [
            same(me, 0, to_x),
            same(me, 1, to_y),
            same(me, 2, to_core),
            same(x0, 3, to_y),
            same(blk_x, 4, to_core),
            same(y1, 5, to_x),
            same(blk_y, 6, to_core),
            same(blk_d, 7, to_core),
        ]
        other = 1 - core
        into = [
            blk_x,
            blk_y,
            view(buf, chip * 2 + other, None),
            d0,
            view(buf, chip_x * 2 + other, None),
            d1,
            view(buf, chip_y * 2 + other, None),
            view(buf, chip_d * 2 + other, None),
        ]

        def arrived(i):
            pltpu.make_async_copy(into[i], into[i], rs.at[i]).wait()

        return sends, arrived

    cot[block(s, rows), :] = cotown_ref[...]
    c_sends, c_arrived = gather_copies(0, cot, row_view)
    for i in range(3):
        c_sends[i].start()

    n_in = map_refs[5].shape[0]
    spots = ((0, 0), (4, 64), (3, 128), (7, 192), (2, 256))
    for m, at in spots:
        stack[at : at + 64, :] = map_refs[m][...]
    stack[320:384, :] = map_refs[1][128:, :]
    stack[384:512, :] = map_refs[1][:128, :]
    base_in, base_out = 512, 512 + n_in
    stack[base_in : base_in + n_in, :] = map_refs[5][...]
    stack[base_out : base_out + n_in, :] = map_refs[6][...]
    lane = lax.broadcasted_iota(jnp.int32, (RANK, ADAPT * RANK), 1)
    column = lax.broadcasted_iota(jnp.int32, (RANK, ADAPT * RANK), 0)
    picks = []
    for g in range(planes):
        picks.append((lane == column + index_ref[g] * RANK).astype(F32).astype(BF16))
        sel[g] = dot_nt(picks[g], stack[...]).astype(BF16)

    def adapter_copy(k):
        g = (z + k) % planes
        return remote(sel.at[g], adm.at[s, z], adz_ssem.at[k - 1], adz_rsem.at[z], (g, s))

    for k in range(1, planes):
        adapter_copy(k).start()
    adm[s, z] = sel[z]
    zstep(1)

    x = tok_ref[...].astype(F32)
    mean = jnp.mean(x, axis=-1, keepdims=True)
    centred = x - mean
    inv = lax.rsqrt(jnp.mean(centred * centred, axis=-1, keepdims=True) + EPSILON)
    normed[block(s, rows), :] = (
        centred * inv * line(gain_ref, ALL) + line(shift_ref, ALL)
    ).astype(BF16)
    n_sends, n_arrived = gather_copies(1, normed, row_view)
    for k in range(1, planes):
        g = (z + k) % planes
        pltpu.make_async_copy(adm.at[s, g], adm.at[s, g], adz_rsem.at[g]).wait()
    m_sends, m_arrived = gather_copies(2, adm, lead_view)
    gathers = ((c_sends, c_arrived), (n_sends, n_arrived), (m_sends, m_arrived))
    for m, (sends, arrived) in enumerate(gathers):
        arrived(0)
        sends[3].start()
        sends[4].start()
        arrived(1)
        sends[5].start()
        sends[6].start()
        if m < 2:
            for i in range(3):
                gathers[m + 1][0][i].start()
            zstep(m + 2)
    zstep(4)
    for m, (sends, arrived) in enumerate(gathers):
        arrived(3)
        arrived(5)
        sends[7].start()
    for sends, arrived in gathers:
        for i in (2, 4, 6, 7):
            arrived(i)
    zstep(5)

    def order(f, carry):
        low_half = lax.broadcasted_iota(jnp.int32, (RANK, 128), 1) < 64

        def swap(v):
            return pltpu.roll(v, 64, 1)

        for pair in range(4):

            def tile(odd, i):
                return adm[2 * pair + odd, f, :, i * 128 : (i + 1) * 128].astype(F32)

            def first(i):
                return jnp.where(low_half, tile(0, i), swap(tile(1, i))).astype(BF16)

            def second(i):
                return jnp.where(low_half, swap(tile(0, i)), tile(1, i)).astype(BF16)

            where = block(f * 4 + pair, 128)
            downs_ref[:RANK, where] = first(0)
            downs_ref[RANK:, where] = second(0)
            ups_ref[:RANK, where] = first(1)
            ups_ref[RANK:, where] = second(1)
            ddown_all[:, where] = first(2)
            turned = swap(tile(1, 3))
            at = (f * 4 + pair) * 3
            qup_all[:, block(at, 128)] = tile(0, 3).astype(BF16)
            qup_all[:, block(at + 1, 128)] = jnp.where(
                low_half, swap(tile(0, 2)), turned
            ).astype(BF16)
            qup_all[:, block(at + 2, 128)] = jnp.where(low_half, turned, tile(1, 2)).astype(BF16)
        return carry

    lax.fori_loop(0, planes, order, 0)
    for j in range(4):
        q = s * 4 + j
        n = n_in
        iup_ref[:, j * n : (j + 1) * n] = adm[q % 8, q // 8, :, base_in : base_in + n]
        odown_ref[:, j * n : (j + 1) * n] = adm[q % 8, q // 8, :, base_out : base_out + n]

    def qup(c):
        return qup_all[:, pl.ds(pl.multiple_of(c * width + s * mine, mine), mine)]

    def ddown():
        return ddown_all[:, block(s, mine)]

    def low(t, carry):
        r = block(t, TILE)
        c = dot_nt(normed[r, :], downs_ref[...])
        coeff[r, :] = c.astype(BF16)
        g = ADAPTER_SCALE * dot_nt(cot[r, :], ups_ref[...])
        cgs[r, :] = g.astype(BF16)
        return carry

    lax.fori_loop(0, tiles, low, 0)
    for copy in own:
        copy.wait()
    zstep(6)
    zfinish(0, 4)

    def project(t, carry):
        r = block(t, TILE)
        cos = cos_ref[r, :]
        sin = sin_ref[r, :]
        for c in range(3):
            v = ADAPTER_SCALE * dot(coeff[r, :RANK], qup(c))
            v = v + line(qb_ref, pl.ds(pl.multiple_of(c * width + s * mine, mine), mine))
            for j in range(planes):
                v = v + dot(normed[r, j * fan : (j + 1) * fan], wq[j, c])
            if c < 2:
                v = turn_all(v, cos, sin, 1.0)
            v = v.astype(BF16)
            if c == 0:
                v = v * jnp.asarray(HD**-0.5, BF16)
            qkv[c, r, :] = v
        g = dot(cgs[r, :RANK], ddown())
        for j in range(planes):
            g = g + dot_nt(cot[r, j * fan : (j + 1) * fan], wd[j])
        hg[r, :] = g.astype(BF16)
        return carry

    lax.fori_loop(0, tiles, project, 0)
    zstep(7)

    dk = ag.at[:, pl.ds(0, mine)]
    dv = ag.at[:, pl.ds(mine, mine)]
    ag[:, : 2 * mine] = jnp.zeros((length, 2 * mine), F32)
    heads = mine // HD

    for b in range(length // BLOCK):
        lo, hi = b * BLOCK, (b + 1) * BLOCK
        acc_a[...] = jnp.zeros_like(acc_a)
        acc_b[...] = jnp.zeros_like(acc_b)

        def one_head(h, carry, lo=lo, hi=hi):
            lane = lax.broadcasted_iota(jnp.int32, (1, mine), 1)
            mask = (lane // HD == h).astype(BF16)
            mask32 = (lane // HD == h).astype(F32)
            q = qkv[0, lo:hi, :] * mask
            g = hg[lo:hi, :] * mask
            k = qkv[1, :hi, :]
            v = qkv[2, :hi, :]
            sc = dot_nt(q, k)
            e = jnp.exp(sc - jnp.max(sc, axis=-1, keepdims=True))
            p = e * (1.0 / jnp.sum(e, axis=-1, keepdims=True))
            pb = p.astype(BF16)
            acc_a[...] += dot(pb, v) * mask32
            dp = dot_nt(g, v)
            ds = (p * (dp - jnp.sum(dp * p, axis=-1, keepdims=True))).astype(BF16)
            acc_b[...] += dot(ds, k) * mask32
            dk[:hi, :] += dot_tn(ds, q)
            dv[:hi, :] += dot_tn(pb, g)
            return carry

        lax.fori_loop(0, heads, one_head, 0)
        att[lo:hi, :] = acc_a[...].astype(BF16)
        back = (acc_b[...] * (HD**-0.5)).astype(BF16).astype(F32)
        pg[0, lo:hi, :] = turn_all(back, cos_ref[lo:hi, :], sin_ref[lo:hi, :], -1.0).astype(BF16)
        if b == 1:
            zstep(8)
        if b == 2:
            zstep(9)
        if b == 3:
            zstep(10)

    def finish(t, carry):
        r = block(t, TILE)
        back = dk[r, :].astype(BF16).astype(F32)
        pg[1, r, :] = turn_all(back, cos_ref[r, :], sin_ref[r, :], -1.0).astype(BF16)
        pg[2, r, :] = dv[r, :].astype(BF16)
        return carry

    lax.fori_loop(0, tiles, finish, 0)

    coeff_t[...] = dot_nt(downs_ref[...], normed[...]).astype(BF16)
    cgs_t[...] = (ADAPTER_SCALE * dot_nt(ups_ref[...], cot[...])).astype(BF16)

    share = width // 8

    def wait_on(ref, sem):
        pltpu.make_async_copy(ref, ref, sem).wait()

    def hop1(w, msg, h1, start):
        for j in range(4):
            to = 4 * (s % 2) + j
            there = (z, to)

            @pl.when(to != s)
            def _(j=j, there=there):
                copy = remote(
                    msg.at[j], h1.at[s // 2], h1_ssem.at[w, j], h1_rsem.at[w, s // 2], there
                )
                if start:
                    copy.start()
                else:
                    copy.wait_send()

            if start:

                @pl.when(to == s)
                def _(j=j):
                    pltpu.make_async_copy(
                        msg.at[j], h1.at[s // 2], h1_rsem.at[w, s // 2]
                    ).start()

    def hop2_copy(w, h1, h2, k):
        g = (z + k) % planes
        return remote(h1.at[g], h2.at[z], h2_ssem.at[w, k - 1], h2_rsem.at[w, z], (g, s))

    def hop2(w, h1, h2):
        for g in range(planes):
            wait_on(h1.at[g], h1_rsem.at[w, g])
        for k in range(1, planes):
            hop2_copy(w, h1, h2, k).start()
        h2[z] = h1[z]

    def landed(w, h1, h2):
        for k in range(1, planes):
            g = (z + k) % planes
            wait_on(h2.at[g], h2_rsem.at[w, g])
        for k in range(1, planes):
            hop2_copy(w, h1, h2, k).wait_send()

    pick_all = jnp.concatenate(picks, axis=0)

    def spread(h2):
        return dot_tn(h2.reshape(planes * RANK, h2.shape[-1]), pick_all)

    def half_rows(v):
        return jnp.where(s % 2 == 0, v[:64], v[64:])

    for c in range(3):
        g = ADAPTER_SCALE * dot(coeff_t[:RANK, :], pg[c])
        for i in range(2):
            qgrad[2 * c + i] = g[:, i * 128 : (i + 1) * 128].astype(BF16)

    def qkv_hop1(start):
        for c in range(3):
            for i in range(2):
                t = 16 * c + 2 * s + i
                for o in range(2):
                    owner = 2 * (t // 3) + o
                    slot = t % 3 - o
                    ok = jnp.logical_and(slot >= 0, slot <= 1)
                    to = owner % 8
                    src = qgrad.at[2 * c + i]
                    n = 4 * c + 2 * i + o

                    @pl.when(jnp.logical_and(ok, to != s))
                    def _(src=src, owner=owner, slot=slot, to=to, n=n):
                        copy = remote(
                            src, q_h1.at[owner // 8, slot], q1_ssem.at[n],
                            q1_rsem.at[owner // 8, slot], (z, to),
                        )
                        if start:
                            copy.start()
                        else:
                            copy.wait_send()

                    if start:

                        @pl.when(jnp.logical_and(ok, to == s))
                        def _(src=src, owner=owner, slot=slot):
                            pltpu.make_async_copy(
                                src, q_h1.at[owner // 8, slot], q1_rsem.at[owner // 8, slot]
                            ).start()

    def qkv_hop2_copy(k):
        g = (z + k) % planes
        return remote(q_h1.at[g], q_h2.at[z], q2_ssem.at[k - 1], q2_rsem.at[z], (g, s))

    def qkv_hop2():
        for g in range(planes):
            for slot in range(2):
                wait_on(q_h1.at[g, slot], q1_rsem.at[g, slot])
        for k in range(1, planes):
            qkv_hop2_copy(k).start()
        q_h2[z] = q_h1[z]

    def qkv_landed():
        for k in range(1, planes):
            g = (z + k) % planes
            wait_on(q_h2.at[g], q2_rsem.at[g])
        for k in range(1, planes):
            qkv_hop2_copy(k).wait_send()

    qkv_hop1(True)
    g = dot(cgs_t[:RANK, :], att[...])
    for j in range(4):
        a_msg[j, :, 256:384] = g[:, (j // 2) * 128 : (j // 2 + 1) * 128].astype(BF16)
    pass
    zfinish(4, 8)
    zstep(11)

    k0 = 0.7978845608028654
    k1 = 0.044715

    def inner(t, carry):
        r = block(t, TILE)
        v = ADAPTER_SCALE * dot(coeff[r, RANK : 2 * RANK], iup_ref[...])
        v = v + line(ib_ref, block(s, units))
        for j in range(planes):
            v = v + dot(normed[r, j * fan : (j + 1) * fan], wi[j])
        sq = v * v
        th = jnp.tanh(k0 * v * (1.0 + k1 * sq))
        act[r, :] = (0.5 * v * (1.0 + th)).astype(BF16)
        pre[r, :] = 0.5 * (1.0 + th) + 0.5 * v * (1.0 - th * th) * (k0 * (1.0 + 3.0 * k1 * sq))
        return carry

    lax.fori_loop(0, tiles, inner, 0)
    for k in range(1, planes):
        adapter_copy(k).wait_send()
    for sends, _ in gathers:
        for copy in sends:
            copy.wait_send()
    spot = (8, planes, RANK, share)
    for i in range(length // (8 * planes * RANK)):
        span = 8 * planes * RANK
        adm[:, :, :, i * share : (i + 1) * share] = normed[
            i * span : (i + 1) * span, block(s, share)
        ].reshape(spot)
    g = dot(cgs_t[RANK : 2 * RANK, :], act[...])
    for j in range(4):
        a_msg[j, :, :256] = g[:, j * 256 : (j + 1) * 256].astype(BF16)
    zstep(12)

    partners = (to_core, to_x, to_y)

    def reduce_copy(w, i):
        src = ar_send.at[0] if w == 0 else ar_low
        dst = ar_recv.at[i] if w == 0 else ar_recv_low.at[i]
        return remote(src, dst, ar_ssem.at[w, i], ar_rsem.at[w, i], partners[i])

    def reduce_round(w, i):
        if i > 0:
            reduce_copy(w, i - 1).wait()
            got = ar_recv[i - 1] if w == 0 else ar_recv_low[i - 1].astype(F32)
            ar_send[w] += got
        if i < 3:
            if w == 1:
                ar_low[...] = ar_send[1].astype(BF16)
            reduce_copy(w, i).start()

    ar_send[0, :RANK, :] = dot_nt(ddown(), att[...])
    ar_send[0, RANK : 2 * RANK, :] = dot_nt(odown_ref[...], act[...])
    p_units = width // UNIT
    per = fan // UNIT
    def attention_back(u, carry):
        j = u // per
        rws = block(u % per, UNIT)
        for h in range(2):
            r = slice(h * length // 2, (h + 1) * length // 2)
            v = dot_nt(pg[0, r, :], wq[j, 0, rws, :])
            for c in range(1, 3):
                v = v + dot_nt(pg[c, r, :], wq[j, c, rws, :])
            normed[r, block(u, UNIT)] = v.astype(BF16)
        return carry

    for i in range(4):
        reduce_round(0, i)
        lax.fori_loop(2 * i, 2 * i + 2, attention_back, 0)
    coeff_dense = ar_send[0].astype(BF16)
    for i in range(2):
        g = ADAPTER_SCALE * dot(
            coeff_dense[i * RANK : (i + 1) * RANK, :], cot[:, block(s, share)]
        )
        for j in range(4):
            at = 384 + i * 128
            a_msg[j, :, at : at + 128] = g[:, (j // 2) * 128 : (j // 2 + 1) * 128].astype(BF16)
    hop1(0, a_msg, a_h1, True)

    p_units = width // UNIT
    per = fan // UNIT
    early = p_units - planes // 2
    total = 2 * p_units

    def branch_place(n):
        return (n % (planes // 2)) * 2, n // (planes // 2)

    def back_place(n):
        return (n - p_units) // per, (n - p_units) % per

    def keep_split(n, k, r):
        slot = n % 2
        a = r[:rows, :]
        b = r[rows:, :]
        first = core == 0
        keep[n % 6, k] = jnp.where(first, a, b)
        s1_send[slot, k] = jnp.where(first, b, a).astype(BF16)

    def keep_pair(n, k, v):
        keep_split(n, 2 * k, v[:TILE])
        keep_split(n, 2 * k + 1, v[TILE:])

    def s1_copy(n):
        return remote(s1_send.at[n % 2], s1_recv.at[n], s1_ssem.at[n % 2], s1_rsem.at[n], to_core)

    def a_copy(n, i):
        return remote(
            a_send.at[n % 3, i], a_recv.at[n, i], a_ssem.at[n % 3, i], a_rsem.at[n, i],
            (to_x, to_y)[i],
        )

    def c_copy(n, i):
        return remote(
            c_send.at[n % 3, i], c_recv.at[n, i], c_ssem.at[n % 3, i], c_rsem.at[n, i],
            (to_x, to_y)[i],
        )

    hu = UNIT // 2

    def stage0_branch(n):
        j, i = branch_place(n)

        def tile(k, carry):
            r = block(k, 2 * TILE)
            cols = block(i, PART)
            w_o = jnp.concatenate([wo[j, :, cols], wo[j + 1, :, cols]], axis=1)
            w_d = jnp.concatenate([wd[j, :, cols], wd[j + 1, :, cols]], axis=1)
            keep_pair(n, k, dot(act[r, :], w_o) + dot(att[r, :], w_d))
            return carry

        lax.fori_loop(0, tiles // 2, tile, 0)
        s1_copy(n).start()

    def stage0_back(n):
        j, i = back_place(n)

        def tile(k, carry):
            r = block(k, 2 * TILE)
            rws = block(i, UNIT)
            v = dot_nt(pgrad[r, :], wi[j, rws, :])
            v = v + normed[r, block(n - p_units, UNIT)].astype(F32)
            keep_pair(n, k, v)
            return carry

        lax.fori_loop(0, tiles // 2, tile, 0)
        s1_copy(n).start()

    def stage1(n):
        s1_copy(n).wait()
        q = n % 6
        for k in range(4):
            keep[q, k] += s1_recv[n, k].astype(F32)
        far = keep[q, chip_d]
        a_send[n % 3, 0] = far[:, :hu].astype(BF16)
        a_send[n % 3, 1] = far[:, hu:].astype(BF16)
        for i in range(2):
            a_copy(n, i).start()

    def stage2(n):
        q = n % 6
        for i in range(2):
            a_copy(n, i).wait()
        keep[q, chip_y, :, :hu] += a_recv[n, 0].astype(F32)
        keep[q, chip_x, :, hu:] += a_recv[n, 1].astype(F32)
        c_send[n % 3, 0] = keep[q, chip_x].astype(BF16)
        c_send[n % 3, 1] = keep[q, chip_y].astype(BF16)
        for i in range(2):
            c_copy(n, i).start()

    def stage3(n):
        q = n % 6
        for i in range(2):
            c_copy(n, i).wait()
        v = keep[q, chip] + c_recv[n, 0].astype(F32) + c_recv[n, 1].astype(F32)

        @pl.when(n < p_units)
        def _():
            j, i = branch_place(n)
            for m in range(2):
                res[:, pl.ds(pl.multiple_of((j + m) * fan + i * PART, PART), PART)] = v[
                    :, m * PART : (m + 1) * PART
                ]

        @pl.when(n >= p_units)
        def _():
            igrad_ref[:, block(n - p_units, UNIT)] = v

    def pipeline(first, lo, hi, stage0, extra=None, units_end=None):
        def body(n, carry):
            if stage0 is not None:
                stage0(n)
            for back, stage in ((1, stage1), (3, stage2), (5, stage3)):
                m = n - back
                ok = m >= first
                if stage0 is None:
                    ok = jnp.logical_and(ok, m < units_end)

                @pl.when(ok)
                def _(m=m, stage=stage):
                    stage(m)

            if extra is not None:
                extra(n)
            return carry

        lax.fori_loop(lo, hi, body, 0)

    zstep(13)
    def act_part(r, i):
        cols = [slice(j * fan + i * PART, j * fan + (i + 1) * PART) for j in range(planes)]
        g = jnp.concatenate([cot[r, c] for c in cols], axis=1)
        w = [wo[j, :, i * PART : (i + 1) * PART] for j in range(planes)]
        return dot_nt(g, jnp.concatenate(w, axis=1))

    per_part = planes // 2
    for i in range(fan // PART - 1):
        zfinish(8 + i, 9 + i)
        pipeline(0, i * per_part, (i + 1) * per_part, stage0_branch)

        def act_back(t, carry, i=i):
            r = block(t, TILE)
            if i == 1:
                v = dot(cgs[r, RANK : 2 * RANK], odown_ref[...]) + act_part(r, 0)
                ag[r, :] = v + act_part(r, 1)
            else:
                ag[r, :] += act_part(r, i)
            return carry

        if i > 0:
            lax.fori_loop(0, tiles, act_back, 0)
    zfinish(11, 12)

    pipeline(0, early, p_units, stage0_branch)

    def act_last(t, carry):
        r = block(t, TILE)
        v = ag[r, :] + act_part(r, fan // PART - 1)
        pgrad[r, :] = (v * pre[r, :]).astype(BF16)
        return carry

    lax.fori_loop(0, tiles, act_last, 0)

    def rounds(n):
        @pl.when(n == p_units)
        def _():
            up_part = dot_nt(iup_ref[...], pgrad[...])
            q_part = dot_nt(qup(0), pg[0])
            for c in range(1, 3):
                q_part = q_part + dot_nt(qup(c), pg[c])
            ar_send[1, :RANK, :] = ADAPTER_SCALE * q_part
            ar_send[1, RANK : 2 * RANK, :] = ADAPTER_SCALE * up_part
            reduce_round(1, 0)
            qkv_hop2()
            hop2(0, a_h1, a_h2)

        @pl.when(n == p_units + 4)
        def _():
            qkv_landed()
            full = [spread(q_h2[:, i]) for i in range(2)]
            full = jnp.concatenate(full, axis=0)
            grad_refs[1][...] = jnp.where(s % 2 == 0, full[:192], full[64:])

        @pl.when(n == p_units + 3)
        def _():
            landed(0, a_h1, a_h2)
            full = spread(a_h2[...])
            grad_refs[6][...] = full[:256]
            grad_refs[2][...] = half_rows(full[256:384])
            grad_refs[3][...] = half_rows(full[384:512])
            grad_refs[7][...] = half_rows(full[512:640])


        for i in range(1, 4):

            @pl.when(n == p_units + (1, 3, 5)[i - 1])
            def _(i=i):
                reduce_round(1, i)
                if i == 2:
                    g = ADAPTER_SCALE * dot(coeff_t[RANK : 2 * RANK, :], pgrad[...])
                    for j in range(4):
                        b_msg[j, :, :256] = g[:, j * 256 : (j + 1) * 256].astype(BF16)
                if i == 3:
                    g = None
                    span = 8 * planes * RANK
                    for m in range(length // span):
                        part = dot(
                            ar_send[1, :, m * span : (m + 1) * span].astype(BF16),
                            adm[:, :, :, m * share : (m + 1) * share].reshape(span, share),
                        )
                        g = part if g is None else g + part
                    for m in range(2):
                        for j in range(4):
                            b_msg[j, :, 256 + m * 128 : 384 + m * 128] = g[
                                m * RANK : (m + 1) * RANK, (j // 2) * 128 : (j // 2 + 1) * 128
                            ].astype(BF16)
                    hop1(1, b_msg, b_h1, True)

    pipeline(0, p_units, total, stage0_back, rounds)
    pipeline(0, total, total + 3, None, None, total)
    hop2(1, b_h1, b_h2)
    pipeline(0, total + 3, total + 5, None, None, total)

    first_t = ar_send[0, :, block(s, rows)].astype(BF16)
    late_t = ar_send[1, :, block(s, rows)].astype(BF16)
    out = tok_ref[...].astype(F32) + res[...] + ADAPTER_SCALE * dot_tn(first_t, ups_ref[...])
    out_ref[...] = (out + line(db_ref, ALL) + line(ob_ref, ALL)).astype(BF16)
    x = tok_ref[...].astype(F32)
    mean = jnp.mean(x, axis=-1, keepdims=True)
    centred = x - mean
    inv = lax.rsqrt(jnp.mean(centred * centred, axis=-1, keepdims=True) + EPSILON)
    xhat = centred * inv
    e = (igrad_ref[...] + dot_tn(late_t, downs_ref[...])) * line(gain_ref, ALL)
    igrad_ref[...] = cotown_ref[...].astype(F32) + inv * (
        e
        - jnp.mean(e, axis=-1, keepdims=True)
        - xhat * jnp.mean(e * xhat, axis=-1, keepdims=True)
    )

    landed(1, b_h1, b_h2)
    full = spread(b_h2[...])
    grad_refs[5][...] = full[:256]
    grad_refs[0][...] = half_rows(full[256:384])
    grad_refs[4][...] = half_rows(full[384:512])

    hop1(0, a_msg, a_h1, False)
    hop1(1, b_msg, b_h1, False)
    qkv_hop1(False)
    for c in range(n_chunks):
        for k in range(planes - 1):
            for direction in (0, 1):

                @pl.when(zhas(direction, k))
                def _(c=c, k=k, direction=direction):
                    zcopy(c, direction, k).wait_send()


def run_layer(planes, args, shapes):
    rows, width, length, units, mine = shapes
    fan = width // planes
    vm = pl.BlockSpec(memory_space=pltpu.VMEM)
    hbm = pl.BlockSpec(memory_space=pl.ANY)
    n_chunks = 8 + fan // PART
    total = 2 * width // UNIT
    dma = pltpu.SemaphoreType.DMA
    maps = args[13:21]
    lanes = sum(m.shape[0] for m in maps)

    def entry(*refs):
        layer_kernel(planes, *refs[:13], refs[13:21], *refs[21:25], refs[25:33], *refs[33:])

    outs = pl.pallas_call(
        entry,
        out_shape=(
            jax.ShapeDtypeStruct((rows, width), BF16),
            jax.ShapeDtypeStruct((rows, width), F32),
            *(jax.ShapeDtypeStruct(m.shape, F32) for m in maps),
        ),
        in_specs=[vm, vm, hbm, hbm, hbm, hbm]
        + [vm] * 6
        + [pl.BlockSpec(memory_space=pltpu.SMEM)]
        + [vm] * 10,
        out_specs=(vm,) * 10,
        scratch_shapes=[
            pltpu.VMEM((lanes, ADAPT * RANK), BF16),
            pltpu.VMEM((planes, RANK, lanes), BF16),
            pltpu.VMEM((8, planes, RANK, lanes), BF16),
            pltpu.VMEM((2 * RANK, width), BF16),
            pltpu.VMEM((2 * RANK, width), BF16),
            pltpu.VMEM((RANK, width), BF16),
            pltpu.VMEM((RANK, 3 * width), BF16),
            pltpu.VMEM((RANK, units), BF16),
            pltpu.VMEM((RANK, units), BF16),
            pltpu.VMEM((6, RANK, 128), BF16),
            pltpu.VMEM((4, RANK, 640), BF16),
            pltpu.VMEM((planes, RANK, 640), BF16),
            pltpu.VMEM((planes, RANK, 640), BF16),
            pltpu.VMEM((4, RANK, 512), BF16),
            pltpu.VMEM((planes, RANK, 512), BF16),
            pltpu.VMEM((planes, RANK, 512), BF16),
            pltpu.VMEM((planes, 2, RANK, 128), BF16),
            pltpu.VMEM((planes, 2, RANK, 128), BF16),
            pltpu.VMEM((length, width), BF16),
            pltpu.VMEM((length, width), BF16),
            pltpu.VMEM((planes, 3, fan, mine), BF16),
            pltpu.VMEM((planes, mine, fan), BF16),
            pltpu.VMEM((planes, fan, units), BF16),
            pltpu.VMEM((planes, units, fan), BF16),
            pltpu.VMEM((3, length, mine), BF16),
            pltpu.VMEM((length, mine), BF16),
            pltpu.VMEM((length, mine), BF16),
            pltpu.VMEM((3, length, mine), BF16),
            pltpu.VMEM((BLOCK, mine), F32),
            pltpu.VMEM((BLOCK, mine), F32),
            pltpu.VMEM((length, units), F32),
            pltpu.VMEM((length, units), BF16),
            pltpu.VMEM((length, units), F32),
            pltpu.VMEM((length, units), BF16),
            pltpu.VMEM((length, 2 * RANK), BF16),
            pltpu.VMEM((length, 2 * RANK), BF16),
            pltpu.VMEM((2 * RANK, length), BF16),
            pltpu.VMEM((2 * RANK, length), BF16),
            pltpu.VMEM((rows, width), F32),
            pltpu.VMEM((6, 4, rows, UNIT), F32),
            pltpu.VMEM((2, 4, rows, UNIT), BF16),
            pltpu.VMEM((total, 4, rows, UNIT), BF16),
            pltpu.VMEM((3, 2, rows, UNIT // 2), BF16),
            pltpu.VMEM((total, 2, rows, UNIT // 2), BF16),
            pltpu.VMEM((3, 2, rows, UNIT), BF16),
            pltpu.VMEM((total, 2, rows, UNIT), BF16),
            pltpu.VMEM((2, 2 * RANK, length), F32),
            pltpu.VMEM((3, 2 * RANK, length), F32),
            pltpu.VMEM((2 * RANK, length), BF16),
            pltpu.VMEM((3, 2 * RANK, length), BF16),
            dma((n_chunks,)),
            dma((n_chunks, 2, planes)),
            dma((n_chunks, planes)),
            dma((3, 8)),
            dma((3, 8)),
            dma((2,)),
            dma((total,)),
            dma((3, 2)),
            dma((total, 2)),
            dma((3, 2)),
            dma((total, 2)),
            dma((2, 3)),
            dma((2, 3)),
            dma((planes,)),
            dma((planes,)),
            dma((2, 4)),
            dma((2, planes)),
            dma((2, planes)),
            dma((2, planes)),
            dma((12,)),
            dma((planes, 2)),
            dma((planes,)),
            dma((planes,)),
        ],
        compiler_params=pltpu.CompilerParams(
            collective_id=0, has_side_effects=True, vmem_limit_bytes=63 * 1024 * 1024
        ),
    )(*args)
    return pl.pallas_call(
        hand_over,
        out_shape=tuple(jax.ShapeDtypeStruct(o.shape, o.dtype) for o in outs),
        in_specs=[vm] * 10,
        out_specs=(vm,) * 10,
    )(*outs)


def hand_over(*refs):
    for i in range(10):
        refs[10 + i][...] = refs[i][...]


def fits(planes, groups, shapes):
    rows, width, length, units, mine = shapes
    return (
        groups == 8
        and planes == 4
        and rows * 2 == TILE
        and length <= 1024
        and width == 2048
        and mine == 256
        and units == 1024
    )


def deliver(packed, sizes, counts, pick, planes, groups):
    s = lax.axis_index("seq")
    everyone = lax.all_gather(packed, "seq", axis=0, tiled=False)
    owned = []
    at = 0
    for i, (n, w) in enumerate(zip(counts, sizes)):
        part = everyone[:, :, at : at + w]
        at += w
        blocks = 3 if i == 1 else 1
        part = part.reshape(groups, RANK, blocks, w // blocks).transpose(1, 2, 0, 3)
        part = part.reshape(RANK, planes, groups, n)
        owned.append(lax.dynamic_index_in_dim(part, s, 2, keepdims=False))
    owned = jnp.concatenate(owned, axis=2).transpose(1, 0, 2)
    arrived = lax.all_to_all(owned, "fsdp", split_axis=0, concat_axis=0, tiled=True)
    place = pick.astype(F32).reshape(planes * RANK, ADAPT * RANK)
    spread = lax.dot_general(
        arrived.reshape(planes * RANK, -1),
        place,
        (((0,), (0,)), ((), ())),
        precision=lax.Precision.HIGHEST,
        preferred_element_type=F32,
    )
    outs = []
    at = 0
    for n in counts:
        outs.append(spread[at : at + n])
        at += n
    return outs


def on_device(
    tokens,
    cotangent,
    adapter_index,
    qkv_weight,
    dense_weight,
    inner_weight,
    outer_weight,
    qkv_bias,
    dense_bias,
    inner_bias,
    outer_bias,
    norm_gain,
    norm_bias,
    *maps,
):
    planes = lax.axis_size("fsdp")
    groups = lax.axis_size("seq")
    rows, width = tokens.shape
    length = rows * groups
    heads = H // groups
    mine = heads * HD
    units = inner_weight.shape[1]
    s = lax.axis_index("seq")

    shapes = (rows, width, length, units, mine)
    if fits(planes, groups, shapes):
        return run_layer(
            planes,
            (
                tokens,
                cotangent,
                qkv_weight,
                dense_weight,
                inner_weight,
                outer_weight,
                qkv_bias,
                dense_bias,
                inner_bias,
                outer_bias,
                norm_gain,
                norm_bias,
                adapter_index,
                *maps,
                *rope_constants(length),
            ),
            shapes,
        )

    counts = [m.shape[0] for m in maps]
    stacked = jnp.concatenate(maps, axis=0)
    wanted = (adapter_index[:, None] * RANK + jnp.arange(RANK)[None, :]).reshape(-1)
    pick = (wanted[:, None] == jnp.arange(ADAPT * RANK)[None, :]).astype(BF16)
    chosen = dot_nt(pick, stacked).astype(BF16).reshape(planes, RANK, -1)
    chosen = lax.all_to_all(chosen, "fsdp", split_axis=0, concat_axis=0, tiled=True)
    chosen = lax.all_gather(chosen, "seq", axis=1, tiled=False)
    full = []
    at = 0
    for n in counts:
        part = chosen[:, :, :, at : at + n]
        full.append(part.transpose(2, 0, 1, 3).reshape(RANK, -1))
        at += n
    qkv_down, qkv_up, dense_down, dense_up, inner_down, inner_up, outer_down, outer_up = full

    def own(m, n):
        return lax.dynamic_slice_in_dim(m, s * n, n, axis=1)

    qkv_up = jnp.concatenate(
        [own(qkv_up[:, c * width : (c + 1) * width], mine) for c in range(3)], axis=1
    )
    dense_down = own(dense_down, mine)
    inner_up = own(inner_up, units)
    outer_down = own(outer_down, units)

    wqkv = lax.all_gather(qkv_weight, "fsdp", axis=1, tiled=True)
    wdense = lax.all_gather(dense_weight, "fsdp", axis=1, tiled=True)
    winner = lax.all_gather(inner_weight, "fsdp", axis=0, tiled=True)
    wouter = lax.all_gather(outer_weight, "fsdp", axis=1, tiled=True)

    gain = norm_gain.astype(F32)
    shift = norm_bias.astype(F32)
    source = tokens.astype(F32)
    normed_own = norm_layer(source, gain, shift).astype(BF16)
    normed = lax.all_gather(normed_own, "seq", axis=0, tiled=True)
    cot = lax.all_gather(cotangent, "seq", axis=0, tiled=True)

    coeffs = dot_nt(normed, jnp.concatenate([qkv_down, inner_down], axis=0)).astype(BF16)
    qkv_coeff, inner_coeff = coeffs[:, :RANK], coeffs[:, RANK:]
    cgs = (
        ADAPTER_SCALE * dot_nt(cot, jnp.concatenate([dense_up, outer_up], axis=0))
    ).astype(BF16)
    dense_cg, outer_cg = cgs[:, :RANK], cgs[:, RANK:]

    bias = jnp.stack([own(qkv_bias.reshape(3, width)[c : c + 1], mine)[0] for c in range(3)])
    projected = (
        jnp.concatenate([dot(normed, wqkv[c]) for c in range(3)], axis=1)
        + bias.reshape(-1).astype(F32)
        + ADAPTER_SCALE * dot(qkv_coeff, qkv_up)
    ).reshape(length, 3, heads, HD)
    cos_table, sin_table = rope_tables(length, heads)
    query = rotate(projected[:, 0], cos_table, sin_table).astype(BF16).transpose(1, 0, 2)
    key = rotate(projected[:, 1], cos_table, sin_table).astype(BF16).transpose(1, 0, 2)
    value = projected[:, 2].astype(BF16).transpose(1, 0, 2)
    attended_grad = (dot_nt(cot, wdense) + dot(dense_cg, dense_down)).astype(BF16)
    head_grad = attended_grad.reshape(length, heads, HD).transpose(1, 0, 2)

    scale = HD ** (-0.5)

    def bmm(spec, a, b):
        return jnp.einsum(spec, a, b, preferred_element_type=F32)

    key_grad = jnp.zeros((heads, length, HD), F32)
    value_grad = jnp.zeros((heads, length, HD), F32)
    attended_parts = []
    query_parts = []
    for b in range(length // BLOCK):
        lo, hi = b * BLOCK, (b + 1) * BLOCK
        q = query[:, lo:hi]
        k = key[:, :hi]
        v = value[:, :hi]
        g = head_grad[:, lo:hi]
        scores = bmm("hqd,hkd->hqk", q, k) * scale
        row_max = jnp.max(scores, axis=-1, keepdims=True)
        exponent = jnp.exp(scores - row_max)
        prob = exponent / jnp.sum(exponent, axis=-1, keepdims=True)
        prob_low = prob.astype(BF16)
        attended_parts.append(bmm("hqk,hkd->hqd", prob_low, v).astype(BF16))
        prob_grad = bmm("hqd,hkd->hqk", g, v)
        row_dot = jnp.sum(prob_grad * prob, axis=-1, keepdims=True)
        score_grad = (prob * (prob_grad - row_dot)).astype(BF16)
        query_parts.append((bmm("hqk,hkd->hqd", score_grad, k) * scale).astype(BF16))
        key_grad = key_grad.at[:, :hi].add(bmm("hqk,hqd->hkd", score_grad, q) * scale)
        value_grad = value_grad.at[:, :hi].add(bmm("hqk,hqd->hkd", prob_low, g))

    def rows_first(x):
        return x.transpose(1, 0, 2)

    attended = rows_first(jnp.concatenate(attended_parts, axis=1)).reshape(length, mine)
    query_grad = rows_first(jnp.concatenate(query_parts, axis=1)).astype(F32)
    key_back = rows_first(key_grad.astype(BF16)).astype(F32)
    value_back = rows_first(value_grad.astype(BF16)).reshape(length, mine)
    projected_grad = jnp.concatenate(
        [
            rotate(query_grad, cos_table, -sin_table).astype(BF16).reshape(length, mine),
            rotate(key_back, cos_table, -sin_table).astype(BF16).reshape(length, mine),
            value_back,
        ],
        axis=1,
    )

    pre_act = (
        dot(normed, winner)
        + own(inner_bias[None], units).astype(F32)
        + ADAPTER_SCALE * dot(inner_coeff, inner_up)
    )
    act32, gelu_back = jax.vjp(lambda v: jax.nn.gelu(v, approximate=True), pre_act)
    activated = act32.astype(BF16)
    act_grad = dot_nt(cot, wouter) + dot(outer_cg, outer_down)
    pre_grad = gelu_back(act_grad)[0].astype(BF16)

    def scatter(x):
        return lax.psum_scatter(x, "seq", scatter_dimension=0, tiled=True)

    branch = scatter((dot(attended, wdense) + dot(activated, wouter)))
    coeff_sum = scatter(
        jnp.concatenate([dot_nt(attended, dense_down), dot_nt(activated, outer_down)], axis=1)
    )
    back = dot_nt(pre_grad, winner)
    for c in range(3):
        back = back + dot_nt(projected_grad[:, c * mine : (c + 1) * mine], wqkv[c])
    back = scatter(back)
    cg_sum = scatter(
        ADAPTER_SCALE
        * jnp.concatenate([dot_nt(projected_grad, qkv_up), dot_nt(pre_grad, inner_up)], axis=1)
    )
    late_own = jnp.concatenate([coeff_sum, cg_sum], axis=1).astype(BF16)
    late = lax.all_gather(late_own, "seq", axis=0, tiled=True)

    layer_out = (
        source
        + branch
        + dense_bias.astype(F32)
        + outer_bias.astype(F32)
        + ADAPTER_SCALE
        * dot(late_own[:, : 2 * RANK], jnp.concatenate([dense_up, outer_up], axis=0))
    ).astype(BF16)
    normed_grad = back + dot(
        late_own[:, 2 * RANK :], jnp.concatenate([qkv_down, inner_down], axis=0)
    )
    row_mean = jnp.mean(source, axis=-1, keepdims=True)
    centred = source - row_mean
    inv = lax.rsqrt(jnp.mean(centred * centred, axis=-1, keepdims=True) + EPSILON)
    xhat = centred * inv
    e = normed_grad * gain
    input_grad = cotangent.astype(F32) + inv * (
        e
        - jnp.mean(e, axis=-1, keepdims=True)
        - xhat * jnp.mean(e * xhat, axis=-1, keepdims=True)
    )

    share = width // groups
    cot_mine = own(cot, share)
    normed_mine = own(normed, share)
    qkv_up_g = ADAPTER_SCALE * dot_tn(qkv_coeff, projected_grad)
    inner_up_g = ADAPTER_SCALE * dot_tn(inner_coeff, pre_grad)
    dense_down_g = dot_tn(dense_cg, attended)
    outer_down_g = dot_tn(outer_cg, activated)
    ups = ADAPTER_SCALE * dot_tn(late[:, : 2 * RANK], cot_mine)
    downs = dot_tn(late[:, 2 * RANK :], normed_mine)
    mine_grads = [
        downs[:RANK],
        qkv_up_g,
        dense_down_g,
        ups[:RANK],
        downs[RANK:],
        inner_up_g,
        outer_down_g,
        ups[RANK:],
    ]
    packed = jnp.concatenate(mine_grads, axis=1)
    sizes = [g.shape[1] for g in mine_grads]
    outs = deliver(packed, sizes, counts, pick, planes, groups)
    return (layer_out, input_grad, *outs)


def solution(mesh):
    both = P(("fsdp", "seq"), None)
    placed = (
        both,
        both,
        P(),
        P(None, "fsdp", "seq"),
        P("seq", "fsdp"),
        P("fsdp", "seq"),
        P("seq", "fsdp"),
    ) + (P(),) * 6 + (both,) * 8
    return jax.shard_map(
        on_device, mesh=mesh, in_specs=placed, out_specs=(both,) * 10, check_vma=False
    )
```
